256 devices in a mesh: gx: 16 (over z_hi, y), yz: 16 (over z_lo, x, core).
Axes of the slice: x: 4, y: 4, z: 8 (z_hi: 4, z_lo: 2; z = z_hi * 2 + z_lo), core: 2. Of those that a mesh axis runs over, the one named last changes fastest.
Arguments:
- solvent_vel: float32 [3, 512, 512, 2, 128], P(None, 'gx', 'yz'), may hold values from -6 to 6
- occupancy: int32 [512, 512, 128], P('gx', 'yz'), may hold values from 0 to 2
- grid_shift: int32 [3], replicated, may hold values from 1 to 3
- axis_index: int32 [128, 128, 64], P('gx', 'yz'), may hold values from 0 to 63
- colloid_pos: float32 [3, 16, 16, 128], P(None, 'gx', 'yz'), may hold values from 0 to 64, as said below
- colloid_vel: float32 [3, 16, 16, 128], P(None, 'gx', 'yz'), may hold values from -6 to 6
- colloid_mass: float32 [16, 16, 128], P('gx', 'yz'), may hold values from 2 to 20
- colloid_count: int32 [16, 16], P('gx', 'yz'), may hold values from 21 to 128, as said below
Outputs:
- solvent_out: float32 [3, 512, 512, 2, 128], P(None, 'gx', 'yz')
- colloid_pos_out: float32 [3, 16, 16, 128], P(None, 'gx', 'yz')
- colloid_vel_out: float32 [3, 16, 16, 128], P(None, 'gx', 'yz')
The draws below stay inside these ranges and needn't reach their ends.
Inputs may be any that keep to these rules, and one draw needn't show every extreme that they name: `colloid_pos`: component 0 lies in [0, 8), component 1 in [0, 8), component 2 in [0, 64). `colloid_count`: some device holds 128 live colloids in every draw.
All inputs are finite; a program needn't handle non-finite values.
Results may differ from the reference program's by a relative error of at most 0.0003.
Values sent between devices are 32-bit elements; how exact they have to be, the bound alone decides.
No kernel may reach another device: no remote copies, remote signals or barrier semaphores. Data moves between devices by JAX's collectives and lax.ppermute only.
A program may use at most 320 MiB of HBM per device.

```python
import math
import jax
import jax.numpy as jnp
from jax import lax

CX = 8
CY = 8
CZ = 64
CMAX = 128
SUB = 4
SLOTS = 2
SUBSTEPS = 4
DIRECTIONS = 64
FX = 32
FY = 32
FZ = 128
NXF = 512
NYF = 512
NX = 128
NY = 128
N_GX = 16
N_YZ = 16


def draw_occupancy(key, part):
    block = 2 * SUB
    blocks_x = (NXF + block - 1) // block
    blocks_y = (NYF + block - 1) // block
    blocks_z = (FZ + 7) // 8
    slots_used = jax.random.randint(jax.random.fold_in(key, 21), (NXF, NYF, FZ), 0, SLOTS + 1)
    sparse = jax.random.randint(jax.random.fold_in(key, 22), (blocks_x * blocks_y * blocks_z,), 0, 4) == 0
    chosen = jax.random.randint(jax.random.fold_in(key, 23), (), 0, blocks_x * blocks_y * blocks_z)
    sparse = jnp.logical_or(sparse, jnp.arange(blocks_x * blocks_y * blocks_z) == chosen)
    sparse = sparse.reshape(blocks_x, blocks_y, blocks_z)
    spread = jnp.repeat(jnp.repeat(jnp.repeat(sparse, block, axis=0), block, axis=1), 8, axis=2)[:NXF, :NYF, :FZ]
    thin_keep = jax.random.randint(jax.random.fold_in(key, 24), (NXF, NYF, FZ), 0, 4) == 0
    keeping = jnp.logical_or(jnp.logical_not(spread), thin_keep)
    return jnp.where(keeping, slots_used, 0).astype(jnp.int32)


def draw_colloid_pos(key, part):
    unit = jax.random.uniform(jax.random.fold_in(key, 5), (3, N_GX, N_YZ, CMAX), jnp.float32)
    extent = jnp.array([CX, CY, CZ], jnp.float32)
    return unit * extent[:, None, None, None] * 0.999


def draw_colloid_count(key, part):
    devices = N_GX * N_YZ
    counts = jax.random.randint(jax.random.fold_in(key, 11), (devices,), CMAX // 6, CMAX // 2 + 1)
    chosen = jax.random.randint(jax.random.fold_in(key, 12), (), 0, devices)
    counts = jnp.where(jnp.arange(devices) == chosen, CMAX, counts)
    return counts.reshape(N_GX, N_YZ).astype(jnp.int32)


def touch_ends(entries, rng, low, high):
    dims = entries.shape
    index_at = [jax.random.randint(jax.random.fold_in(rng, axis), (), 0, dims[axis]) for axis in range(len(dims))]
    entries = entries.at[tuple(index_at)].set(low)
    longest = dims.index(max(dims))
    index_at[longest] = (index_at[longest] + 1) % dims[longest]
    return entries.at[tuple(index_at)].set(high)


def block_levels(key, dims, cuts, low, high):
    def one(dim, parts):
        draws = jax.random.uniform(jax.random.fold_in(jax.random.fold_in(key, 6), dim), (parts,), jnp.float32, low / len(cuts), high / len(cuts))
        return jnp.repeat(jnp.exp(draws), dims[dim] // parts).reshape((-1,) + (1,) * (len(dims) - dim - 1))

    loudness = one(*cuts[0])
    for cut in cuts[1:]:
        loudness = loudness * one(*cut)
    return loudness


def noise(stream_key, dims, scale, bound, split=(), dtype=jnp.bfloat16):
    loudness = block_levels(stream_key, dims, split, -0.22, 0.18) if split else 1.0
    values = jax.random.normal(stream_key, dims, jnp.float32) * scale * loudness
    return jnp.minimum(jnp.maximum(values, -bound), bound).astype(dtype)


def setup_inputs(seed: int = 0) -> dict:
    key_of = jax.random.split(jax.random.key(seed), 9)
    solvent_vel = noise(key_of[0], (3, NXF, NYF, SLOTS, FZ), 1.0, 6.0, ((1, 16), (2, 16)), jnp.float32)
    occupancy = draw_occupancy(jax.random.fold_in(key_of[8], 71), 0)
    grid_shift = jax.random.randint(key_of[2], (3,), 1, SUB).astype(jnp.int32)
    axis_index = touch_ends(jax.random.randint(key_of[3], (NX, NY, CZ), 0, DIRECTIONS), jax.random.fold_in(key_of[3], 1), 0, DIRECTIONS - 1).astype(jnp.int32)
    colloid_pos = draw_colloid_pos(jax.random.fold_in(key_of[8], 71), 0)
    colloid_vel = noise(key_of[5], (3, N_GX, N_YZ, CMAX), 1.0, 6.0, ((1, 16), (2, 16)), jnp.float32)
    colloid_mass = jnp.clip(jnp.exp(math.log(20.0) - 2.3025851 * jax.random.uniform(key_of[6], (N_GX, N_YZ, CMAX), jnp.float32) ** block_levels(key_of[6], (N_GX, N_YZ, CMAX), ((0, 16), (1, 16)), -0.2, 0.2)), 2.0, 20.0)
    colloid_count = draw_colloid_count(jax.random.fold_in(key_of[8], 71), 0)
    return {"solvent_vel": solvent_vel, "occupancy": occupancy, "grid_shift": grid_shift, "axis_index": axis_index, "colloid_pos": colloid_pos, "colloid_vel": colloid_vel, "colloid_mass": colloid_mass, "colloid_count": colloid_count}


turn_angle = 130.0 * math.pi / 180.0
cos_angle = math.cos(turn_angle)
sin_angle = math.sin(turn_angle)
golden = math.pi * (3.0 - math.sqrt(5.0))
cutoff = 1.5
stiffness = 20.0
timestep = 0.05
fill_mass = 16.0

def directions(index):
    number = index.astype(jnp.float32)
    height = 1.0 - (2.0 * number + 1.0) / DIRECTIONS
    radius = jnp.sqrt(1.0 - height * height)
    phase = number * golden
    return jnp.stack([radius * jnp.cos(phase), radius * jnp.sin(phase), height])

def rotate(mean, axis, velocity):
    rel = velocity - mean
    cross = jnp.stack([axis[1] * rel[2] - axis[2] * rel[1], axis[2] * rel[0] - axis[0] * rel[2], axis[0] * rel[1] - axis[1] * rel[0]])
    along = lax.optimization_barrier(jnp.sum(axis * rel, axis=0))
    return mean + cos_angle * rel + sin_angle * cross + (1.0 - cos_angle) * along[None] * axis

def cell_fields(totals, axis_index):
    width_x, width_y, width_z = (totals.shape[1], totals.shape[2], totals.shape[3])
    cells_x, cells_y, cells_z = (width_x // SUB, width_y // SUB, width_z // 2)
    cell = totals.reshape(4, cells_x, SUB, cells_y, SUB, cells_z, 2).sum(axis=(2, 4, 6))
    mean = cell[:3] / jnp.maximum(cell[3], fill_mass)[None]
    both = jnp.concatenate([mean, directions(axis_index)])
    spread = jnp.broadcast_to(both[:, :, None, :, None, :, None], (6, cells_x, SUB, cells_y, SUB, cells_z, 2))
    return spread.reshape(6, width_x, width_y, width_z)

def pair_parts(own, other, other_live):
    diff_x = own[0][..., :, None] - other[0][..., None, :]
    diff_y = own[1][..., :, None] - other[1][..., None, :]
    height = own[2][..., :, None] - other[2][..., None, :]
    height = jnp.where(height > 0.5 * CZ, height - CZ, jnp.where(height < -0.5 * CZ, height + CZ, height))
    radius_sq = diff_x * diff_x + diff_y * diff_y + height * height
    reach = 1.0 - radius_sq / (cutoff * cutoff)
    weight = jnp.where(radius_sq < cutoff * cutoff, reach * reach, 0.0) * other_live[..., None, :]
    return (weight, diff_x, diff_y, height)

def pair_force(own, other, other_live):
    weight, diff_x, diff_y, height = pair_parts(own, other, other_live)
    return stiffness * jnp.stack([lax.optimization_barrier(jnp.sum(weight * diff_x, axis=-1)), lax.optimization_barrier(jnp.sum(weight * diff_y, axis=-1)), lax.optimization_barrier(jnp.sum(weight * height, axis=-1))])

def all_forces(position, alive):
    total = jnp.zeros_like(position)
    for step_x in (-1, 0, 1):
        for step_y in (-1, 0, 1):
            other = jnp.roll(position, (-step_x, -step_y), axis=(1, 2))
            other = jnp.stack([other[0] + step_x * CX, other[1] + step_y * CY, other[2]])
            other_live = jnp.roll(alive, (-step_x, -step_y), axis=(0, 1))
            total = total + pair_force(position, other, other_live)
    return total

def reference(solvent_vel, occupancy, grid_shift, axis_index, colloid_pos, colloid_vel, colloid_mass, colloid_count):
    nxf, nyf, nzf = occupancy.shape
    live = (lax.broadcasted_iota(jnp.int32, solvent_vel.shape[1:], 2) < occupancy[:, :, None, :]).astype(jnp.float32)
    moment = solvent_vel * live[None]
    alive = (lax.broadcasted_iota(jnp.int32, colloid_mass.shape, 2) < colloid_count[:, :, None]).astype(jnp.float32)
    row = lax.broadcasted_iota(jnp.int32, colloid_mass.shape, 0)
    column = lax.broadcasted_iota(jnp.int32, colloid_mass.shape, 1)
    cell_x = row * FX + jnp.clip(jnp.floor(colloid_pos[0] * SUB).astype(jnp.int32), 0, FX - 1)
    cell_y = column * FY + jnp.clip(jnp.floor(colloid_pos[1] * SUB).astype(jnp.int32), 0, FY - 1)
    cell_z = jnp.clip(jnp.floor(colloid_pos[2] * 2.0).astype(jnp.int32), 0, FZ - 1)
    flat = ((cell_x * nyf + cell_y) * nzf + cell_z).reshape(-1)
    weight = colloid_mass * alive
    values = jnp.concatenate([colloid_vel * weight[None], weight[None]]).reshape(4, -1)
    deposit = jnp.zeros((4, nxf * nyf * nzf), jnp.float32).at[:, flat].add(values).reshape(4, nxf, nyf, nzf)
    totals = jnp.concatenate([lax.optimization_barrier(jnp.sum(moment, axis=3)), lax.optimization_barrier(jnp.sum(live, axis=2))[None]]) + deposit
    forward = (grid_shift[0], grid_shift[1], grid_shift[2])
    backward = (-grid_shift[0], -grid_shift[1], -grid_shift[2])
    totals = jnp.roll(totals, forward, axis=(1, 2, 3))
    fields = jnp.roll(cell_fields(totals, axis_index), backward, axis=(1, 2, 3))
    turned = rotate(fields[:3, :, :, None], fields[3:, :, :, None], solvent_vel)
    solvent_out = jnp.where(live[None] > 0, turned, solvent_vel)
    picked = fields.reshape(6, -1)[:, flat].reshape((6,) + colloid_mass.shape)
    velocity = jnp.where(alive[None] > 0, rotate(picked[:3], picked[3:], colloid_vel), colloid_vel)
    position = colloid_pos
    for step in range(SUBSTEPS):
        force = all_forces(position, alive)
        velocity = velocity + timestep * force / colloid_mass[None]
        position = position + timestep * velocity
    keep = alive[None] > 0
    return (solvent_out, jnp.where(keep, position, colloid_pos), jnp.where(keep, velocity, colloid_vel))
```

```python
import math

import jax
import jax.numpy as jnp
from jax import lax
from jax.experimental import pallas as pl
from jax.experimental.pallas import tpu as pltpu
from jax.sharding import PartitionSpec as P

CX = 8
CY = 8
CZ = 64
SUB = 4
SUBSTEPS = 4
DIRECTIONS = 64
FX = 32
FY = 32
FZ = 128
KX = CX + 1
JY = CY + 1
JP = 16
ROWS = KX * JP

turn_angle = 130.0 * math.pi / 180.0
cos_angle = math.cos(turn_angle)
sin_angle = math.sin(turn_angle)
golden = math.pi * (3.0 - math.sqrt(5.0))
cutoff = 1.5
stiffness = 20.0
timestep = 0.05
fill_mass = 16.0

SMEM = pltpu.SMEM
VMEM = pltpu.VMEM
HBM = pl.BlockSpec(memory_space=pltpu.HBM)
IN_VMEM = pl.BlockSpec(memory_space=VMEM)
IN_SMEM = pl.BlockSpec(memory_space=SMEM)
DMA = pltpu.SemaphoreType.DMA
NT = (((1,), (1,)), ((), ()))
NN = (((1,), (0,)), ((), ()))
STATE = 2 * ROWS
NUMBERS = STATE + 16
BASE = NUMBERS + ROWS
SMALL_LIMIT = 8 * 1024 * 1024
TURN_LIMIT = 52 * 1024 * 1024


def shifted(value, axis, steps):
    count = lax.axis_size(axis)
    return lax.ppermute(value, axis, [(i, (i + steps) % count) for i in range(count)])


def struct(*shape):
    return jax.ShapeDtypeStruct(shape, jnp.float32)


def exact_dot(left, right, dims):
    right = right.astype(jnp.bfloat16)
    total = None
    for part in range(3):
        piece = left.astype(jnp.bfloat16)
        term = lax.dot_general(piece, right, dims, preferred_element_type=jnp.float32)
        total = term if total is None else total + term
        if part < 2:
            left = left - piece.astype(jnp.float32)
    return total


def colloid_cells(pos, sx, sy, sz):
    cell_x = jnp.clip(jnp.floor(pos[0] * SUB).astype(jnp.int32), 0, FX - 1)
    cell_y = jnp.clip(jnp.floor(pos[1] * SUB).astype(jnp.int32), 0, FY - 1)
    cell_z = jnp.clip(jnp.floor(pos[2] * 2.0).astype(jnp.int32), 0, FZ - 1)
    return ((cell_x + sx) >> 2, (cell_y + sy) >> 2, ((cell_z + sz) & (FZ - 1)) >> 1)


def live_row(count):
    return lax.broadcasted_iota(jnp.int32, (1, FZ), 1) < count


def store_twice(occ, twice, q):
    slots = occ[SUB * q : SUB * q + SUB].reshape(SUB * FY, FZ).astype(jnp.float32)
    base = 2 * SUB * FY * q
    twice[pl.ds(base, SUB * FY, 2), :] = slots
    twice[pl.ds(base + 1, SUB * FY, 2), :] = slots


def sums_kernel(
    shift_at, count_at, v_at, occ_at, axis_at, pos_at, vel_at, mass_at,
    base, up, down,
    shift, count, v, occ, axis, pos, vel, mass, twice, partial, sem, vsem, osem,
):
    small = [
        pltpu.make_async_copy(a, b, sem.at[i])
        for i, (a, b) in enumerate(
            [
                (shift_at, shift),
                (count_at, count),
                (axis_at, axis),
                (pos_at, pos),
                (vel_at, vel),
                (mass_at, mass),
            ]
        )
    ]
    large = []
    for q in range(CX):
        part = pl.ds(SUB * q, SUB)
        large.append(pltpu.make_async_copy(occ_at.at[part], occ.at[part], osem.at[q]))
        large.append(pltpu.make_async_copy(v_at.at[:, part], v.at[:, part], vsem.at[q]))
    for copy in small[:2] + large[:2] + small[2:] + large[2:]:
        copy.start()
    for copy in small[:2]:
        copy.wait()
    sx, sy, sz = shift[0], shift[1], shift[2]
    row = lax.broadcasted_iota(jnp.int32, (2 * FY, FZ), 0)
    slot = (row & 1).astype(jnp.float32)
    low = (row[:8] < 8 - 2 * sy)[None]

    def plane(x, acc):
        live = twice[pl.ds(pl.multiple_of(x * 2 * FY, 2 * FY), 2 * FY), :] > slot
        masked = [jnp.where(live, v[c, x], 0.0) for c in range(3)] + [jnp.where(live, 1.0, 0.0)]
        return tuple(a + m for a, m in zip(acc, masked))

    zero = jnp.zeros((2 * FY, FZ), jnp.float32)
    blank = jnp.zeros((1, 8, FZ), jnp.float32)
    partial[:, :, 8:JP, :] = jnp.zeros((4, KX, JP - 8, FZ), jnp.float32)

    for k in range(KX):
        if k < CX:
            large[2 * k].wait()
            store_twice(occ, twice, k)
            large[2 * k + 1].wait()
        acc = (zero,) * 4
        if k == 0:
            acc = lax.fori_loop(0, SUB - sx, plane, acc)
        elif k == CX:
            acc = lax.fori_loop(FX - sx, FX, plane, acc)
        else:
            for j in range(SUB):
                acc = plane(k * SUB - sx + j, acc)
        for c in range(4):
            parts = acc[c].reshape(CY, 8, FZ)
            picked = jnp.where(
                low, jnp.concatenate([parts, blank]), jnp.concatenate([blank, parts])
            )
            partial[c, k, 0:JY, :] = jnp.sum(picked, axis=1)

    for copy in small[2:]:
        copy.wait()
    kx, jy, lz = colloid_cells(pos, sx, sy, sz)
    alive = live_row(count[0, 0]).astype(jnp.float32)
    weight = mass[0] * alive
    hit = lax.broadcasted_iota(jnp.int32, (ROWS, FZ), 0) == kx * JP + jy
    carried = [jnp.where(hit, vel[c] * weight, 0.0) for c in range(3)]
    carried.append(jnp.where(hit, weight, 0.0))
    target = lax.broadcasted_iota(jnp.int32, (CZ, FZ), 0)
    layer = lax.broadcasted_iota(jnp.int32, (CZ, FZ), 1)
    to_cell = (((layer + sz) & (FZ - 1)) >> 1 == target).astype(jnp.float32)
    to_place = (target == lz).astype(jnp.float32)
    one = jnp.concatenate([to_cell, to_place], axis=1)
    none = jnp.zeros_like(one)
    right = jnp.concatenate(
        [jnp.concatenate([one, none], axis=1), jnp.concatenate([none, one], axis=1)], axis=0
    )
    for p in range(2):
        left = jnp.concatenate(
            [
                partial[2 * p].reshape(ROWS, FZ),
                carried[2 * p],
                partial[2 * p + 1].reshape(ROWS, FZ),
                carried[2 * p + 1],
            ],
            axis=1,
        )
        total = exact_dot(left, right, NT)
        base[p * ROWS : p * ROWS + ROWS] = total
        last = CX * JP
        down[8 * p : 8 * p + 8] = total[0:8]
        down[16 + p : 17 + p] = total[8:9]
        up[8 * p : 8 * p + 8] = total[last : last + 8]
        up[16 + p : 17 + p] = total[last + 8 : last + 9]
    for packet in (up, down):
        for c in range(3):
            packet[18 + c : 19 + c] = pos[c]
        packet[21:22] = alive
        packet[22:24] = jnp.zeros((2, FZ), jnp.float32)
    for c in range(3):
        base[STATE + c : STATE + c + 1] = pos[c]
        base[STATE + 3 + c : STATE + 4 + c] = vel[c]
    base[STATE + 6 : STATE + 7] = mass[0]
    base[STATE + 7 : STATE + 8] = alive
    base[STATE + 8 : STATE + 9] = (kx * JP + jy).astype(jnp.float32)
    base[STATE + 9 : STATE + 10] = lz.astype(jnp.float32)
    base[STATE + 10 : STATE + 16] = jnp.zeros((6, FZ), jnp.float32)
    base[NUMBERS : NUMBERS + ROWS] = jnp.zeros((ROWS, FZ), jnp.float32)
    for k in range(CX):
        number = axis[k].astype(jnp.float32)
        number = jnp.concatenate([number, number], axis=1)
        base[NUMBERS + JP * k : NUMBERS + JP * k + CY] = number
        if k == 0:
            down[24:32] = number


def cell_sums(grid_shift, count, v, occ, axis_index, pos, vel, mass):
    return pl.pallas_call(
        sums_kernel,
        out_shape=(
            struct(BASE, FZ),
            struct(24, FZ),
            struct(32, FZ),
        ),
        in_specs=[HBM] * 8,
        out_specs=(IN_VMEM,) * 3,
        scratch_shapes=[
            SMEM((3,), jnp.int32),
            SMEM((1, 1), jnp.int32),
            VMEM((3, FX, 2 * FY, FZ), jnp.float32),
            VMEM((FX, FY, FZ), jnp.int32),
            VMEM((CX, CY, CZ), jnp.int32),
            VMEM((3, 1, FZ), jnp.float32),
            VMEM((3, 1, FZ), jnp.float32),
            VMEM((1, 1, FZ), jnp.float32),
            VMEM((2 * FX * FY, FZ), jnp.float32),
            VMEM((4, KX, JP, FZ), jnp.float32),
            DMA((6,)),
            DMA((CX,)),
            DMA((CX,)),
        ],
        cost_estimate=pl.CostEstimate(flops=4_000_000, bytes_accessed=3_700_000, transcendentals=0),
        name="cell_sums",
    )(grid_shift, count, v, occ, axis_index, pos, vel, mass)


def prepare_kernel(base, part, state, numbers):
    part[...] = base[0:STATE]
    state[...] = base[STATE:NUMBERS]
    numbers[...] = base[NUMBERS:BASE]


def prepare(base):
    return pl.pallas_call(
        prepare_kernel,
        out_shape=(struct(STATE, FZ), struct(16, FZ), struct(ROWS, FZ)),
        in_specs=[IN_VMEM],
        out_specs=(IN_VMEM,) * 3,
        compiler_params=pltpu.CompilerParams(vmem_limit_bytes=SMALL_LIMIT),
        cost_estimate=pl.CostEstimate(flops=10_000, bytes_accessed=460_000, transcendentals=0),
        name="prepare",
    )(base)


def add_x(part, up, down, full):
    for p in range(2):
        base = p * ROWS
        full[base : base + ROWS] = part[base : base + ROWS]
        full[base : base + 8] += up[8 * p : 8 * p + 8]
        full[base + 8 : base + 9] += up[16 + p : 17 + p]
        last = base + CX * JP
        full[last : last + 8] += down[8 * p : 8 * p + 8]
        full[last + 8 : last + 9] += down[16 + p : 17 + p]


def columns_kernel(part, up1, down1, state, numbers, up, down, full):
    add_x(part, up1, down1, full)
    for p in range(2):
        down[9 * p : 9 * p + 9] = full[pl.ds(p * ROWS, KX, JP), :]
        up[9 * p : 9 * p + 9] = full[pl.ds(p * ROWS + 8, KX, JP), :]
    for packet in (up, down):
        packet[18:22] = up1[18:22]
        packet[22:25] = state[0:3]
        packet[25:26] = state[7:8]
        packet[26:30] = down1[18:22]
    up[30:32] = jnp.zeros((2, FZ), jnp.float32)
    down[30:38] = numbers[pl.ds(0, CX, JP), :]
    down[38:39] = down1[24:25]
    down[39:40] = jnp.zeros((1, FZ), jnp.float32)


def columns(part, up1, down1, state, numbers):
    return pl.pallas_call(
        columns_kernel,
        out_shape=(struct(32, FZ), struct(40, FZ)),
        in_specs=[IN_VMEM] * 5,
        out_specs=(IN_VMEM,) * 2,
        scratch_shapes=[VMEM((2 * ROWS, FZ), jnp.float32)],
        compiler_params=pltpu.CompilerParams(vmem_limit_bytes=SMALL_LIMIT),
        cost_estimate=pl.CostEstimate(flops=100_000, bytes_accessed=500_000, transcendentals=0),
        name="columns",
    )(part, up1, down1, state, numbers)


def pair_force(own, others, rows, terms):
    for i, other in enumerate(others):
        for c in range(4):
            rows[4 * i + c] = jnp.broadcast_to(other[c], (8, FZ))
    column = jnp.concatenate(list(own) + [jnp.zeros((5, FZ), jnp.float32)], axis=0).T
    for t in range(FZ // 16):
        part = column[16 * t : 16 * t + 16]
        mine = [
            jnp.broadcast_to(part[:, c : c + 1], (16, FZ)).reshape(2, 8, FZ) for c in range(3)
        ]
        total = None
        for i in range(len(others)):
            dx = mine[0] - rows[4 * i][None]
            dy = mine[1] - rows[4 * i + 1][None]
            dz = mine[2] - rows[4 * i + 2][None]
            dz = jnp.where(
                dz > 0.5 * CZ, dz - CZ, jnp.where(dz < -0.5 * CZ, dz + CZ, dz)
            )
            reach = jnp.maximum(
                rows[4 * i + 3][None]
                - (dx * dx + dy * dy + dz * dz) * (1.0 / (cutoff * cutoff)),
                0.0,
            )
            weight = reach * reach
            new = (weight * dx, weight * dy, weight * dz)
            total = new if total is None else tuple(a + b for a, b in zip(total, new))
        for c in range(3):
            terms[FZ * c + 16 * t : FZ * c + 16 * t + 16] = total[c].reshape(16, FZ)
    ones = jnp.ones((8, FZ), jnp.bfloat16)
    left = terms[...]
    back = None
    for part in range(3):
        piece = left.astype(jnp.bfloat16)
        term = lax.dot_general(ones, piece, NT, preferred_element_type=jnp.float32)
        back = term if back is None else back + term
        if part < 2:
            left = left - piece.astype(jnp.float32)
    return [stiffness * back[0:1, FZ * c : FZ * c + FZ] for c in range(3)]


PAIR_SCRATCH = [VMEM((36, 8, FZ), jnp.float32), VMEM((3 * FZ, FZ), jnp.float32)]


def around(column, live):
    others = []
    for b in range(3):
        for a in range(3):
            x, y, z = column(b, a)
            limit = jnp.where(live(b, a) > 0.0, 1.0, -1.0)
            others.append((x + (a - 1) * float(CX), y + (b - 1) * float(CY), z, limit))
    return others


def advance(own, velocity, mass, others, rows, terms):
    force = pair_force(own, others, rows, terms)
    velocity = [velocity[c] + timestep * force[c] / mass for c in range(3)]
    return [own[c] + timestep * velocity[c] for c in range(3)], velocity


def fields_kernel(
    part, up1, down1, up2, down2, state, numbers_in,
    field_out, live_out, vel_out, pos_out,
    full, numbers, pair_rows, pair_terms,
):
    add_x(part, up1, down1, full)
    for p in range(2):
        first = pl.ds(p * ROWS, KX, JP)
        full[first, :] = full[first, :] + up2[9 * p : 9 * p + 9]
        last = pl.ds(p * ROWS + 8, KX, JP)
        full[last, :] = full[last, :] + down2[9 * p : 9 * p + 9]
    numbers[...] = numbers_in[...]
    numbers[JP * CX : JP * CX + 8] = down1[24:32]
    numbers[pl.ds(8, KX, JP), :] = down2[30:39]

    lane = lax.broadcasted_iota(jnp.int32, (8, FZ), 1)
    number = (lane & (DIRECTIONS - 1)).astype(jnp.float32)
    height = 1.0 - (2.0 * number + 1.0) / DIRECTIONS
    radius = jnp.sqrt(1.0 - height * height)
    phase = number * golden
    index = numbers[...].astype(jnp.int32)
    n0, n1, n2 = [
        jnp.take_along_axis(jnp.broadcast_to(table[0:1], (ROWS, FZ)), index, axis=1)
        for table in (radius * jnp.cos(phase), radius * jnp.sin(phase), height)
    ]

    lower = lax.broadcasted_iota(jnp.int32, (ROWS, FZ), 1) < CZ
    first, second = full[0:ROWS], full[ROWS : 2 * ROWS]
    heavy = jnp.maximum(jnp.where(lower, pltpu.roll(second, CZ, 1), second), fill_mass)
    mean_xy = first / heavy
    mean_z = second / heavy
    mean_yx = pltpu.roll(mean_xy, CZ, 1)
    mean_z_up = pltpu.roll(mean_z, CZ, 1)
    turn = 1.0 - cos_angle
    t0, t1, t2 = turn * n0, turn * n1, turn * n2
    s0, s1, s2 = sin_angle * n0, sin_angle * n1, sin_angle * n2
    field_out[0] = jnp.where(lower, cos_angle + t0 * n0, t0 * n1 - s2)
    field_out[1] = jnp.where(lower, t0 * n2 + s1, t0 * n1 + s2)
    field_out[2] = jnp.where(lower, cos_angle + t1 * n1, t1 * n2 - s0)
    field_out[3] = jnp.where(lower, t0 * n2 - s1, t1 * n2 + s0)
    field_out[4] = jnp.where(lower, cos_angle + t2 * n2, mean_yx)
    field_out[5] = jnp.where(lower, mean_yx, mean_z_up)

    place = state[8:9].astype(jnp.int32)
    lz = state[9:10].astype(jnp.int32)
    to_place = (lax.broadcasted_iota(jnp.int32, (CZ, FZ), 0) == lz).astype(jnp.float32)
    none = jnp.zeros_like(to_place)
    right = jnp.concatenate(
        [jnp.concatenate([to_place, none], axis=1), jnp.concatenate([none, to_place], axis=1)],
        axis=0,
    )
    hit = lax.broadcasted_iota(jnp.int32, (ROWS, FZ), 0) == place
    picked = []
    for pair in (mean_xy, jnp.where(lower, mean_z, n0), jnp.where(lower, n1, n2)):
        at_z = exact_dot(pair, right, NN)
        for half in (at_z[:, :FZ], at_z[:, FZ:]):
            picked.append(jnp.sum(jnp.where(hit, half, 0.0), axis=0, keepdims=True))
    u, n = picked[:3], picked[3:]
    alive = state[7:8] > 0.0
    old = [state[3 + c : 4 + c] for c in range(3)]
    rel = [old[c] - u[c] for c in range(3)]
    cross = [n[1] * rel[2] - n[2] * rel[1], n[2] * rel[0] - n[0] * rel[2], n[0] * rel[1] - n[1] * rel[0]]
    along = n[0] * rel[0] + n[1] * rel[1] + n[2] * rel[2]
    velocity = [
        jnp.where(
            alive,
            u[c] + cos_angle * rel[c] + sin_angle * cross[c] + turn * along * n[c],
            old[c],
        )
        for c in range(3)
    ]

    own = [state[c : c + 1] for c in range(3)]
    alive_row = state[7:8]

    def rows(b, a):
        if b == 1 and a == 1:
            return own + [alive_row]
        if b == 1:
            source, base = (up1, 18) if a == 0 else (down1, 18)
        else:
            source, base = (up2 if b == 0 else down2), 18 + 4 * a
        return [source[base + c : base + c + 1] for c in range(4)]

    live_out[9:16] = state[0:7]
    for b in range(3):
        for a in range(3):
            live_out[3 * b + a : 3 * b + a + 1] = rows(b, a)[3]
    others = around(lambda b, a: rows(b, a)[:3], lambda b, a: rows(b, a)[3])
    moved, velocity = advance(own, velocity, state[6:7], others, pair_rows, pair_terms)
    for c in range(3):
        vel_out[c : c + 1] = velocity[c]
        pos_out[c : c + 1] = moved[c]
    vel_out[3:4] = jnp.zeros((1, FZ), jnp.float32)
    pos_out[3:4] = jnp.zeros((1, FZ), jnp.float32)


def cell_fields(part, up1, down1, up2, down2, state, numbers):
    return pl.pallas_call(
        fields_kernel,
        out_shape=(struct(6, ROWS, FZ), struct(16, FZ), struct(4, FZ), struct(4, FZ)),
        in_specs=[IN_VMEM] * 7,
        out_specs=(IN_VMEM,) * 4,
        scratch_shapes=[
            VMEM((2 * ROWS, FZ), jnp.float32),
            VMEM((ROWS, FZ), jnp.float32),
            *PAIR_SCRATCH,
        ],
        compiler_params=pltpu.CompilerParams(vmem_limit_bytes=SMALL_LIMIT),
        cost_estimate=pl.CostEstimate(flops=4_000_000, bytes_accessed=1_000_000, transcendentals=0),
        name="cell_fields",
    )(part, up1, down1, up2, down2, state, numbers)


def substep_moves(rest, own, column, up, down, vel, rows, terms):
    mine = [own[c : c + 1] for c in range(3)]
    old = [vel[c : c + 1] for c in range(3)]
    source = (up, column, down)
    others = around(
        lambda b, a: [source[b][4 * a + c : 4 * a + c + 1] for c in range(3)],
        lambda b, a: rest[3 * b + a : 3 * b + a + 1],
    )
    return advance(mine, old, rest[15:16], others, rows, terms)


def substep_kernel(rest, own, column, up, down, vel, vel_out, pos_out, rows, terms):
    moved, velocity = substep_moves(rest, own, column, up, down, vel, rows, terms)
    for c in range(3):
        vel_out[c : c + 1] = velocity[c]
        pos_out[c : c + 1] = moved[c]
    vel_out[3:4] = jnp.zeros((1, FZ), jnp.float32)
    pos_out[3:4] = jnp.zeros((1, FZ), jnp.float32)


def last_kernel(rest, own, column, up, down, vel, vel_out, pos_out, rows, terms):
    moved, velocity = substep_moves(rest, own, column, up, down, vel, rows, terms)
    keep = rest[4:5] > 0.0
    for c in range(3):
        pos_out[c] = jnp.where(keep, moved[c], rest[9 + c : 10 + c])
        vel_out[c] = jnp.where(keep, velocity[c], rest[12 + c : 13 + c])


def substep(kernel, shape, rest, own, column, up, down, vel):
    return pl.pallas_call(
        kernel,
        out_shape=(struct(*shape), struct(*shape)),
        in_specs=[IN_VMEM] * 6,
        out_specs=(IN_VMEM,) * 2,
        scratch_shapes=PAIR_SCRATCH,
        compiler_params=pltpu.CompilerParams(vmem_limit_bytes=SMALL_LIMIT),
        cost_estimate=pl.CostEstimate(flops=4_000_000, bytes_accessed=30_000, transcendentals=0),
        name="substep",
    )(rest, own, column, up, down, vel)


def turn_kernel(shift_at, v_at, occ_at, field, out_at, shift, v, occ, out, twice, wide, sem, vsem, osem, wsem):
    first = pltpu.make_async_copy(shift_at, shift, sem.at[0])
    first.start()
    large = []
    stores = []
    for q in range(CX):
        part = pl.ds(SUB * q, SUB)
        large.append(pltpu.make_async_copy(occ_at.at[part], occ.at[part], osem.at[q]))
        large.append(pltpu.make_async_copy(v_at.at[:, part], v.at[:, part], vsem.at[q]))
        stores.append(pltpu.make_async_copy(out.at[:, part], out_at.at[:, part], wsem.at[q]))
    for copy in large:
        copy.start()
    first.wait()
    sx, sy, sz = shift[0], shift[1], shift[2]
    source = lax.broadcasted_iota(jnp.int32, (CZ, FZ), 0)
    layer = lax.broadcasted_iota(jnp.int32, (CZ, FZ), 1)
    spread = (((layer + sz) & (FZ - 1)) >> 1 == source).astype(jnp.float32)
    none = jnp.zeros_like(spread)
    right = jnp.concatenate(
        [jnp.concatenate([spread, none], axis=1), jnp.concatenate([none, spread], axis=1)],
        axis=0,
    )
    for f in range(6):
        both = exact_dot(field[f], right, NN)
        wide[2 * f] = both[:, :FZ]
        wide[2 * f + 1] = both[:, FZ:]
    row = lax.broadcasted_iota(jnp.int32, (8, FZ), 0)
    slot = (row & 1).astype(jnp.float32)
    low = row < 8 - 2 * sy

    for k in range(KX):
        if k < CX:
            large[2 * k].wait()
            store_twice(occ, twice, k)
            large[2 * k + 1].wait()

        def column(t, carry, k=k):
            f = [
                jnp.where(
                    low, wide[i, pl.ds(k * JP + t, 1), :], wide[i, pl.ds(k * JP + t + 1, 1), :]
                )
                for i in range(12)
            ]
            rows = pl.ds(pl.multiple_of(8 * t, 8), 8)

            def plane(x, carry):
                live = twice[pl.ds(pl.multiple_of(x * 2 * FY + 8 * t, 8), 8), :] > slot
                old = [v[c, x, rows, :] for c in range(3)]
                rel = [old[c] - f[9 + c] for c in range(3)]
                for c in range(3):
                    new = f[9 + c] + (
                        f[3 * c] * rel[0] + f[3 * c + 1] * rel[1] + f[3 * c + 2] * rel[2]
                    )
                    out[c, x, rows, :] = jnp.where(live, new, old[c])
                return carry

            if k == 0:
                lax.fori_loop(0, SUB - sx, plane, 0)
            elif k == CX:
                lax.fori_loop(FX - sx, FX, plane, 0)
            else:
                for j in range(SUB):
                    plane(k * SUB - sx + j, 0)
            return carry

        lax.fori_loop(0, CY, column, 0)
        if k:
            stores[k - 1].start()
    for copy in stores:
        copy.wait()


def turn_solvent(grid_shift, v, occ, field):
    return pl.pallas_call(
        turn_kernel,
        out_shape=struct(*v.shape),
        in_specs=[HBM, HBM, HBM, IN_VMEM],
        out_specs=HBM,
        scratch_shapes=[
            SMEM((3,), jnp.int32),
            VMEM((3, FX, 2 * FY, FZ), jnp.float32),
            VMEM((FX, FY, FZ), jnp.int32),
            VMEM((3, FX, 2 * FY, FZ), jnp.float32),
            VMEM((2 * FX * FY, FZ), jnp.float32),
            VMEM((12, ROWS, FZ), jnp.float32),
            DMA((1,)),
            DMA((CX,)),
            DMA((CX,)),
            DMA((CX,)),
        ],
        compiler_params=pltpu.CompilerParams(vmem_limit_bytes=TURN_LIMIT),
        cost_estimate=pl.CostEstimate(flops=8_000_000, bytes_accessed=7_000_000, transcendentals=0),
        name="turn_solvent",
    )(grid_shift, v, occ, field)


def per_device(
    solvent_vel,
    occupancy,
    grid_shift,
    axis_index,
    colloid_pos,
    colloid_vel,
    colloid_mass,
    colloid_count,
):
    v = solvent_vel.reshape(3, FX, 2 * FY, FZ)
    pos = colloid_pos.reshape(3, 1, FZ)
    vel = colloid_vel.reshape(3, 1, FZ)
    mass = colloid_mass
    count = colloid_count

    base, up, down = cell_sums(grid_shift, count, v, occupancy, axis_index, pos, vel, mass)
    up1, down1 = shifted(up, "gx", 1), shifted(down, "gx", -1)
    part, state, numbers = prepare(base)
    up, down = columns(part, up1, down1, state, numbers)
    up2, down2 = shifted(up, "yz", 1), shifted(down, "yz", -1)
    field, rest, velocity, position = cell_fields(part, up1, down1, up2, down2, state, numbers)
    solvent_out = turn_solvent(grid_shift, v, occupancy, field)
    for step in range(1, SUBSTEPS):
        column = jnp.concatenate([shifted(position, "gx", 1), position, shifted(position, "gx", -1)])
        up, down = shifted(column, "yz", 1), shifted(column, "yz", -1)
        kernel, shape = (
            (substep_kernel, (4, FZ)) if step < SUBSTEPS - 1 else (last_kernel, (3, 1, FZ))
        )
        velocity, position = substep(
            kernel, shape, rest, position, column, up, down, velocity
        )
    return (
        solvent_out.reshape(solvent_vel.shape),
        position[:, None],
        velocity[:, None],
    )


def solution(mesh):
    return jax.shard_map(
        per_device,
        mesh=mesh,
        in_specs=(
            P(None, "gx", "yz", None, None),
            P("gx", "yz", None),
            P(),
            P("gx", "yz", None),
            P(None, "gx", "yz", None),
            P(None, "gx", "yz", None),
            P("gx", "yz", None),
            P("gx", "yz"),
        ),
        out_specs=(
            P(None, "gx", "yz", None, None),
            P(None, "gx", "yz", None),
            P(None, "gx", "yz", None),
        ),
        check_vma=False,
    )
```

```python
import functools
import math

import jax
import jax.numpy as jnp
from jax import lax
from jax.experimental import pallas as pl
from jax.experimental.pallas import tpu as pltpu
from jax.sharding import PartitionSpec as P

CX = 8
CY = 8
CZ = 64
SUB = 4
SUBSTEPS = 4
DIRECTIONS = 64
FX = 32
FY = 32
FZ = 128
KX = CX + 1
JY = CY + 1
JP = 16
ROWS = KX * JP

turn_angle = 130.0 * math.pi / 180.0
cos_angle = math.cos(turn_angle)
sin_angle = math.sin(turn_angle)
golden = math.pi * (3.0 - math.sqrt(5.0))
cutoff = 1.5
stiffness = 20.0
timestep = 0.05
fill_mass = 16.0

SMEM = pltpu.SMEM
VMEM = pltpu.VMEM
HBM = pl.BlockSpec(memory_space=pltpu.HBM)
IN_VMEM = pl.BlockSpec(memory_space=VMEM)
IN_SMEM = pl.BlockSpec(memory_space=SMEM)
DMA = pltpu.SemaphoreType.DMA
NT = (((1,), (1,)), ((), ()))
NN = (((1,), (0,)), ((), ()))
STATE = 2 * ROWS
NUMBERS = STATE + 16
BASE = NUMBERS + ROWS
TURNED = ((1, 2, 3), (4, 5, 6), (7, CX))
TILE = 32
SMALL_LIMIT = 8 * 1024 * 1024
TURN_LIMIT = 16 * 1024 * 1024


def swapped(value, axis, first):
    count = lax.axis_size(axis)
    pairs = []
    for low in range(first, count + first, 2):
        a, b = low % count, (low + 1) % count
        pairs += [(a, b), (b, a)]
    return lax.ppermute(value, axis, pairs)


def swap_both(odd, even, axis):
    return swapped(odd, axis, 1), swapped(even, axis, 0)


def struct(*shape):
    return jax.ShapeDtypeStruct(shape, jnp.float32)


def exact_dot(left, right, dims):
    right = right.astype(jnp.bfloat16)
    total = None
    for part in range(3):
        piece = left.astype(jnp.bfloat16)
        term = lax.dot_general(piece, right, dims, preferred_element_type=jnp.float32)
        total = term if total is None else total + term
        if part < 2:
            left = left - piece.astype(jnp.float32)
    return total


def colloid_cells(pos, sx, sy, sz):
    cell_x = jnp.clip(jnp.floor(pos[0] * SUB).astype(jnp.int32), 0, FX - 1)
    cell_y = jnp.clip(jnp.floor(pos[1] * SUB).astype(jnp.int32), 0, FY - 1)
    cell_z = jnp.clip(jnp.floor(pos[2] * 2.0).astype(jnp.int32), 0, FZ - 1)
    return ((cell_x + sx) >> 2, (cell_y + sy) >> 2, ((cell_z + sz) & (FZ - 1)) >> 1)


def live_row(count):
    return lax.broadcasted_iota(jnp.int32, (1, FZ), 1) < count


def store_twice(occ, twice, q):
    slots = occ[SUB * q : SUB * q + SUB].reshape(SUB * FY, FZ).astype(jnp.float32)
    base = 2 * SUB * FY * q
    twice[pl.ds(base, SUB * FY, 2), :] = slots
    twice[pl.ds(base + 1, SUB * FY, 2), :] = slots


def parity(axis):
    return lax.axis_index(axis) & 1


def sums_kernel(
    shift_at, count_at, v_at, occ_at, axis_at, pos_at, vel_at, mass_at,
    base, odd, even,
    shift, count, v, occ, axis, pos, vel, mass, twice, partial, sem, vsem, osem,
):
    small = [
        pltpu.make_async_copy(a, b, sem.at[i])
        for i, (a, b) in enumerate(
            [
                (shift_at, shift),
                (count_at, count),
                (axis_at, axis),
                (pos_at, pos),
                (vel_at, vel),
                (mass_at, mass),
            ]
        )
    ]
    large = []
    for q in range(CX):
        part = pl.ds(SUB * q, SUB)
        large.append(pltpu.make_async_copy(occ_at.at[part], occ.at[part], osem.at[q]))
        large.append(pltpu.make_async_copy(v_at.at[:, part], v.at[:, part], vsem.at[q]))
    for copy in small[:2] + large[:2] + small[2:] + large[2:]:
        copy.start()
    for copy in small[:2]:
        copy.wait()
    sx, sy, sz = shift[0], shift[1], shift[2]
    row = lax.broadcasted_iota(jnp.int32, (2 * FY, FZ), 0)
    slot = (row & 1).astype(jnp.float32)
    low = (row[:8] < 8 - 2 * sy)[None]

    def plane(x, acc):
        live = twice[pl.ds(pl.multiple_of(x * 2 * FY, 2 * FY), 2 * FY), :] > slot
        masked = [jnp.where(live, v[c, x], 0.0) for c in range(3)] + [jnp.where(live, 1.0, 0.0)]
        return tuple(a + m for a, m in zip(acc, masked))

    zero = jnp.zeros((2 * FY, FZ), jnp.float32)
    blank = jnp.zeros((1, 8, FZ), jnp.float32)
    partial[:, :, 8:JP, :] = jnp.zeros((4, KX, JP - 8, FZ), jnp.float32)

    for k in range(KX):
        if k < CX:
            large[2 * k].wait()
            store_twice(occ, twice, k)
            large[2 * k + 1].wait()
        acc = (zero,) * 4
        if k == 0:
            acc = lax.fori_loop(0, SUB - sx, plane, acc)
        elif k == CX:
            acc = lax.fori_loop(FX - sx, FX, plane, acc)
        else:
            for j in range(SUB):
                acc = plane(k * SUB - sx + j, acc)
        for c in range(4):
            parts = acc[c].reshape(CY, 8, FZ)
            picked = jnp.where(
                low, jnp.concatenate([parts, blank]), jnp.concatenate([blank, parts])
            )
            partial[c, k, 0:JY, :] = jnp.sum(picked, axis=1)

    for copy in small[2:]:
        copy.wait()
    kx, jy, lz = colloid_cells(pos, sx, sy, sz)
    alive = live_row(count[0, 0]).astype(jnp.float32)
    weight = mass[0] * alive
    hit = lax.broadcasted_iota(jnp.int32, (ROWS, FZ), 0) == kx * JP + jy
    carried = [jnp.where(hit, vel[c] * weight, 0.0) for c in range(3)]
    carried.append(jnp.where(hit, weight, 0.0))
    target = lax.broadcasted_iota(jnp.int32, (CZ, FZ), 0)
    layer = lax.broadcasted_iota(jnp.int32, (CZ, FZ), 1)
    to_cell = (((layer + sz) & (FZ - 1)) >> 1 == target).astype(jnp.float32)
    to_place = (target == lz).astype(jnp.float32)
    one = jnp.concatenate([to_cell, to_place], axis=1)
    none = jnp.zeros_like(one)
    right = jnp.concatenate(
        [jnp.concatenate([one, none], axis=1), jnp.concatenate([none, one], axis=1)], axis=0
    )
    for p in range(2):
        left = jnp.concatenate(
            [
                partial[2 * p].reshape(ROWS, FZ),
                carried[2 * p],
                partial[2 * p + 1].reshape(ROWS, FZ),
                carried[2 * p + 1],
            ],
            axis=1,
        )
        total = exact_dot(left, right, NT)
        base[p * ROWS : p * ROWS + ROWS] = total
    turned = parity("gx") * (CX * JP)
    for p in range(2):
        for packet, place in ((odd, turned), (even, CX * JP - turned)):
            start = pl.multiple_of(p * ROWS + place, JP)
            packet[8 * p : 8 * p + 8] = base[pl.ds(start, 8), :]
            packet[16 + p : 17 + p] = base[pl.ds(start + 8, 1), :]
    for packet in (odd, even):
        for c in range(3):
            packet[18 + c : 19 + c] = pos[c]
        packet[21:22] = alive
        packet[22:24] = jnp.zeros((2, FZ), jnp.float32)
    for c in range(3):
        base[STATE + c : STATE + c + 1] = pos[c]
        base[STATE + 3 + c : STATE + 4 + c] = vel[c]
    base[STATE + 6 : STATE + 7] = mass[0]
    base[STATE + 7 : STATE + 8] = alive
    base[STATE + 8 : STATE + 9] = (kx * JP + jy).astype(jnp.float32)
    base[STATE + 9 : STATE + 10] = lz.astype(jnp.float32)
    base[STATE + 10 : STATE + 16] = jnp.zeros((6, FZ), jnp.float32)
    base[NUMBERS : NUMBERS + ROWS] = jnp.zeros((ROWS, FZ), jnp.float32)
    for k in range(CX):
        number = axis[k].astype(jnp.float32)
        number = jnp.concatenate([number, number], axis=1)
        base[NUMBERS + JP * k : NUMBERS + JP * k + CY] = number
        if k == 0:
            odd[24:32] = number
            even[24:32] = number


def cell_sums(grid_shift, count, v, occ, axis_index, pos, vel, mass):
    return pl.pallas_call(
        sums_kernel,
        out_shape=(
            struct(BASE, FZ),
            struct(32, FZ),
            struct(32, FZ),
        ),
        in_specs=[HBM] * 8,
        out_specs=(IN_VMEM,) * 3,
        scratch_shapes=[
            SMEM((3,), jnp.int32),
            SMEM((1, 1), jnp.int32),
            VMEM((3, FX, 2 * FY, FZ), jnp.float32),
            VMEM((FX, FY, FZ), jnp.int32),
            VMEM((CX, CY, CZ), jnp.int32),
            VMEM((3, 1, FZ), jnp.float32),
            VMEM((3, 1, FZ), jnp.float32),
            VMEM((1, 1, FZ), jnp.float32),
            VMEM((2 * FX * FY, FZ), jnp.float32),
            VMEM((4, KX, JP, FZ), jnp.float32),
            DMA((6,)),
            DMA((CX,)),
            DMA((CX,)),
        ],
        cost_estimate=pl.CostEstimate(flops=4_000_000, bytes_accessed=3_700_000, transcendentals=0),
        name="cell_sums",
    )(grid_shift, count, v, occ, axis_index, pos, vel, mass)


def prepare_kernel(base, part, state, numbers):
    part[...] = base[0:STATE]
    state[...] = base[STATE:NUMBERS]
    numbers[...] = base[NUMBERS:BASE]


def prepare(base):
    return pl.pallas_call(
        prepare_kernel,
        out_shape=(struct(STATE, FZ), struct(16, FZ), struct(ROWS, FZ)),
        in_specs=[IN_VMEM],
        out_specs=(IN_VMEM,) * 3,
        compiler_params=pltpu.CompilerParams(vmem_limit_bytes=SMALL_LIMIT),
        cost_estimate=pl.CostEstimate(flops=10_000, bytes_accessed=460_000, transcendentals=0),
        name="prepare",
    )(base)


def add_x(part, odd, even, full):
    full[...] = part[...]
    turned = parity("gx") * (CX * JP)
    for p in range(2):
        for packet, place in ((odd, turned), (even, CX * JP - turned)):
            start = pl.multiple_of(p * ROWS + place, JP)
            full[pl.ds(start, 8), :] += packet[8 * p : 8 * p + 8]
            full[pl.ds(start + 8, 1), :] += packet[16 + p : 17 + p]


def later_x(odd, even, rows):
    return jnp.where(parity("gx") == 1, odd[rows], even[rows])


def columns_kernel(part, odd1, even1, state, numbers, odd, even, full, ends):
    add_x(part, odd1, even1, full)
    for p in range(2):
        ends[0, 9 * p : 9 * p + 9] = full[pl.ds(p * ROWS, KX, JP), :]
        ends[1, 9 * p : 9 * p + 9] = full[pl.ds(p * ROWS + 8, KX, JP), :]
    side = parity("yz")
    for packet, end in ((odd, side), (even, 1 - side)):
        packet[0:18] = ends[end, 0:18]
        packet[18:22] = odd1[18:22]
        packet[22:25] = state[0:3]
        packet[25:26] = state[7:8]
        packet[26:30] = even1[18:22]
        packet[30:38] = numbers[pl.ds(0, CX, JP), :]
        packet[38:39] = later_x(odd1, even1, slice(24, 25))
        packet[39:40] = jnp.zeros((1, FZ), jnp.float32)


def columns(part, odd1, even1, state, numbers):
    return pl.pallas_call(
        columns_kernel,
        out_shape=(struct(40, FZ), struct(40, FZ)),
        in_specs=[IN_VMEM] * 5,
        out_specs=(IN_VMEM,) * 2,
        scratch_shapes=[VMEM((2 * ROWS, FZ), jnp.float32), VMEM((2, 24, FZ), jnp.float32)],
        compiler_params=pltpu.CompilerParams(vmem_limit_bytes=SMALL_LIMIT),
        cost_estimate=pl.CostEstimate(flops=100_000, bytes_accessed=500_000, transcendentals=0),
        name="columns",
    )(part, odd1, even1, state, numbers)


def pair_force(count, own, others, rows, terms):
    for i, other in enumerate(others):
        for c in range(4):
            rows[4 * i + c] = jnp.broadcast_to(other[c], (8, FZ))
    column = jnp.concatenate(list(own) + [jnp.zeros((5, FZ), jnp.float32)], axis=0).T
    rows_at = TILE // 8

    def tile(t):
        part = column[TILE * t : TILE * t + TILE]
        mine = [
            jnp.broadcast_to(part[:, c : c + 1], (TILE, FZ)).reshape(rows_at, 8, FZ)
            for c in range(3)
        ]
        total = None
        for i in range(len(others)):
            dx = mine[0] - rows[4 * i][None]
            dy = mine[1] - rows[4 * i + 1][None]
            dz = mine[2] - rows[4 * i + 2][None]
            dz = jnp.where(
                dz > 0.5 * CZ, dz - CZ, jnp.where(dz < -0.5 * CZ, dz + CZ, dz)
            )
            reach = jnp.maximum(
                rows[4 * i + 3][None]
                - (dx * dx + dy * dy + dz * dz) * (1.0 / (cutoff * cutoff)),
                0.0,
            )
            weight = reach * reach
            new = (weight * dx, weight * dy, weight * dz)
            total = new if total is None else tuple(a + b for a, b in zip(total, new))
        for c in range(3):
            terms[FZ * c + TILE * t : FZ * c + TILE * t + TILE] = total[c].reshape(TILE, FZ)

    for t in range(FZ // TILE):
        if TILE * t < 21:
            tile(t)
        else:
            pl.when(TILE * t < count)(functools.partial(tile, t))
    ones = jnp.ones((8, FZ), jnp.bfloat16)
    slot = lax.broadcasted_iota(jnp.int32, (FZ, FZ), 0) < count
    left = jnp.where(jnp.concatenate([slot] * 3), terms[...], 0.0)
    back = None
    for part in range(3):
        piece = left.astype(jnp.bfloat16)
        term = lax.dot_general(ones, piece, NT, preferred_element_type=jnp.float32)
        back = term if back is None else back + term
        if part < 2:
            left = left - piece.astype(jnp.float32)
    return [stiffness * back[0:1, FZ * c : FZ * c + FZ] for c in range(3)]


PAIR_SCRATCH = [VMEM((36, 8, FZ), jnp.float32), VMEM((3 * FZ, FZ), jnp.float32)]


def around(column, live):
    toward_x = ((2 * parity("gx") - 1) * CX).astype(jnp.float32)
    toward_y = ((2 * parity("yz") - 1) * CY).astype(jnp.float32)
    others = []
    for b in range(3):
        for a in range(3):
            x, y, z = column(b, a)
            limit = jnp.where(live(b, a) > 0.0, 1.0, -1.0)
            others.append((x + (1 - a) * toward_x, y + (1 - b) * toward_y, z, limit))
    return others


def advance(count, own, velocity, mass, others, rows, terms):
    live = live_row(count)
    force = [jnp.where(live, f, 0.0) for f in pair_force(count, own, others, rows, terms)]
    velocity = [velocity[c] + timestep * force[c] / mass for c in range(3)]
    return [own[c] + timestep * velocity[c] for c in range(3)], velocity


def fields_kernel(
    count, part, odd1, even1, odd2, even2, state, numbers_in,
    field_out, live_out, vel_out, pos_out,
    full, numbers, pair_rows, pair_terms,
):
    add_x(part, odd1, even1, full)
    forward = parity("yz") == 1
    for p in range(2):
        rows = slice(9 * p, 9 * p + 9)
        first = pl.ds(p * ROWS, KX, JP)
        full[first, :] = full[first, :] + jnp.where(forward, even2[rows], odd2[rows])
        last = pl.ds(p * ROWS + 8, KX, JP)
        full[last, :] = full[last, :] + jnp.where(forward, odd2[rows], even2[rows])
    numbers[...] = numbers_in[...]
    numbers[JP * CX : JP * CX + 8] = later_x(odd1, even1, slice(24, 32))
    numbers[pl.ds(8, KX, JP), :] = jnp.where(forward, odd2[30:39], even2[30:39])

    lane = lax.broadcasted_iota(jnp.int32, (8, FZ), 1)
    number = (lane & (DIRECTIONS - 1)).astype(jnp.float32)
    height = 1.0 - (2.0 * number + 1.0) / DIRECTIONS
    radius = jnp.sqrt(1.0 - height * height)
    phase = number * golden
    index = numbers[...].astype(jnp.int32)
    n0, n1, n2 = [
        jnp.take_along_axis(jnp.broadcast_to(table[0:1], (ROWS, FZ)), index, axis=1)
        for table in (radius * jnp.cos(phase), radius * jnp.sin(phase), height)
    ]

    lower = lax.broadcasted_iota(jnp.int32, (ROWS, FZ), 1) < CZ
    first, second = full[0:ROWS], full[ROWS : 2 * ROWS]
    heavy = jnp.maximum(jnp.where(lower, pltpu.roll(second, CZ, 1), second), fill_mass)
    mean_xy = first / heavy
    mean_z = second / heavy
    mean_yx = pltpu.roll(mean_xy, CZ, 1)
    mean_z_up = pltpu.roll(mean_z, CZ, 1)
    turn = 1.0 - cos_angle
    t0, t1, t2 = turn * n0, turn * n1, turn * n2
    s0, s1, s2 = sin_angle * n0, sin_angle * n1, sin_angle * n2
    field_out[0] = jnp.where(lower, cos_angle + t0 * n0, t0 * n1 - s2)
    field_out[1] = jnp.where(lower, t0 * n2 + s1, t0 * n1 + s2)
    field_out[2] = jnp.where(lower, cos_angle + t1 * n1, t1 * n2 - s0)
    field_out[3] = jnp.where(lower, t0 * n2 - s1, t1 * n2 + s0)
    field_out[4] = jnp.where(lower, cos_angle + t2 * n2, mean_yx)
    field_out[5] = jnp.where(lower, mean_yx, mean_z_up)

    place = state[8:9].astype(jnp.int32)
    lz = state[9:10].astype(jnp.int32)
    to_place = (lax.broadcasted_iota(jnp.int32, (CZ, FZ), 0) == lz).astype(jnp.float32)
    none = jnp.zeros_like(to_place)
    right = jnp.concatenate(
        [jnp.concatenate([to_place, none], axis=1), jnp.concatenate([none, to_place], axis=1)],
        axis=0,
    )
    hit = lax.broadcasted_iota(jnp.int32, (ROWS, FZ), 0) == place
    picked = []
    for pair in (mean_xy, jnp.where(lower, mean_z, n0), jnp.where(lower, n1, n2)):
        at_z = exact_dot(pair, right, NN)
        for half in (at_z[:, :FZ], at_z[:, FZ:]):
            picked.append(jnp.sum(jnp.where(hit, half, 0.0), axis=0, keepdims=True))
    u, n = picked[:3], picked[3:]
    alive = state[7:8] > 0.0
    old = [state[3 + c : 4 + c] for c in range(3)]
    rel = [old[c] - u[c] for c in range(3)]
    cross = [n[1] * rel[2] - n[2] * rel[1], n[2] * rel[0] - n[0] * rel[2], n[0] * rel[1] - n[1] * rel[0]]
    along = n[0] * rel[0] + n[1] * rel[1] + n[2] * rel[2]
    velocity = [
        jnp.where(
            alive,
            u[c] + cos_angle * rel[c] + sin_angle * cross[c] + turn * along * n[c],
            old[c],
        )
        for c in range(3)
    ]

    own = [state[c : c + 1] for c in range(3)]
    alive_row = state[7:8]

    def rows(b, a):
        if b == 1 and a == 1:
            return own + [alive_row]
        if b == 1:
            source, base = (odd1, 18) if a == 0 else (even1, 18)
        else:
            source, base = (odd2 if b == 0 else even2), 18 + 4 * a
        return [source[base + c : base + c + 1] for c in range(4)]

    live_out[9:16] = state[0:7]
    for b in range(3):
        for a in range(3):
            live_out[3 * b + a : 3 * b + a + 1] = rows(b, a)[3]
    others = around(lambda b, a: rows(b, a)[:3], lambda b, a: rows(b, a)[3])
    moved, velocity = advance(
        count[0, 0], own, velocity, state[6:7], others, pair_rows, pair_terms
    )
    for c in range(3):
        vel_out[c : c + 1] = velocity[c]
        pos_out[c : c + 1] = moved[c]
    vel_out[3:4] = jnp.zeros((1, FZ), jnp.float32)
    pos_out[3:4] = jnp.zeros((1, FZ), jnp.float32)


def cell_fields(count, part, odd1, even1, odd2, even2, state, numbers):
    return pl.pallas_call(
        fields_kernel,
        out_shape=(struct(6, ROWS, FZ), struct(16, FZ), struct(4, FZ), struct(4, FZ)),
        in_specs=[IN_SMEM] + [IN_VMEM] * 7,
        out_specs=(IN_VMEM,) * 4,
        scratch_shapes=[
            VMEM((2 * ROWS, FZ), jnp.float32),
            VMEM((ROWS, FZ), jnp.float32),
            *PAIR_SCRATCH,
        ],
        compiler_params=pltpu.CompilerParams(vmem_limit_bytes=SMALL_LIMIT),
        cost_estimate=pl.CostEstimate(flops=4_000_000, bytes_accessed=1_000_000, transcendentals=0),
        name="cell_fields",
    )(count, part, odd1, even1, odd2, even2, state, numbers)


def substep_moves(count, rest, own, column, odd, even, vel, rows, terms):
    mine = [own[c : c + 1] for c in range(3)]
    old = [vel[c : c + 1] for c in range(3)]
    source = (odd, column, even)
    others = around(
        lambda b, a: [source[b][4 * a + c : 4 * a + c + 1] for c in range(3)],
        lambda b, a: rest[3 * b + a : 3 * b + a + 1],
    )
    return advance(count[0, 0], mine, old, rest[15:16], others, rows, terms)


def substep_kernel(count, rest, own, column, odd, even, vel, vel_out, pos_out, rows, terms):
    moved, velocity = substep_moves(count, rest, own, column, odd, even, vel, rows, terms)
    for c in range(3):
        vel_out[c : c + 1] = velocity[c]
        pos_out[c : c + 1] = moved[c]
    vel_out[3:4] = jnp.zeros((1, FZ), jnp.float32)
    pos_out[3:4] = jnp.zeros((1, FZ), jnp.float32)


def last_kernel(count, rest, own, column, odd, even, vel, vel_out, pos_out, rows, terms):
    moved, velocity = substep_moves(count, rest, own, column, odd, even, vel, rows, terms)
    keep = rest[4:5] > 0.0
    for c in range(3):
        pos_out[c] = jnp.where(keep, moved[c], rest[9 + c : 10 + c])
        vel_out[c] = jnp.where(keep, velocity[c], rest[12 + c : 13 + c])


def substep(kernel, shape, count, rest, own, column, odd, even, vel):
    return pl.pallas_call(
        kernel,
        out_shape=(struct(*shape), struct(*shape)),
        in_specs=[IN_SMEM] + [IN_VMEM] * 6,
        out_specs=(IN_VMEM,) * 2,
        scratch_shapes=PAIR_SCRATCH,
        compiler_params=pltpu.CompilerParams(vmem_limit_bytes=SMALL_LIMIT),
        cost_estimate=pl.CostEstimate(flops=4_000_000, bytes_accessed=30_000, transcendentals=0),
        name="substep",
    )(count, rest, own, column, odd, even, vel)


def turn_kernel(ks, shift, v, occ, field, *refs):
    out_at, out, twice, wide, wsem = refs[-5:]
    sx, sy, sz = shift[0], shift[1], shift[2]
    places = []
    stores = []
    for i, k in enumerate(ks):
        if k < CX:
            places += [k * SUB - sx + j for j in range(SUB)]
            here, there = pl.ds(SUB * i, SUB), pl.ds(SUB * k - sx, SUB)
            stores.append(
                [pltpu.make_async_copy(out.at[:, here], out_at.at[:, there], wsem.at[SUB * i])]
            )
        else:
            around_end = [(FX - sx + j) & (FX - 1) for j in range(SUB)]
            places += around_end
            stores.append(
                [
                    pltpu.make_async_copy(
                        out.at[:, pl.ds(SUB * i + j, 1)],
                        out_at.at[:, pl.ds(x, 1)],
                        wsem.at[SUB * i + j],
                    )
                    for j, x in enumerate(around_end)
                ]
            )
    source = lax.broadcasted_iota(jnp.int32, (CZ, FZ), 0)
    layer = lax.broadcasted_iota(jnp.int32, (CZ, FZ), 1)
    spread = (((layer + sz) & (FZ - 1)) >> 1 == source).astype(jnp.float32)
    none = jnp.zeros_like(spread)
    right = jnp.concatenate(
        [jnp.concatenate([spread, none], axis=1), jnp.concatenate([none, spread], axis=1)],
        axis=0,
    )
    layers = list(ks) + ([0] if CX in ks else [])
    for f in range(6):
        left = jnp.concatenate([field[f, JP * k : JP * k + JP] for k in layers])
        both = exact_dot(left, right, NN)
        wide[2 * f] = both[:, :FZ]
        wide[2 * f + 1] = both[:, FZ:]
    row = lax.broadcasted_iota(jnp.int32, (8, FZ), 0)
    slot = (row & 1).astype(jnp.float32)
    low = row < 8 - 2 * sy

    def turn_layer(at, planes, t):
        f = [
            jnp.where(low, wide[i, pl.ds(JP * at + t, 1), :], wide[i, pl.ds(JP * at + t + 1, 1), :])
            for i in range(12)
        ]
        rows = pl.ds(pl.multiple_of(8 * t, 8), 8)

        def plane(n, x):
            live = twice[pl.ds(pl.multiple_of(n * 2 * FY + 8 * t, 8), 8), :] > slot
            old = [v[c, x, rows, :] for c in range(3)]
            rel = [old[c] - f[9 + c] for c in range(3)]
            for c in range(3):
                new = f[9 + c] + (
                    f[3 * c] * rel[0] + f[3 * c + 1] * rel[1] + f[3 * c + 2] * rel[2]
                )
                out[c, n, rows, :] = jnp.where(live, new, old[c])

        planes(plane)

    for n, x in enumerate(places):
        slots = occ[x].astype(jnp.float32)
        twice[pl.ds(2 * FY * n, FY, 2), :] = slots
        twice[pl.ds(2 * FY * n + 1, FY, 2), :] = slots

    for i, k in enumerate(ks):

        def column(t, carry, i=i, k=k):
            def some(first, last):
                def run(plane):
                    def step(j, carry):
                        plane(SUB * i + j, (FX - sx + j) & (FX - 1))
                        return carry

                    lax.fori_loop(first, last, step, 0)

                return run

            if k < CX:
                turn_layer(
                    i, lambda plane: [plane(SUB * i + j, places[SUB * i + j]) for j in range(SUB)], t
                )
            else:
                turn_layer(i, some(0, sx), t)
                turn_layer(i + 1, some(sx, SUB), t)
            return carry

        lax.fori_loop(0, CY, column, 0)
        for copy in stores[i]:
            copy.start()
    for group in stores:
        for copy in group:
            copy.wait()


def turn_solvent(ks, grid_shift, v, occ, field, done=None):
    planes = SUB * len(ks)
    layers = len(ks) + (CX in ks)
    return pl.pallas_call(
        functools.partial(turn_kernel, ks),
        out_shape=struct(*v.shape),
        in_specs=[IN_SMEM, IN_VMEM, IN_VMEM, IN_VMEM] + [HBM] * (done is not None),
        out_specs=HBM,
        input_output_aliases={} if done is None else {4: 0},
        scratch_shapes=[
            VMEM((3, planes, 2 * FY, FZ), jnp.float32),
            VMEM((2 * planes * FY, FZ), jnp.float32),
            VMEM((12, JP * layers, FZ), jnp.float32),
            DMA((planes,)),
        ],
        compiler_params=pltpu.CompilerParams(vmem_limit_bytes=TURN_LIMIT),
        cost_estimate=pl.CostEstimate(flops=3_000_000, bytes_accessed=1_300_000, transcendentals=0),
        name="turn_solvent",
    )(grid_shift, v, occ, field, *([] if done is None else [done]))


def per_device(
    solvent_vel,
    occupancy,
    grid_shift,
    axis_index,
    colloid_pos,
    colloid_vel,
    colloid_mass,
    colloid_count,
):
    v = solvent_vel.reshape(3, FX, 2 * FY, FZ)
    pos = colloid_pos.reshape(3, 1, FZ)
    vel = colloid_vel.reshape(3, 1, FZ)
    mass = colloid_mass
    count = colloid_count

    base, odd, even = cell_sums(grid_shift, count, v, occupancy, axis_index, pos, vel, mass)
    odd1, even1 = swap_both(odd, even, "gx")
    part, state, numbers = prepare(base)
    odd, even = columns(part, odd1, even1, state, numbers)
    odd2, even2 = swap_both(odd, even, "yz")
    field, rest, velocity, position = cell_fields(
        count, part, odd1, even1, odd2, even2, state, numbers
    )
    solvent_out = None
    for step in range(1, SUBSTEPS):
        ks = TURNED[step - 1]
        if step > 1:
            position, solvent_out = lax.optimization_barrier((position, solvent_out))
        solvent_out = turn_solvent(ks, grid_shift, v, occupancy, field, solvent_out)
        odd, even = swap_both(position, position, "gx")
        odd, solvent_out = lax.optimization_barrier((odd, solvent_out))
        column = jnp.concatenate([odd, position, even])
        odd, even = swap_both(column, column, "yz")
        odd, velocity = lax.optimization_barrier((odd, velocity))
        kernel, shape = (
            (substep_kernel, (4, FZ)) if step < SUBSTEPS - 1 else (last_kernel, (3, 1, FZ))
        )
        velocity, position = substep(
            kernel, shape, count, rest, position, column, odd, even, velocity
        )
    return (
        solvent_out.reshape(solvent_vel.shape),
        position[:, None],
        velocity[:, None],
    )


def solution(mesh):
    return jax.shard_map(
        per_device,
        mesh=mesh,
        in_specs=(
            P(None, "gx", "yz", None, None),
            P("gx", "yz", None),
            P(),
            P("gx", "yz", None),
            P(None, "gx", "yz", None),
            P(None, "gx", "yz", None),
            P("gx", "yz", None),
            P("gx", "yz"),
        ),
        out_specs=(
            P(None, "gx", "yz", None, None),
            P(None, "gx", "yz", None),
            P(None, "gx", "yz", None),
        ),
        check_vma=False,
    )
```

```python
import functools
import math

import jax
import jax.numpy as jnp
from jax import lax
from jax.experimental import pallas as pl
from jax.experimental.pallas import tpu as pltpu
from jax.sharding import PartitionSpec as P

CX = 8
CY = 8
CZ = 64
SUB = 4
SUBSTEPS = 4
DIRECTIONS = 64
FX = 32
FY = 32
FZ = 128
KX = CX + 1
JY = CY + 1
JP = 16
ROWS = KX * JP

turn_angle = 130.0 * math.pi / 180.0
cos_angle = math.cos(turn_angle)
sin_angle = math.sin(turn_angle)
golden = math.pi * (3.0 - math.sqrt(5.0))
cutoff = 1.5
stiffness = 20.0
timestep = 0.05
fill_mass = 16.0

SMEM = pltpu.SMEM
VMEM = pltpu.VMEM
HBM = pl.BlockSpec(memory_space=pltpu.HBM)
IN_VMEM = pl.BlockSpec(memory_space=VMEM)
IN_SMEM = pl.BlockSpec(memory_space=SMEM)
DMA = pltpu.SemaphoreType.DMA
NT = (((1,), (1,)), ((), ()))
NN = (((1,), (0,)), ((), ()))
STATE = 2 * ROWS
NUMBERS = STATE + 16
BASE = NUMBERS + ROWS
TURNED = ((1, 2, 3), (4, 5, 6), (7, CX))
TILE = 32
SMALL_LIMIT = 8 * 1024 * 1024
TURN_LIMIT = 16 * 1024 * 1024


def swapped(value, axis, first):
    count = lax.axis_size(axis)
    pairs = []
    for low in range(first, count + first, 2):
        a, b = low % count, (low + 1) % count
        pairs += [(a, b), (b, a)]
    return lax.ppermute(value, axis, pairs)


def swap_both(odd, even, axis):
    return swapped(odd, axis, 1), swapped(even, axis, 0)


def struct(*shape):
    return jax.ShapeDtypeStruct(shape, jnp.float32)


def exact_dot(left, right, dims):
    right = right.astype(jnp.bfloat16)
    total = None
    for part in range(3):
        piece = left.astype(jnp.bfloat16)
        term = lax.dot_general(piece, right, dims, preferred_element_type=jnp.float32)
        total = term if total is None else total + term
        if part < 2:
            left = left - piece.astype(jnp.float32)
    return total


def colloid_cells(pos, sx, sy, sz):
    cell_x = jnp.clip(jnp.floor(pos[0] * SUB).astype(jnp.int32), 0, FX - 1)
    cell_y = jnp.clip(jnp.floor(pos[1] * SUB).astype(jnp.int32), 0, FY - 1)
    cell_z = jnp.clip(jnp.floor(pos[2] * 2.0).astype(jnp.int32), 0, FZ - 1)
    return ((cell_x + sx) >> 2, (cell_y + sy) >> 2, ((cell_z + sz) & (FZ - 1)) >> 1)


def live_row(count):
    return lax.broadcasted_iota(jnp.int32, (1, FZ), 1) < count


def store_twice(occ, twice, q):
    slots = occ[SUB * q : SUB * q + SUB].reshape(SUB * FY, FZ).astype(jnp.float32)
    base = 2 * SUB * FY * q
    twice[pl.ds(base, SUB * FY, 2), :] = slots
    twice[pl.ds(base + 1, SUB * FY, 2), :] = slots


def parity(axis):
    return lax.axis_index(axis) & 1


def sums_kernel(
    shift_at, count_at, v_at, occ_at, axis_at, pos_at, vel_at, mass_at,
    base, odd, even,
    shift, count, v, occ, axis, pos, vel, mass, twice, partial, sem, vsem, osem,
):
    small = [
        pltpu.make_async_copy(a, b, sem.at[i])
        for i, (a, b) in enumerate(
            [
                (shift_at, shift),
                (count_at, count),
                (axis_at, axis),
                (pos_at, pos),
                (vel_at, vel),
                (mass_at, mass),
            ]
        )
    ]
    large = []
    for q in range(CX):
        part = pl.ds(SUB * q, SUB)
        large.append(pltpu.make_async_copy(occ_at.at[part], occ.at[part], osem.at[q]))
        large.append(pltpu.make_async_copy(v_at.at[:, part], v.at[:, part], vsem.at[q]))
    for copy in small[:2] + large[:2] + small[2:] + large[2:]:
        copy.start()
    for copy in small[:2]:
        copy.wait()
    sx, sy, sz = shift[0], shift[1], shift[2]
    row = lax.broadcasted_iota(jnp.int32, (2 * FY, FZ), 0)
    slot = (row & 1).astype(jnp.float32)
    low = (row[:8] < 8 - 2 * sy)[None]

    def plane(x, acc):
        live = twice[pl.ds(pl.multiple_of(x * 2 * FY, 2 * FY), 2 * FY), :] > slot
        masked = [jnp.where(live, v[c, x], 0.0) for c in range(3)] + [jnp.where(live, 1.0, 0.0)]
        return tuple(a + m for a, m in zip(acc, masked))

    zero = jnp.zeros((2 * FY, FZ), jnp.float32)
    blank = jnp.zeros((1, 8, FZ), jnp.float32)
    partial[:, :, 8:JP, :] = jnp.zeros((4, KX, JP - 8, FZ), jnp.float32)

    for k in range(KX):
        if k < CX:
            large[2 * k].wait()
            store_twice(occ, twice, k)
            large[2 * k + 1].wait()
        acc = (zero,) * 4
        if k == 0:
            acc = lax.fori_loop(0, SUB - sx, plane, acc)
        elif k == CX:
            acc = lax.fori_loop(FX - sx, FX, plane, acc)
        else:
            for j in range(SUB):
                acc = plane(k * SUB - sx + j, acc)
        for c in range(4):
            parts = acc[c].reshape(CY, 8, FZ)
            picked = jnp.where(
                low, jnp.concatenate([parts, blank]), jnp.concatenate([blank, parts])
            )
            partial[c, k, 0:JY, :] = jnp.sum(picked, axis=1)

    for copy in small[2:]:
        copy.wait()
    kx, jy, lz = colloid_cells(pos, sx, sy, sz)
    alive = live_row(count[0, 0]).astype(jnp.float32)
    weight = mass[0] * alive
    hit = lax.broadcasted_iota(jnp.int32, (ROWS, FZ), 0) == kx * JP + jy
    carried = [jnp.where(hit, vel[c] * weight, 0.0) for c in range(3)]
    carried.append(jnp.where(hit, weight, 0.0))
    target = lax.broadcasted_iota(jnp.int32, (CZ, FZ), 0)
    layer = lax.broadcasted_iota(jnp.int32, (CZ, FZ), 1)
    to_cell = (((layer + sz) & (FZ - 1)) >> 1 == target).astype(jnp.float32)
    to_place = (target == lz).astype(jnp.float32)
    one = jnp.concatenate([to_cell, to_place], axis=1)
    none = jnp.zeros_like(one)
    right = jnp.concatenate(
        [jnp.concatenate([one, none], axis=1), jnp.concatenate([none, one], axis=1)], axis=0
    )
    for p in range(2):
        left = jnp.concatenate(
            [
                partial[2 * p].reshape(ROWS, FZ),
                carried[2 * p],
                partial[2 * p + 1].reshape(ROWS, FZ),
                carried[2 * p + 1],
            ],
            axis=1,
        )
        total = exact_dot(left, right, NT)
        base[p * ROWS : p * ROWS + ROWS] = total
    turned = parity("gx") * (CX * JP)
    for p in range(2):
        for packet, place in ((odd, turned), (even, CX * JP - turned)):
            start = pl.multiple_of(p * ROWS + place, JP)
            packet[8 * p : 8 * p + 8] = base[pl.ds(start, 8), :]
            packet[16 + p : 17 + p] = base[pl.ds(start + 8, 1), :]
    for packet in (odd, even):
        for c in range(3):
            packet[18 + c : 19 + c] = pos[c]
        packet[21:22] = alive
        packet[22:24] = jnp.zeros((2, FZ), jnp.float32)
    for c in range(3):
        base[STATE + c : STATE + c + 1] = pos[c]
        base[STATE + 3 + c : STATE + 4 + c] = vel[c]
    base[STATE + 6 : STATE + 7] = mass[0]
    base[STATE + 7 : STATE + 8] = alive
    base[STATE + 8 : STATE + 9] = (kx * JP + jy).astype(jnp.float32)
    base[STATE + 9 : STATE + 10] = lz.astype(jnp.float32)
    base[STATE + 10 : STATE + 16] = jnp.zeros((6, FZ), jnp.float32)
    base[NUMBERS : NUMBERS + ROWS] = jnp.zeros((ROWS, FZ), jnp.float32)
    for k in range(CX):
        number = axis[k].astype(jnp.float32)
        number = jnp.concatenate([number, number], axis=1)
        base[NUMBERS + JP * k : NUMBERS + JP * k + CY] = number
        if k == 0:
            odd[24:32] = number
            even[24:32] = number


def cell_sums(grid_shift, count, v, occ, axis_index, pos, vel, mass):
    return pl.pallas_call(
        sums_kernel,
        out_shape=(
            struct(BASE, FZ),
            struct(32, FZ),
            struct(32, FZ),
        ),
        in_specs=[HBM] * 8,
        out_specs=(IN_VMEM,) * 3,
        scratch_shapes=[
            SMEM((3,), jnp.int32),
            SMEM((1, 1), jnp.int32),
            VMEM((3, FX, 2 * FY, FZ), jnp.float32),
            VMEM((FX, FY, FZ), jnp.int32),
            VMEM((CX, CY, CZ), jnp.int32),
            VMEM((3, 1, FZ), jnp.float32),
            VMEM((3, 1, FZ), jnp.float32),
            VMEM((1, 1, FZ), jnp.float32),
            VMEM((2 * FX * FY, FZ), jnp.float32),
            VMEM((4, KX, JP, FZ), jnp.float32),
            DMA((6,)),
            DMA((CX,)),
            DMA((CX,)),
        ],
        cost_estimate=pl.CostEstimate(flops=4_000_000, bytes_accessed=3_700_000, transcendentals=0),
        name="cell_sums",
    )(grid_shift, count, v, occ, axis_index, pos, vel, mass)


def prepare_kernel(base, part, state, numbers):
    part[...] = base[0:STATE]
    state[...] = base[STATE:NUMBERS]
    numbers[...] = base[NUMBERS:BASE]


def prepare(base):
    return pl.pallas_call(
        prepare_kernel,
        out_shape=(struct(STATE, FZ), struct(16, FZ), struct(ROWS, FZ)),
        in_specs=[IN_VMEM],
        out_specs=(IN_VMEM,) * 3,
        compiler_params=pltpu.CompilerParams(vmem_limit_bytes=SMALL_LIMIT),
        cost_estimate=pl.CostEstimate(flops=10_000, bytes_accessed=460_000, transcendentals=0),
        name="prepare",
    )(base)


def add_x(part, odd, even, full):
    full[...] = part[...]
    turned = parity("gx") * (CX * JP)
    for p in range(2):
        for packet, place in ((odd, turned), (even, CX * JP - turned)):
            start = pl.multiple_of(p * ROWS + place, JP)
            full[pl.ds(start, 8), :] += packet[8 * p : 8 * p + 8]
            full[pl.ds(start + 8, 1), :] += packet[16 + p : 17 + p]


def later_x(odd, even, rows):
    return jnp.where(parity("gx") == 1, odd[rows], even[rows])


def columns_kernel(part, odd1, even1, state, numbers, odd, even, full, ends):
    add_x(part, odd1, even1, full)
    for p in range(2):
        ends[0, 9 * p : 9 * p + 9] = full[pl.ds(p * ROWS, KX, JP), :]
        ends[1, 9 * p : 9 * p + 9] = full[pl.ds(p * ROWS + 8, KX, JP), :]
    side = parity("yz")
    for packet, end in ((odd, side), (even, 1 - side)):
        packet[0:18] = ends[end, 0:18]
        packet[18:22] = odd1[18:22]
        packet[22:25] = state[0:3]
        packet[25:26] = state[7:8]
        packet[26:30] = even1[18:22]
        packet[30:38] = numbers[pl.ds(0, CX, JP), :]
        packet[38:39] = later_x(odd1, even1, slice(24, 25))
        packet[39:40] = jnp.zeros((1, FZ), jnp.float32)


def columns(part, odd1, even1, state, numbers):
    return pl.pallas_call(
        columns_kernel,
        out_shape=(struct(40, FZ), struct(40, FZ)),
        in_specs=[IN_VMEM] * 5,
        out_specs=(IN_VMEM,) * 2,
        scratch_shapes=[VMEM((2 * ROWS, FZ), jnp.float32), VMEM((2, 24, FZ), jnp.float32)],
        compiler_params=pltpu.CompilerParams(vmem_limit_bytes=SMALL_LIMIT),
        cost_estimate=pl.CostEstimate(flops=100_000, bytes_accessed=500_000, transcendentals=0),
        name="columns",
    )(part, odd1, even1, state, numbers)


def pair_force(devices, rows, terms):
    ones = jnp.ones((8, FZ), jnp.bfloat16)
    slot = lax.broadcasted_iota(jnp.int32, (FZ, FZ), 0)
    sub = TILE // 8

    for n, (own, live, others) in enumerate(devices):
        column = jnp.concatenate(list(own) + [jnp.zeros((5, FZ), jnp.float32)], axis=0).T

        def tile(t, n=n, column=column, others=others):
            part = column[TILE * t : TILE * t + TILE]
            mine = [
                jnp.broadcast_to(part[:, c : c + 1], (TILE, FZ)).reshape(sub, 8, FZ)
                for c in range(3)
            ]
            moved = {step: mine[0] - step * float(CX) for step in (-1, 0, 1)}
            total = None
            for place, step in others:
                dx = moved[step] - rows[4 * place][None]
                dy = mine[1] - rows[4 * place + 1][None]
                dz = mine[2] - rows[4 * place + 2][None]
                dz = jnp.where(
                    dz > 0.5 * CZ, dz - CZ, jnp.where(dz < -0.5 * CZ, dz + CZ, dz)
                )
                reach = jnp.maximum(
                    rows[4 * place + 3][None]
                    - (dx * dx + dy * dy + dz * dz) * (1.0 / (cutoff * cutoff)),
                    0.0,
                )
                weight = reach * reach
                new = (weight * dx, weight * dy, weight * dz)
                total = new if total is None else tuple(a + b for a, b in zip(total, new))
            for c in range(3):
                start = FZ * (3 * n + c) + TILE * t
                terms[start : start + TILE] = total[c].reshape(TILE, FZ)

        for t in range(FZ // TILE):
            pl.when(TILE * t < live)(functools.partial(tile, t))

    forces = []
    for n, (own, live, others) in enumerate(devices):
        left = jnp.where(
            jnp.concatenate([slot < live] * 3), terms[3 * FZ * n : 3 * FZ * (n + 1)], 0.0
        )
        back = None
        for part in range(3):
            piece = left.astype(jnp.bfloat16)
            term = lax.dot_general(ones, piece, NT, preferred_element_type=jnp.float32)
            back = term if back is None else back + term
            if part < 2:
                left = left - piece.astype(jnp.float32)
        forces.append([stiffness * back[0:1, FZ * c : FZ * c + FZ] for c in range(3)])
    return forces


def pair_scratch(width):
    return [
        VMEM((12 * (width + 2), 8, FZ), jnp.float32),
        VMEM((3 * FZ * width, FZ), jnp.float32),
    ]


def store_rows(rows, place, packet, step_y):
    x, y, z, alive = packet
    values = (x, y + step_y, z, jnp.where(alive > 0.0, 1.0, -1.0))
    for c in range(4):
        rows[4 * place + c] = jnp.broadcast_to(values[c], (8, FZ))


def toward(axis, cells):
    return ((2 * parity(axis) - 1) * cells).astype(jnp.float32)


def live_count(alive):
    return jnp.sum(alive).astype(jnp.int32)


def advance(own, velocity, mass, alive, force):
    velocity = [
        velocity[c] + timestep * jnp.where(alive > 0.0, force[c], 0.0) / mass for c in range(3)
    ]
    return [own[c] + timestep * velocity[c] for c in range(3)], velocity


def fields_kernel(
    count, part, odd1, even1, odd2, even2, state, numbers_in,
    field_out, rest_out, packets,
    full, numbers, pair_rows, pair_terms,
):
    add_x(part, odd1, even1, full)
    forward = parity("yz") == 1
    for p in range(2):
        rows = slice(9 * p, 9 * p + 9)
        first = pl.ds(p * ROWS, KX, JP)
        full[first, :] = full[first, :] + jnp.where(forward, even2[rows], odd2[rows])
        last = pl.ds(p * ROWS + 8, KX, JP)
        full[last, :] = full[last, :] + jnp.where(forward, odd2[rows], even2[rows])
    numbers[...] = numbers_in[...]
    numbers[JP * CX : JP * CX + 8] = later_x(odd1, even1, slice(24, 32))
    numbers[pl.ds(8, KX, JP), :] = jnp.where(forward, odd2[30:39], even2[30:39])

    lane = lax.broadcasted_iota(jnp.int32, (8, FZ), 1)
    number = (lane & (DIRECTIONS - 1)).astype(jnp.float32)
    height = 1.0 - (2.0 * number + 1.0) / DIRECTIONS
    radius = jnp.sqrt(1.0 - height * height)
    phase = number * golden
    index = numbers[...].astype(jnp.int32)
    n0, n1, n2 = [
        jnp.take_along_axis(jnp.broadcast_to(table[0:1], (ROWS, FZ)), index, axis=1)
        for table in (radius * jnp.cos(phase), radius * jnp.sin(phase), height)
    ]

    lower = lax.broadcasted_iota(jnp.int32, (ROWS, FZ), 1) < CZ
    first, second = full[0:ROWS], full[ROWS : 2 * ROWS]
    heavy = jnp.maximum(jnp.where(lower, pltpu.roll(second, CZ, 1), second), fill_mass)
    mean_xy = first / heavy
    mean_z = second / heavy
    mean_yx = pltpu.roll(mean_xy, CZ, 1)
    mean_z_up = pltpu.roll(mean_z, CZ, 1)
    turn = 1.0 - cos_angle
    t0, t1, t2 = turn * n0, turn * n1, turn * n2
    s0, s1, s2 = sin_angle * n0, sin_angle * n1, sin_angle * n2
    field_out[0] = jnp.where(lower, cos_angle + t0 * n0, t0 * n1 - s2)
    field_out[1] = jnp.where(lower, t0 * n2 + s1, t0 * n1 + s2)
    field_out[2] = jnp.where(lower, cos_angle + t1 * n1, t1 * n2 - s0)
    field_out[3] = jnp.where(lower, t0 * n2 - s1, t1 * n2 + s0)
    field_out[4] = jnp.where(lower, cos_angle + t2 * n2, mean_yx)
    field_out[5] = jnp.where(lower, mean_yx, mean_z_up)

    place = state[8:9].astype(jnp.int32)
    lz = state[9:10].astype(jnp.int32)
    to_place = (lax.broadcasted_iota(jnp.int32, (CZ, FZ), 0) == lz).astype(jnp.float32)
    none = jnp.zeros_like(to_place)
    right = jnp.concatenate(
        [jnp.concatenate([to_place, none], axis=1), jnp.concatenate([none, to_place], axis=1)],
        axis=0,
    )
    hit = lax.broadcasted_iota(jnp.int32, (ROWS, FZ), 0) == place
    picked = []
    for pair in (mean_xy, jnp.where(lower, mean_z, n0), jnp.where(lower, n1, n2)):
        at_z = exact_dot(pair, right, NN)
        for half in (at_z[:, :FZ], at_z[:, FZ:]):
            picked.append(jnp.sum(jnp.where(hit, half, 0.0), axis=0, keepdims=True))
    u, n = picked[:3], picked[3:]
    alive = state[7:8] > 0.0
    old = [state[3 + c : 4 + c] for c in range(3)]
    rel = [old[c] - u[c] for c in range(3)]
    cross = [n[1] * rel[2] - n[2] * rel[1], n[2] * rel[0] - n[0] * rel[2], n[0] * rel[1] - n[1] * rel[0]]
    along = n[0] * rel[0] + n[1] * rel[1] + n[2] * rel[2]
    velocity = [
        jnp.where(
            alive,
            u[c] + cos_angle * rel[c] + sin_angle * cross[c] + turn * along * n[c],
            old[c],
        )
        for c in range(3)
    ]

    own = [state[c : c + 1] for c in range(3)]
    alive_row = state[7:8]

    def rows(b, a):
        if b == 1 and a == 1:
            return own + [alive_row]
        if b == 1:
            source, base = (odd1, 18) if a == 0 else (even1, 18)
        else:
            source, base = (odd2 if b == 0 else even2), 18 + 4 * a
        return [source[base + c : base + c + 1] for c in range(4)]

    rest_out[0:7] = state[0:7]
    rest_out[7:8] = alive_row
    after = parity("gx") == 1
    for b in range(3):
        step_y = (1 - b) * toward("yz", CY)
        slots = [rows(b, a) for a in range(3)]
        first = [jnp.where(after, e, o) for o, e in zip(slots[0], slots[2])]
        last = [jnp.where(after, o, e) for o, e in zip(slots[0], slots[2])]
        for a, packet in enumerate((first, slots[1], last)):
            store_rows(pair_rows, 3 * b + a, packet, step_y)
    others = [(3 * b + a, a - 1) for b in range(3) for a in range(3)]
    force = pair_force([(own, count[0, 0], others)], pair_rows, pair_terms)[0]
    moved, velocity = advance(own, velocity, state[6:7], alive_row, force)
    packet = jnp.concatenate(moved + [alive_row] + velocity + [state[6:7]], axis=0)
    for g in range(packets.shape[0]):
        packets[g] = packet


def cell_fields(count, part, odd1, even1, odd2, even2, state, numbers):
    return pl.pallas_call(
        fields_kernel,
        out_shape=(struct(6, ROWS, FZ), struct(8, FZ), struct(lax.axis_size("gx"), 8, FZ)),
        in_specs=[IN_SMEM] + [IN_VMEM] * 7,
        out_specs=(IN_VMEM,) * 3,
        scratch_shapes=[
            VMEM((2 * ROWS, FZ), jnp.float32),
            VMEM((ROWS, FZ), jnp.float32),
            *pair_scratch(1),
        ],
        compiler_params=pltpu.CompilerParams(vmem_limit_bytes=SMALL_LIMIT),
        cost_estimate=pl.CostEstimate(flops=4_000_000, bytes_accessed=1_000_000, transcendentals=0),
        name="cell_fields",
    )(count, part, odd1, even1, odd2, even2, state, numbers)


def padded(rows):
    return -(-rows // 8) * 8


def clear_tail(ref, used):
    if used < ref.shape[0]:
        ref[used:] = jnp.zeros((ref.shape[0] - used, FZ), jnp.float32)


def pick_kernel(width, packets, row_out, moving_out):
    count = packets.shape[0]
    me = lax.axis_index("gx")
    for a in range(width):
        source = lax.rem(me + a - width // 2 + 8 * count, count)
        row_out[4 * a : 4 * a + 4] = packets[source, 0:4]
        if 0 < a < width - 1:
            moving_out[4 * a - 4 : 4 * a] = packets[source, 4:8]
    clear_tail(row_out, 4 * width)
    clear_tail(moving_out, 4 * (width - 2))


def pick(width, packets):
    return pl.pallas_call(
        functools.partial(pick_kernel, width),
        out_shape=(struct(padded(4 * width), FZ), struct(padded(4 * (width - 2)), FZ)),
        in_specs=[IN_VMEM],
        out_specs=(IN_VMEM,) * 2,
        compiler_params=pltpu.CompilerParams(vmem_limit_bytes=SMALL_LIMIT),
        cost_estimate=pl.CostEstimate(flops=10_000, bytes_accessed=100_000, transcendentals=0),
        name="pick",
    )(packets)


def substep_moves(width, row, moving, odd, even, rows, terms):
    span = width + 2
    for b, source in enumerate((odd, row, even)):
        step_y = (1 - b) * toward("yz", CY)
        for a in range(span):
            packet = [source[4 * a + c : 4 * a + c + 1] for c in range(4)]
            store_rows(rows, span * b + a, packet, step_y)
    devices = []
    for n in range(width):
        at = 4 * (n + 1)
        own = [row[at + c : at + c + 1] for c in range(3)]
        others = [(span * b + n + 1 + step, step) for b in range(3) for step in (-1, 0, 1)]
        devices.append((own, live_count(row[at + 3 : at + 4]), others))
    forces = pair_force(devices, rows, terms)
    results = []
    for n in range(width):
        alive = row[4 * n + 7 : 4 * n + 8]
        velocity = [moving[4 * n + c : 4 * n + c + 1] for c in range(3)]
        mass = moving[4 * n + 3 : 4 * n + 4]
        results.append((*advance(devices[n][0], velocity, mass, alive, forces[n]), alive, mass))
    return results


def substep_kernel(width, row, moving, odd, even, row_out, moving_out, rows, terms):
    results = substep_moves(width, row, moving, odd, even, rows, terms)
    for n, (moved, velocity, alive, mass) in enumerate(results):
        row_out[4 * n : 4 * n + 4] = jnp.concatenate(moved + [alive], axis=0)
        if 0 < n < width - 1:
            moving_out[4 * n - 4 : 4 * n] = jnp.concatenate(velocity + [mass], axis=0)
    clear_tail(row_out, 4 * width)
    clear_tail(moving_out, 4 * (width - 2))


def last_kernel(row, moving, odd, even, rest, pos_out, vel_out, rows, terms):
    ((moved, velocity, alive, mass),) = substep_moves(1, row, moving, odd, even, rows, terms)
    keep = rest[7:8] > 0.0
    for c in range(3):
        pos_out[c] = jnp.where(keep, moved[c], rest[c : c + 1])
        vel_out[c] = jnp.where(keep, velocity[c], rest[3 + c : 4 + c])


def substep(width, row, moving, odd, even, rest):
    if width > 1:
        kernel = functools.partial(substep_kernel, width)
        shapes = (struct(padded(4 * width), FZ), struct(padded(4 * (width - 2)), FZ))
        operands = (row, moving, odd, even)
    else:
        kernel = last_kernel
        shapes = (struct(3, 1, FZ), struct(3, 1, FZ))
        operands = (row, moving, odd, even, rest)
    return pl.pallas_call(
        kernel,
        out_shape=shapes,
        in_specs=[IN_VMEM] * len(operands),
        out_specs=(IN_VMEM,) * 2,
        scratch_shapes=pair_scratch(width),
        compiler_params=pltpu.CompilerParams(vmem_limit_bytes=SMALL_LIMIT),
        cost_estimate=pl.CostEstimate(
            flops=4_000_000 * width, bytes_accessed=100_000, transcendentals=0
        ),
        name="substep",
    )(*operands)


def turn_kernel(ks, shift, v, occ, field, *refs):
    out_at, out, twice, wide, wsem = refs[-5:]
    sx, sy, sz = shift[0], shift[1], shift[2]
    places = []
    stores = []
    for i, k in enumerate(ks):
        if k < CX:
            places += [k * SUB - sx + j for j in range(SUB)]
            here, there = pl.ds(SUB * i, SUB), pl.ds(SUB * k - sx, SUB)
            stores.append(
                [pltpu.make_async_copy(out.at[:, here], out_at.at[:, there], wsem.at[SUB * i])]
            )
        else:
            around_end = [(FX - sx + j) & (FX - 1) for j in range(SUB)]
            places += around_end
            stores.append(
                [
                    pltpu.make_async_copy(
                        out.at[:, pl.ds(SUB * i + j, 1)],
                        out_at.at[:, pl.ds(x, 1)],
                        wsem.at[SUB * i + j],
                    )
                    for j, x in enumerate(around_end)
                ]
            )
    source = lax.broadcasted_iota(jnp.int32, (CZ, FZ), 0)
    layer = lax.broadcasted_iota(jnp.int32, (CZ, FZ), 1)
    spread = (((layer + sz) & (FZ - 1)) >> 1 == source).astype(jnp.float32)
    none = jnp.zeros_like(spread)
    right = jnp.concatenate(
        [jnp.concatenate([spread, none], axis=1), jnp.concatenate([none, spread], axis=1)],
        axis=0,
    )
    layers = list(ks) + ([0] if CX in ks else [])
    for f in range(6):
        left = jnp.concatenate([field[f, JP * k : JP * k + JP] for k in layers])
        both = exact_dot(left, right, NN)
        wide[2 * f] = both[:, :FZ]
        wide[2 * f + 1] = both[:, FZ:]
    row = lax.broadcasted_iota(jnp.int32, (8, FZ), 0)
    slot = (row & 1).astype(jnp.float32)
    low = row < 8 - 2 * sy

    def turn_layer(at, planes, t):
        f = [
            jnp.where(low, wide[i, pl.ds(JP * at + t, 1), :], wide[i, pl.ds(JP * at + t + 1, 1), :])
            for i in range(12)
        ]
        rows = pl.ds(pl.multiple_of(8 * t, 8), 8)

        def plane(n, x):
            live = twice[pl.ds(pl.multiple_of(n * 2 * FY + 8 * t, 8), 8), :] > slot
            old = [v[c, x, rows, :] for c in range(3)]
            rel = [old[c] - f[9 + c] for c in range(3)]
            for c in range(3):
                new = f[9 + c] + (
                    f[3 * c] * rel[0] + f[3 * c + 1] * rel[1] + f[3 * c + 2] * rel[2]
                )
                out[c, n, rows, :] = jnp.where(live, new, old[c])

        planes(plane)

    for n, x in enumerate(places):
        slots = occ[x].astype(jnp.float32)
        twice[pl.ds(2 * FY * n, FY, 2), :] = slots
        twice[pl.ds(2 * FY * n + 1, FY, 2), :] = slots

    for i, k in enumerate(ks):

        def column(t, carry, i=i, k=k):
            def some(first, last):
                def run(plane):
                    def step(j, carry):
                        plane(SUB * i + j, (FX - sx + j) & (FX - 1))
                        return carry

                    lax.fori_loop(first, last, step, 0)

                return run

            if k < CX:
                turn_layer(
                    i, lambda plane: [plane(SUB * i + j, places[SUB * i + j]) for j in range(SUB)], t
                )
            else:
                turn_layer(i, some(0, sx), t)
                turn_layer(i + 1, some(sx, SUB), t)
            return carry

        lax.fori_loop(0, CY, column, 0)
        for copy in stores[i]:
            copy.start()
    for group in stores:
        for copy in group:
            copy.wait()


def turn_solvent(ks, grid_shift, v, occ, field, done=None):
    planes = SUB * len(ks)
    layers = len(ks) + (CX in ks)
    return pl.pallas_call(
        functools.partial(turn_kernel, ks),
        out_shape=struct(*v.shape),
        in_specs=[IN_SMEM, IN_VMEM, IN_VMEM, IN_VMEM] + [HBM] * (done is not None),
        out_specs=HBM,
        input_output_aliases={} if done is None else {4: 0},
        scratch_shapes=[
            VMEM((3, planes, 2 * FY, FZ), jnp.float32),
            VMEM((2 * planes * FY, FZ), jnp.float32),
            VMEM((12, JP * layers, FZ), jnp.float32),
            DMA((planes,)),
        ],
        compiler_params=pltpu.CompilerParams(vmem_limit_bytes=TURN_LIMIT),
        cost_estimate=pl.CostEstimate(flops=3_000_000, bytes_accessed=1_300_000, transcendentals=0),
        name="turn_solvent",
    )(grid_shift, v, occ, field, *([] if done is None else [done]))


def per_device(
    solvent_vel,
    occupancy,
    grid_shift,
    axis_index,
    colloid_pos,
    colloid_vel,
    colloid_mass,
    colloid_count,
):
    v = solvent_vel.reshape(3, FX, 2 * FY, FZ)
    pos = colloid_pos.reshape(3, 1, FZ)
    vel = colloid_vel.reshape(3, 1, FZ)
    mass = colloid_mass
    count = colloid_count

    base, odd, even = cell_sums(grid_shift, count, v, occupancy, axis_index, pos, vel, mass)
    odd1, even1 = swap_both(odd, even, "gx")
    part, state, numbers = prepare(base)
    odd, even = columns(part, odd1, even1, state, numbers)
    odd2, even2 = swap_both(odd, even, "yz")
    field, rest, packets = cell_fields(count, part, odd1, even1, odd2, even2, state, numbers)
    packets = lax.all_to_all(packets, "gx", 0, 0)
    width = 2 * (SUBSTEPS - 1) + 1
    row, moving = pick(width, packets)
    solvent_out = None
    for ks in TURNED:
        width -= 2
        if solvent_out is None:
            row, field = lax.optimization_barrier((row, field))
        else:
            row, solvent_out = lax.optimization_barrier((row, solvent_out))
        solvent_out = turn_solvent(ks, grid_shift, v, occupancy, field, solvent_out)
        odd, even = swap_both(row, row, "yz")
        odd, solvent_out = lax.optimization_barrier((odd, solvent_out))
        row, moving = substep(width, row, moving, odd, even, rest)
    position, velocity = row, moving
    return (
        solvent_out.reshape(solvent_vel.shape),
        position[:, None],
        velocity[:, None],
    )


def solution(mesh):
    return jax.shard_map(
        per_device,
        mesh=mesh,
        in_specs=(
            P(None, "gx", "yz", None, None),
            P("gx", "yz", None),
            P(),
            P("gx", "yz", None),
            P(None, "gx", "yz", None),
            P(None, "gx", "yz", None),
            P("gx", "yz", None),
            P("gx", "yz"),
        ),
        out_specs=(
            P(None, "gx", "yz", None, None),
            P(None, "gx", "yz", None),
            P(None, "gx", "yz", None),
        ),
        check_vma=False,
    )
```

```python
import functools
import math

import jax
import jax.numpy as jnp
from jax import lax
from jax.experimental import pallas as pl
from jax.experimental.pallas import tpu as pltpu
from jax.sharding import PartitionSpec as P

CX = 8
CY = 8
CZ = 64
SUB = 4
SUBSTEPS = 4
DIRECTIONS = 64
FX = 32
FY = 32
FZ = 128
KX = CX + 1
JY = CY + 1
JP = 16
ROWS = KX * JP

turn_angle = 130.0 * math.pi / 180.0
cos_angle = math.cos(turn_angle)
sin_angle = math.sin(turn_angle)
golden = math.pi * (3.0 - math.sqrt(5.0))
cutoff = 1.5
stiffness = 20.0
timestep = 0.05
fill_mass = 16.0

SMEM = pltpu.SMEM
VMEM = pltpu.VMEM
HBM = pl.BlockSpec(memory_space=pltpu.HBM)
IN_VMEM = pl.BlockSpec(memory_space=VMEM)
IN_SMEM = pl.BlockSpec(memory_space=SMEM)
DMA = pltpu.SemaphoreType.DMA
NT = (((1,), (1,)), ((), ()))
NN = (((1,), (0,)), ((), ()))
STATE = 4 * JP
NUMBERS = STATE + 16
BASE = NUMBERS + ROWS
TURNED = ((1, 2, 3), (4, 5, 6), (7, CX))
TILE = 32
SMALL_LIMIT = 8 * 1024 * 1024
TURN_LIMIT = 16 * 1024 * 1024


def swapped(value, axis, first):
    count = lax.axis_size(axis)
    pairs = []
    for low in range(first, count + first, 2):
        a, b = low % count, (low + 1) % count
        pairs += [(a, b), (b, a)]
    return lax.ppermute(value, axis, pairs)


def swap_both(odd, even, axis):
    return swapped(odd, axis, 1), swapped(even, axis, 0)


def struct(*shape):
    return jax.ShapeDtypeStruct(shape, jnp.float32)


def exact_dot(left, right, dims):
    right = right.astype(jnp.bfloat16)
    total = None
    for part in range(3):
        piece = left.astype(jnp.bfloat16)
        term = lax.dot_general(piece, right, dims, preferred_element_type=jnp.float32)
        total = term if total is None else total + term
        if part < 2:
            left = left - piece.astype(jnp.float32)
    return total


def colloid_cells(pos, sx, sy, sz):
    cell_x = jnp.clip(jnp.floor(pos[0] * SUB).astype(jnp.int32), 0, FX - 1)
    cell_y = jnp.clip(jnp.floor(pos[1] * SUB).astype(jnp.int32), 0, FY - 1)
    cell_z = jnp.clip(jnp.floor(pos[2] * 2.0).astype(jnp.int32), 0, FZ - 1)
    return ((cell_x + sx) >> 2, (cell_y + sy) >> 2, ((cell_z + sz) & (FZ - 1)) >> 1)


def live_row(count):
    return lax.broadcasted_iota(jnp.int32, (1, FZ), 1) < count


def parity(axis):
    return lax.axis_index(axis) & 1


def live_planes(occ, places, twice):
    for n, x in enumerate(places):
        slots = occ[x].astype(jnp.float32)
        twice[pl.ds(2 * FY * n, FY, 2), :] = slots
        twice[pl.ds(2 * FY * n + 1, FY, 2), :] = slots


def add_plane(v, twice, slot, n, x, acc):
    live = twice[pl.ds(pl.multiple_of(n * 2 * FY, 2 * FY), 2 * FY), :] > slot
    masked = [jnp.where(live, v[c, x], 0.0) for c in range(3)] + [jnp.where(live, 1.0, 0.0)]
    return tuple(a + m for a, m in zip(acc, masked))


def store_cells(acc, sy, partial, at):
    row = lax.broadcasted_iota(jnp.int32, (8, FZ), 0)
    low = (row < 8 - 2 * sy)[None]
    blank = jnp.zeros((1, 8, FZ), jnp.float32)
    for c in range(4):
        parts = acc[c].reshape(CY, 8, FZ)
        picked = jnp.where(low, jnp.concatenate([parts, blank]), jnp.concatenate([blank, parts]))
        partial[c, at, 0:JY, :] = jnp.sum(picked, axis=1)


def slot_rows():
    return (lax.broadcasted_iota(jnp.int32, (2 * FY, FZ), 0) & 1).astype(jnp.float32)


def along_z(partial, carried, sz, lz, p):
    target = lax.broadcasted_iota(jnp.int32, (CZ, FZ), 0)
    layer = lax.broadcasted_iota(jnp.int32, (CZ, FZ), 1)
    to_cell = (((layer + sz) & (FZ - 1)) >> 1 == target).astype(jnp.float32)
    to_place = (target == lz).astype(jnp.float32)
    one = jnp.concatenate([to_cell, to_place], axis=1)
    none = jnp.zeros_like(one)
    right = jnp.concatenate(
        [jnp.concatenate([one, none], axis=1), jnp.concatenate([none, one], axis=1)], axis=0
    )
    size = carried[0].shape[0]
    left = jnp.concatenate(
        [
            partial[2 * p].reshape(size, FZ),
            carried[2 * p],
            partial[2 * p + 1].reshape(size, FZ),
            carried[2 * p + 1],
        ],
        axis=1,
    )
    return exact_dot(left, right, NT)


def border_kernel(
    shift_at, count_at, v_at, occ_at, axis_at, pos_at, vel_at, mass_at,
    base, odd, even,
    shift, count, v, occ, axis, pos, vel, mass, twice, partial, sem,
):
    ends = ((pl.ds(0, SUB - 1), pl.ds(0, SUB - 1)), (pl.ds(FX - SUB + 1, SUB - 1), pl.ds(SUB - 1, SUB - 1)))
    pairs = [(shift_at, shift)]
    pairs += [(occ_at.at[there], occ.at[here]) for there, here in ends]
    pairs += [(v_at.at[:, there], v.at[:, here]) for there, here in ends]
    pairs += [(count_at, count), (pos_at, pos), (vel_at, vel), (mass_at, mass), (axis_at, axis)]
    copies = [pltpu.make_async_copy(a, b, sem.at[i]) for i, (a, b) in enumerate(pairs)]
    for copy in copies:
        copy.start()
    partial[:, :, 8:JP, :] = jnp.zeros((4, 2, JP - 8, FZ), jnp.float32)
    slot = slot_rows()
    zero = jnp.zeros((2 * FY, FZ), jnp.float32)
    for copy in copies[:3]:
        copy.wait()
    sx, sy, sz = shift[0], shift[1], shift[2]
    planes = 2 * (SUB - 1)
    live_planes(occ, range(planes), twice)
    for copy in copies[3:]:
        copy.wait()

    def plane(x, acc):
        return add_plane(v, twice, slot, x, x, acc)

    store_cells(lax.fori_loop(0, SUB - sx, plane, (zero,) * 4), sy, partial, 0)
    store_cells(lax.fori_loop(planes - sx, planes, plane, (zero,) * 4), sy, partial, 1)

    kx, jy, lz = colloid_cells(pos, sx, sy, sz)
    alive = live_row(count[0, 0]).astype(jnp.float32)
    weight = mass[0] * alive
    place = jnp.where(kx == 0, jy, jnp.where(kx == CX, JP + jy, 2 * JP))
    hit = lax.broadcasted_iota(jnp.int32, (2 * JP, FZ), 0) == place
    carried = [jnp.where(hit, vel[c] * weight, 0.0) for c in range(3)]
    carried.append(jnp.where(hit, weight, 0.0))
    for p in range(2):
        base[2 * JP * p : 2 * JP * (p + 1)] = along_z(partial, carried, sz, lz, p)
    side = parity("gx")
    number = None
    base[NUMBERS : NUMBERS + ROWS] = jnp.zeros((ROWS, FZ), jnp.float32)
    for k in range(CX):
        row = axis[k].astype(jnp.float32)
        row = jnp.concatenate([row, row], axis=1)
        base[NUMBERS + JP * k : NUMBERS + JP * k + CY] = row
        number = row if k == 0 else number
    for packet, end in ((odd, side), (even, 1 - side)):
        for p in range(2):
            start = pl.multiple_of(2 * JP * p + JP * end, JP)
            packet[8 * p : 8 * p + 8] = base[pl.ds(start, 8), :]
            packet[16 + p : 17 + p] = base[pl.ds(start + 8, 1), :]
        for c in range(3):
            packet[18 + c : 19 + c] = pos[c]
        packet[21:22] = alive
        packet[22:24] = jnp.zeros((2, FZ), jnp.float32)
        packet[24:32] = number
    for c in range(3):
        base[STATE + c : STATE + c + 1] = pos[c]
        base[STATE + 3 + c : STATE + 4 + c] = vel[c]
    base[STATE + 6 : STATE + 7] = mass[0]
    base[STATE + 7 : STATE + 8] = alive
    base[STATE + 8 : STATE + 9] = (kx * JP + jy).astype(jnp.float32)
    base[STATE + 9 : STATE + 10] = lz.astype(jnp.float32)
    base[STATE + 10 : STATE + 16] = jnp.zeros((6, FZ), jnp.float32)


def border_sums(grid_shift, count, v, occ, axis_index, pos, vel, mass):
    planes = 2 * (SUB - 1)
    return pl.pallas_call(
        border_kernel,
        out_shape=(struct(BASE, FZ), struct(32, FZ), struct(32, FZ)),
        in_specs=[HBM] * 8,
        out_specs=(IN_VMEM,) * 3,
        scratch_shapes=[
            SMEM((3,), jnp.int32),
            SMEM((1, 1), jnp.int32),
            VMEM((3, planes, 2 * FY, FZ), jnp.float32),
            VMEM((planes, FY, FZ), jnp.int32),
            VMEM((CX, CY, CZ), jnp.int32),
            VMEM((3, 1, FZ), jnp.float32),
            VMEM((3, 1, FZ), jnp.float32),
            VMEM((1, 1, FZ), jnp.float32),
            VMEM((2 * planes * FY, FZ), jnp.float32),
            VMEM((4, 2, JP, FZ), jnp.float32),
            DMA((10,)),
        ],
        cost_estimate=pl.CostEstimate(flops=1_000_000, bytes_accessed=800_000, transcendentals=0),
        name="border_sums",
    )(grid_shift, count, v, occ, axis_index, pos, vel, mass)


def inner_kernel(shift, v, occ, base, part, state, numbers, twice, partial):
    sx, sy, sz = shift[0], shift[1], shift[2]
    state[...] = base[STATE:NUMBERS]
    numbers[...] = base[NUMBERS:BASE]
    partial[:, :, 8:JP, :] = jnp.zeros((4, CX - 1, JP - 8, FZ), jnp.float32)
    slot = slot_rows()
    zero = jnp.zeros((2 * FY, FZ), jnp.float32)
    live_planes(occ, [SUB - sx + n for n in range(SUB * (CX - 1))], twice)
    for k in range(1, CX):
        acc = (zero,) * 4
        for j in range(SUB):
            acc = add_plane(v, twice, slot, SUB * (k - 1) + j, k * SUB - sx + j, acc)
        store_cells(acc, sy, partial, k - 1)
    weight = base[STATE + 6 : STATE + 7] * base[STATE + 7 : STATE + 8]
    place = base[STATE + 8 : STATE + 9].astype(jnp.int32) - JP
    lz = base[STATE + 9 : STATE + 10].astype(jnp.int32)
    inner = JP * (CX - 1)
    hit = lax.broadcasted_iota(jnp.int32, (inner, FZ), 0) == place
    carried = [
        jnp.where(hit, base[STATE + 3 + c : STATE + 4 + c] * weight, 0.0) for c in range(3)
    ]
    carried.append(jnp.where(hit, weight, 0.0))
    for p in range(2):
        first = p * ROWS
        part[first : first + JP] = base[2 * JP * p : 2 * JP * p + JP]
        part[first + JP : first + JP + inner] = along_z(partial, carried, sz, lz, p)
        part[first + CX * JP : first + ROWS] = base[2 * JP * p + JP : 2 * JP * (p + 1)]


def inner_sums(grid_shift, v, occ, base):
    return pl.pallas_call(
        inner_kernel,
        out_shape=(struct(2 * ROWS, FZ), struct(16, FZ), struct(ROWS, FZ)),
        in_specs=[IN_SMEM] + [IN_VMEM] * 3,
        out_specs=(IN_VMEM,) * 3,
        scratch_shapes=[
            VMEM((2 * SUB * (CX - 1) * FY, FZ), jnp.float32),
            VMEM((4, CX - 1, JP, FZ), jnp.float32),
        ],
        compiler_params=pltpu.CompilerParams(vmem_limit_bytes=TURN_LIMIT),
        cost_estimate=pl.CostEstimate(flops=4_000_000, bytes_accessed=3_700_000, transcendentals=0),
        name="inner_sums",
    )(grid_shift, v, occ, base)


def add_x(part, odd, even, full):
    full[...] = part[...]
    turned = parity("gx") * (CX * JP)
    for p in range(2):
        for packet, place in ((odd, turned), (even, CX * JP - turned)):
            start = pl.multiple_of(p * ROWS + place, JP)
            full[pl.ds(start, 8), :] += packet[8 * p : 8 * p + 8]
            full[pl.ds(start + 8, 1), :] += packet[16 + p : 17 + p]


def later_x(odd, even, rows):
    return jnp.where(parity("gx") == 1, odd[rows], even[rows])


def columns_kernel(part, odd1, even1, state, numbers, odd, even, full, ends):
    add_x(part, odd1, even1, full)
    for p in range(2):
        ends[0, 9 * p : 9 * p + 9] = full[pl.ds(p * ROWS, KX, JP), :]
        ends[1, 9 * p : 9 * p + 9] = full[pl.ds(p * ROWS + 8, KX, JP), :]
    side = parity("yz")
    for packet, end in ((odd, side), (even, 1 - side)):
        packet[0:18] = ends[end, 0:18]
        packet[18:22] = odd1[18:22]
        packet[22:25] = state[0:3]
        packet[25:26] = state[7:8]
        packet[26:30] = even1[18:22]
        packet[30:38] = numbers[pl.ds(0, CX, JP), :]
        packet[38:39] = later_x(odd1, even1, slice(24, 25))
        packet[39:40] = jnp.zeros((1, FZ), jnp.float32)


def columns(part, odd1, even1, state, numbers):
    return pl.pallas_call(
        columns_kernel,
        out_shape=(struct(40, FZ), struct(40, FZ)),
        in_specs=[IN_VMEM] * 5,
        out_specs=(IN_VMEM,) * 2,
        scratch_shapes=[VMEM((2 * ROWS, FZ), jnp.float32), VMEM((2, 24, FZ), jnp.float32)],
        compiler_params=pltpu.CompilerParams(vmem_limit_bytes=SMALL_LIMIT),
        cost_estimate=pl.CostEstimate(flops=100_000, bytes_accessed=500_000, transcendentals=0),
        name="columns",
    )(part, odd1, even1, state, numbers)


def pair_force(devices, rows, terms):
    ones = jnp.ones((8, FZ), jnp.bfloat16)
    slot = lax.broadcasted_iota(jnp.int32, (FZ, FZ), 0)
    sub = TILE // 8

    for n, (own, live, others) in enumerate(devices):
        column = jnp.concatenate(list(own) + [jnp.zeros((5, FZ), jnp.float32)], axis=0).T

        def tile(t, n=n, column=column, others=others):
            part = column[TILE * t : TILE * t + TILE]
            mine = [
                jnp.broadcast_to(part[:, c : c + 1], (TILE, FZ)).reshape(sub, 8, FZ)
                for c in range(3)
            ]
            moved = {step: mine[0] - step * float(CX) for step in (-1, 0, 1)}
            total = None
            for place, step in others:
                dx = moved[step] - rows[4 * place][None]
                dy = mine[1] - rows[4 * place + 1][None]
                dz = mine[2] - rows[4 * place + 2][None]
                dz = jnp.where(
                    dz > 0.5 * CZ, dz - CZ, jnp.where(dz < -0.5 * CZ, dz + CZ, dz)
                )
                reach = jnp.maximum(
                    rows[4 * place + 3][None]
                    - (dx * dx + dy * dy + dz * dz) * (1.0 / (cutoff * cutoff)),
                    0.0,
                )
                weight = reach * reach
                new = (weight * dx, weight * dy, weight * dz)
                total = new if total is None else tuple(a + b for a, b in zip(total, new))
            for c in range(3):
                start = FZ * (3 * n + c) + TILE * t
                terms[start : start + TILE] = total[c].reshape(TILE, FZ)

        for t in range(FZ // TILE):
            pl.when(TILE * t < live)(functools.partial(tile, t))

    forces = []
    for n, (own, live, others) in enumerate(devices):
        left = jnp.where(
            jnp.concatenate([slot < live] * 3), terms[3 * FZ * n : 3 * FZ * (n + 1)], 0.0
        )
        back = None
        for part in range(3):
            piece = left.astype(jnp.bfloat16)
            term = lax.dot_general(ones, piece, NT, preferred_element_type=jnp.float32)
            back = term if back is None else back + term
            if part < 2:
                left = left - piece.astype(jnp.float32)
        forces.append([stiffness * back[0:1, FZ * c : FZ * c + FZ] for c in range(3)])
    return forces


def pair_scratch(width):
    return [
        VMEM((12 * (width + 2), 8, FZ), jnp.float32),
        VMEM((3 * FZ * width, FZ), jnp.float32),
    ]


def store_rows(rows, place, packet, step_y):
    x, y, z, alive = packet
    values = (x, y + step_y, z, jnp.where(alive > 0.0, 1.0, -1.0))
    for c in range(4):
        rows[4 * place + c] = jnp.broadcast_to(values[c], (8, FZ))


def toward(axis, cells):
    return ((2 * parity(axis) - 1) * cells).astype(jnp.float32)


def live_count(alive):
    return jnp.sum(alive).astype(jnp.int32)


def advance(own, velocity, mass, alive, force):
    velocity = [
        velocity[c] + timestep * jnp.where(alive > 0.0, force[c], 0.0) / mass for c in range(3)
    ]
    return [own[c] + timestep * velocity[c] for c in range(3)], velocity


def fields_kernel(
    count, part, odd1, even1, odd2, even2, state, numbers_in,
    field_out, rest_out, packets,
    full, numbers, pair_rows, pair_terms,
):
    add_x(part, odd1, even1, full)
    forward = parity("yz") == 1
    for p in range(2):
        rows = slice(9 * p, 9 * p + 9)
        first = pl.ds(p * ROWS, KX, JP)
        full[first, :] = full[first, :] + jnp.where(forward, even2[rows], odd2[rows])
        last = pl.ds(p * ROWS + 8, KX, JP)
        full[last, :] = full[last, :] + jnp.where(forward, odd2[rows], even2[rows])
    numbers[...] = numbers_in[...]
    numbers[JP * CX : JP * CX + 8] = later_x(odd1, even1, slice(24, 32))
    numbers[pl.ds(8, KX, JP), :] = jnp.where(forward, odd2[30:39], even2[30:39])

    lane = lax.broadcasted_iota(jnp.int32, (8, FZ), 1)
    number = (lane & (DIRECTIONS - 1)).astype(jnp.float32)
    height = 1.0 - (2.0 * number + 1.0) / DIRECTIONS
    radius = jnp.sqrt(1.0 - height * height)
    phase = number * golden
    index = numbers[...].astype(jnp.int32)
    n0, n1, n2 = [
        jnp.take_along_axis(jnp.broadcast_to(table[0:1], (ROWS, FZ)), index, axis=1)
        for table in (radius * jnp.cos(phase), radius * jnp.sin(phase), height)
    ]

    lower = lax.broadcasted_iota(jnp.int32, (ROWS, FZ), 1) < CZ
    first, second = full[0:ROWS], full[ROWS : 2 * ROWS]
    heavy = jnp.maximum(jnp.where(lower, pltpu.roll(second, CZ, 1), second), fill_mass)
    mean_xy = first / heavy
    mean_z = second / heavy
    mean_yx = pltpu.roll(mean_xy, CZ, 1)
    mean_z_up = pltpu.roll(mean_z, CZ, 1)
    turn = 1.0 - cos_angle
    t0, t1, t2 = turn * n0, turn * n1, turn * n2
    s0, s1, s2 = sin_angle * n0, sin_angle * n1, sin_angle * n2
    field_out[0] = jnp.where(lower, cos_angle + t0 * n0, t0 * n1 - s2)
    field_out[1] = jnp.where(lower, t0 * n2 + s1, t0 * n1 + s2)
    field_out[2] = jnp.where(lower, cos_angle + t1 * n1, t1 * n2 - s0)
    field_out[3] = jnp.where(lower, t0 * n2 - s1, t1 * n2 + s0)
    field_out[4] = jnp.where(lower, cos_angle + t2 * n2, mean_yx)
    field_out[5] = jnp.where(lower, mean_yx, mean_z_up)

    place = state[8:9].astype(jnp.int32)
    lz = state[9:10].astype(jnp.int32)
    to_place = (lax.broadcasted_iota(jnp.int32, (CZ, FZ), 0) == lz).astype(jnp.float32)
    none = jnp.zeros_like(to_place)
    right = jnp.concatenate(
        [jnp.concatenate([to_place, none], axis=1), jnp.concatenate([none, to_place], axis=1)],
        axis=0,
    )
    hit = lax.broadcasted_iota(jnp.int32, (ROWS, FZ), 0) == place
    picked = []
    for pair in (mean_xy, jnp.where(lower, mean_z, n0), jnp.where(lower, n1, n2)):
        at_z = exact_dot(pair, right, NN)
        for half in (at_z[:, :FZ], at_z[:, FZ:]):
            picked.append(jnp.sum(jnp.where(hit, half, 0.0), axis=0, keepdims=True))
    u, n = picked[:3], picked[3:]
    alive = state[7:8] > 0.0
    old = [state[3 + c : 4 + c] for c in range(3)]
    rel = [old[c] - u[c] for c in range(3)]
    cross = [n[1] * rel[2] - n[2] * rel[1], n[2] * rel[0] - n[0] * rel[2], n[0] * rel[1] - n[1] * rel[0]]
    along = n[0] * rel[0] + n[1] * rel[1] + n[2] * rel[2]
    velocity = [
        jnp.where(
            alive,
            u[c] + cos_angle * rel[c] + sin_angle * cross[c] + turn * along * n[c],
            old[c],
        )
        for c in range(3)
    ]

    own = [state[c : c + 1] for c in range(3)]
    alive_row = state[7:8]

    def rows(b, a):
        if b == 1 and a == 1:
            return own + [alive_row]
        if b == 1:
            source, base = (odd1, 18) if a == 0 else (even1, 18)
        else:
            source, base = (odd2 if b == 0 else even2), 18 + 4 * a
        return [source[base + c : base + c + 1] for c in range(4)]

    rest_out[0:7] = state[0:7]
    rest_out[7:8] = alive_row
    after = parity("gx") == 1
    for b in range(3):
        step_y = (1 - b) * toward("yz", CY)
        slots = [rows(b, a) for a in range(3)]
        first = [jnp.where(after, e, o) for o, e in zip(slots[0], slots[2])]
        last = [jnp.where(after, o, e) for o, e in zip(slots[0], slots[2])]
        for a, packet in enumerate((first, slots[1], last)):
            store_rows(pair_rows, 3 * b + a, packet, step_y)
    others = [(3 * b + a, a - 1) for b in range(3) for a in range(3)]
    force = pair_force([(own, count[0, 0], others)], pair_rows, pair_terms)[0]
    moved, velocity = advance(own, velocity, state[6:7], alive_row, force)
    packet = jnp.concatenate(moved + [alive_row] + velocity + [state[6:7]], axis=0)
    for g in range(packets.shape[0]):
        packets[g] = packet


def cell_fields(count, part, odd1, even1, odd2, even2, state, numbers):
    return pl.pallas_call(
        fields_kernel,
        out_shape=(struct(6, ROWS, FZ), struct(8, FZ), struct(lax.axis_size("gx"), 8, FZ)),
        in_specs=[IN_SMEM] + [IN_VMEM] * 7,
        out_specs=(IN_VMEM,) * 3,
        scratch_shapes=[
            VMEM((2 * ROWS, FZ), jnp.float32),
            VMEM((ROWS, FZ), jnp.float32),
            *pair_scratch(1),
        ],
        compiler_params=pltpu.CompilerParams(vmem_limit_bytes=SMALL_LIMIT),
        cost_estimate=pl.CostEstimate(flops=4_000_000, bytes_accessed=1_000_000, transcendentals=0),
        name="cell_fields",
    )(count, part, odd1, even1, odd2, even2, state, numbers)


def padded(rows):
    return -(-rows // 8) * 8


def clear_tail(ref, used):
    if used < ref.shape[0]:
        ref[used:] = jnp.zeros((ref.shape[0] - used, FZ), jnp.float32)


def pick_kernel(width, packets, row_out, moving_out):
    count = packets.shape[0]
    me = lax.axis_index("gx")
    for a in range(width):
        source = lax.rem(me + a - width // 2 + 8 * count, count)
        row_out[4 * a : 4 * a + 4] = packets[source, 0:4]
        if 0 < a < width - 1:
            moving_out[4 * a - 4 : 4 * a] = packets[source, 4:8]
    clear_tail(row_out, 4 * width)
    clear_tail(moving_out, 4 * (width - 2))


def pick(width, packets):
    return pl.pallas_call(
        functools.partial(pick_kernel, width),
        out_shape=(struct(padded(4 * width), FZ), struct(padded(4 * (width - 2)), FZ)),
        in_specs=[IN_VMEM],
        out_specs=(IN_VMEM,) * 2,
        compiler_params=pltpu.CompilerParams(vmem_limit_bytes=SMALL_LIMIT),
        cost_estimate=pl.CostEstimate(flops=10_000, bytes_accessed=100_000, transcendentals=0),
        name="pick",
    )(packets)


def substep_moves(width, row, moving, odd, even, rows, terms):
    span = width + 2
    for b, source in enumerate((odd, row, even)):
        step_y = (1 - b) * toward("yz", CY)
        for a in range(span):
            packet = [source[4 * a + c : 4 * a + c + 1] for c in range(4)]
            store_rows(rows, span * b + a, packet, step_y)
    devices = []
    for n in range(width):
        at = 4 * (n + 1)
        own = [row[at + c : at + c + 1] for c in range(3)]
        others = [(span * b + n + 1 + step, step) for b in range(3) for step in (-1, 0, 1)]
        devices.append((own, live_count(row[at + 3 : at + 4]), others))
    forces = pair_force(devices, rows, terms)
    results = []
    for n in range(width):
        alive = row[4 * n + 7 : 4 * n + 8]
        velocity = [moving[4 * n + c : 4 * n + c + 1] for c in range(3)]
        mass = moving[4 * n + 3 : 4 * n + 4]
        results.append((*advance(devices[n][0], velocity, mass, alive, forces[n]), alive, mass))
    return results


def substep_kernel(width, row, moving, odd, even, row_out, moving_out, rows, terms):
    results = substep_moves(width, row, moving, odd, even, rows, terms)
    for n, (moved, velocity, alive, mass) in enumerate(results):
        row_out[4 * n : 4 * n + 4] = jnp.concatenate(moved + [alive], axis=0)
        if 0 < n < width - 1:
            moving_out[4 * n - 4 : 4 * n] = jnp.concatenate(velocity + [mass], axis=0)
    clear_tail(row_out, 4 * width)
    clear_tail(moving_out, 4 * (width - 2))


def last_kernel(row, moving, odd, even, rest, pos_out, vel_out, rows, terms):
    ((moved, velocity, alive, mass),) = substep_moves(1, row, moving, odd, even, rows, terms)
    keep = rest[7:8] > 0.0
    for c in range(3):
        pos_out[c] = jnp.where(keep, moved[c], rest[c : c + 1])
        vel_out[c] = jnp.where(keep, velocity[c], rest[3 + c : 4 + c])


def substep(width, row, moving, odd, even, rest):
    if width > 1:
        kernel = functools.partial(substep_kernel, width)
        shapes = (struct(padded(4 * width), FZ), struct(padded(4 * (width - 2)), FZ))
        operands = (row, moving, odd, even)
    else:
        kernel = last_kernel
        shapes = (struct(3, 1, FZ), struct(3, 1, FZ))
        operands = (row, moving, odd, even, rest)
    return pl.pallas_call(
        kernel,
        out_shape=shapes,
        in_specs=[IN_VMEM] * len(operands),
        out_specs=(IN_VMEM,) * 2,
        scratch_shapes=pair_scratch(width),
        compiler_params=pltpu.CompilerParams(vmem_limit_bytes=SMALL_LIMIT),
        cost_estimate=pl.CostEstimate(
            flops=4_000_000 * width, bytes_accessed=100_000, transcendentals=0
        ),
        name="substep",
    )(*operands)


def turn_kernel(ks, shift, v, occ, field, *refs):
    out_at, out, twice, wide, wsem = refs[-5:]
    sx, sy, sz = shift[0], shift[1], shift[2]
    places = []
    stores = []
    for i, k in enumerate(ks):
        if k < CX:
            places += [k * SUB - sx + j for j in range(SUB)]
            here, there = pl.ds(SUB * i, SUB), pl.ds(SUB * k - sx, SUB)
            stores.append(
                [pltpu.make_async_copy(out.at[:, here], out_at.at[:, there], wsem.at[SUB * i])]
            )
        else:
            around_end = [(FX - sx + j) & (FX - 1) for j in range(SUB)]
            places += around_end
            stores.append(
                [
                    pltpu.make_async_copy(
                        out.at[:, pl.ds(SUB * i + j, 1)],
                        out_at.at[:, pl.ds(x, 1)],
                        wsem.at[SUB * i + j],
                    )
                    for j, x in enumerate(around_end)
                ]
            )
    source = lax.broadcasted_iota(jnp.int32, (CZ, FZ), 0)
    layer = lax.broadcasted_iota(jnp.int32, (CZ, FZ), 1)
    spread = (((layer + sz) & (FZ - 1)) >> 1 == source).astype(jnp.float32)
    none = jnp.zeros_like(spread)
    right = jnp.concatenate(
        [jnp.concatenate([spread, none], axis=1), jnp.concatenate([none, spread], axis=1)],
        axis=0,
    )
    layers = list(ks) + ([0] if CX in ks else [])
    for f in range(6):
        left = jnp.concatenate([field[f, JP * k : JP * k + JP] for k in layers])
        both = exact_dot(left, right, NN)
        wide[2 * f] = both[:, :FZ]
        wide[2 * f + 1] = both[:, FZ:]
    row = lax.broadcasted_iota(jnp.int32, (8, FZ), 0)
    slot = (row & 1).astype(jnp.float32)
    low = row < 8 - 2 * sy

    def turn_layer(at, planes, t):
        f = [
            jnp.where(low, wide[i, pl.ds(JP * at + t, 1), :], wide[i, pl.ds(JP * at + t + 1, 1), :])
            for i in range(12)
        ]
        rows = pl.ds(pl.multiple_of(8 * t, 8), 8)

        def plane(n, x):
            live = twice[pl.ds(pl.multiple_of(n * 2 * FY + 8 * t, 8), 8), :] > slot
            old = [v[c, x, rows, :] for c in range(3)]
            rel = [old[c] - f[9 + c] for c in range(3)]
            for c in range(3):
                new = f[9 + c] + (
                    f[3 * c] * rel[0] + f[3 * c + 1] * rel[1] + f[3 * c + 2] * rel[2]
                )
                out[c, n, rows, :] = jnp.where(live, new, old[c])

        planes(plane)

    live_planes(occ, places, twice)
    for i, k in enumerate(ks):

        def column(t, carry, i=i, k=k):
            def some(first, last):
                def run(plane):
                    def step(j, carry):
                        plane(SUB * i + j, (FX - sx + j) & (FX - 1))
                        return carry

                    lax.fori_loop(first, last, step, 0)

                return run

            if k < CX:
                turn_layer(
                    i, lambda plane: [plane(SUB * i + j, places[SUB * i + j]) for j in range(SUB)], t
                )
            else:
                turn_layer(i, some(0, sx), t)
                turn_layer(i + 1, some(sx, SUB), t)
            return carry

        lax.fori_loop(0, CY, column, 0)
        for copy in stores[i]:
            copy.start()
    for group in stores:
        for copy in group:
            copy.wait()


def turn_solvent(ks, grid_shift, v, occ, field, done=None):
    planes = SUB * len(ks)
    layers = len(ks) + (CX in ks)
    return pl.pallas_call(
        functools.partial(turn_kernel, ks),
        out_shape=struct(*v.shape),
        in_specs=[IN_SMEM, IN_VMEM, IN_VMEM, IN_VMEM] + [HBM] * (done is not None),
        out_specs=HBM,
        input_output_aliases={} if done is None else {4: 0},
        scratch_shapes=[
            VMEM((3, planes, 2 * FY, FZ), jnp.float32),
            VMEM((2 * planes * FY, FZ), jnp.float32),
            VMEM((12, JP * layers, FZ), jnp.float32),
            DMA((planes,)),
        ],
        compiler_params=pltpu.CompilerParams(vmem_limit_bytes=TURN_LIMIT),
        cost_estimate=pl.CostEstimate(flops=3_000_000, bytes_accessed=1_300_000, transcendentals=0),
        name="turn_solvent",
    )(grid_shift, v, occ, field, *([] if done is None else [done]))


def per_device(
    solvent_vel,
    occupancy,
    grid_shift,
    axis_index,
    colloid_pos,
    colloid_vel,
    colloid_mass,
    colloid_count,
):
    v = solvent_vel.reshape(3, FX, 2 * FY, FZ)
    pos = colloid_pos.reshape(3, 1, FZ)
    vel = colloid_vel.reshape(3, 1, FZ)
    mass = colloid_mass
    count = colloid_count

    base, odd, even = border_sums(grid_shift, count, v, occupancy, axis_index, pos, vel, mass)
    odd1, even1 = swap_both(odd, even, "gx")
    part, state, numbers = inner_sums(grid_shift, v, occupancy, base)
    odd, even = columns(part, odd1, even1, state, numbers)
    odd2, even2 = swap_both(odd, even, "yz")
    field, rest, packets = cell_fields(count, part, odd1, even1, odd2, even2, state, numbers)
    packets = lax.all_to_all(packets, "gx", 0, 0)
    width = 2 * (SUBSTEPS - 1) + 1
    row, moving = pick(width, packets)
    solvent_out = None
    for ks in TURNED:
        width -= 2
        if solvent_out is None:
            row, field = lax.optimization_barrier((row, field))
        else:
            row, solvent_out = lax.optimization_barrier((row, solvent_out))
        solvent_out = turn_solvent(ks, grid_shift, v, occupancy, field, solvent_out)
        odd, even = swap_both(row, row, "yz")
        odd, solvent_out = lax.optimization_barrier((odd, solvent_out))
        row, moving = substep(width, row, moving, odd, even, rest)
    position, velocity = row, moving
    return (
        solvent_out.reshape(solvent_vel.shape),
        position[:, None],
        velocity[:, None],
    )


def solution(mesh):
    return jax.shard_map(
        per_device,
        mesh=mesh,
        in_specs=(
            P(None, "gx", "yz", None, None),
            P("gx", "yz", None),
            P(),
            P("gx", "yz", None),
            P(None, "gx", "yz", None),
            P(None, "gx", "yz", None),
            P("gx", "yz", None),
            P("gx", "yz"),
        ),
        out_specs=(
            P(None, "gx", "yz", None, None),
            P(None, "gx", "yz", None),
            P(None, "gx", "yz", None),
        ),
        check_vma=False,
    )
```

```python
import functools
import math

import jax
import jax.numpy as jnp
from jax import lax
from jax.experimental import pallas as pl
from jax.experimental.pallas import tpu as pltpu
from jax.sharding import PartitionSpec as P

CX = 8
CY = 8
CZ = 64
SUB = 4
SUBSTEPS = 4
DIRECTIONS = 64
FX = 32
FY = 32
FZ = 128
KX = CX + 1
JY = CY + 1
JP = 16
ROWS = KX * JP

turn_angle = 130.0 * math.pi / 180.0
cos_angle = math.cos(turn_angle)
sin_angle = math.sin(turn_angle)
golden = math.pi * (3.0 - math.sqrt(5.0))
cutoff = 1.5
stiffness = 20.0
timestep = 0.05
fill_mass = 16.0

SMEM = pltpu.SMEM
VMEM = pltpu.VMEM
HBM = pl.BlockSpec(memory_space=pltpu.HBM)
IN_VMEM = pl.BlockSpec(memory_space=VMEM)
IN_SMEM = pl.BlockSpec(memory_space=SMEM)
DMA = pltpu.SemaphoreType.DMA
NT = (((1,), (1,)), ((), ()))
NN = (((1,), (0,)), ((), ()))
STATE = 4 * JP
NUMBERS = STATE + 16
BASE = NUMBERS + ROWS
TURNED = ((1, 2, 3), (4, 5, 6), (7, CX))
TILE = 32
SMALL_LIMIT = 8 * 1024 * 1024
TURN_LIMIT = 16 * 1024 * 1024


def swapped(value, axis, first):
    count = lax.axis_size(axis)
    pairs = []
    for low in range(first, count + first, 2):
        a, b = low % count, (low + 1) % count
        pairs += [(a, b), (b, a)]
    return lax.ppermute(value, axis, pairs)


def swap_both(odd, even, axis):
    return swapped(odd, axis, 1), swapped(even, axis, 0)


def struct(*shape):
    return jax.ShapeDtypeStruct(shape, jnp.float32)


def exact_dot(left, right, dims, parts=3):
    right = right.astype(jnp.bfloat16)
    total = None
    for part in range(parts):
        piece = left.astype(jnp.bfloat16)
        term = lax.dot_general(piece, right, dims, preferred_element_type=jnp.float32)
        total = term if total is None else total + term
        if part < parts - 1:
            left = left - piece.astype(jnp.float32)
    return total


def colloid_cells(pos, sx, sy, sz):
    cell_x = jnp.clip(jnp.floor(pos[0] * SUB).astype(jnp.int32), 0, FX - 1)
    cell_y = jnp.clip(jnp.floor(pos[1] * SUB).astype(jnp.int32), 0, FY - 1)
    cell_z = jnp.clip(jnp.floor(pos[2] * 2.0).astype(jnp.int32), 0, FZ - 1)
    return ((cell_x + sx) >> 2, (cell_y + sy) >> 2, ((cell_z + sz) & (FZ - 1)) >> 1)


def live_row(count):
    return lax.broadcasted_iota(jnp.int32, (1, FZ), 1) < count


def parity(axis):
    return lax.axis_index(axis) & 1


def live_planes(occ, places, twice):
    for n, x in enumerate(places):
        slots = occ[x].astype(jnp.float32)
        twice[pl.ds(2 * FY * n, FY, 2), :] = slots
        twice[pl.ds(2 * FY * n + 1, FY, 2), :] = slots


def add_plane(v, twice, slot, n, x, acc):
    live = twice[pl.ds(pl.multiple_of(n * 2 * FY, 2 * FY), 2 * FY), :] > slot
    masked = [jnp.where(live, v[c, x], 0.0) for c in range(3)] + [jnp.where(live, 1.0, 0.0)]
    return tuple(a + m for a, m in zip(acc, masked))


def store_cells(acc, sy, partial, at):
    row = lax.broadcasted_iota(jnp.int32, (8, FZ), 0)
    low = (row < 8 - 2 * sy)[None]
    blank = jnp.zeros((1, 8, FZ), jnp.float32)
    for c in range(4):
        parts = acc[c].reshape(CY, 8, FZ)
        picked = jnp.where(low, jnp.concatenate([parts, blank]), jnp.concatenate([blank, parts]))
        partial[c, at, 0:JY, :] = jnp.sum(picked, axis=1)


def slot_rows():
    return (lax.broadcasted_iota(jnp.int32, (2 * FY, FZ), 0) & 1).astype(jnp.float32)


def along_z(partial, carried, sz, lz, p):
    target = lax.broadcasted_iota(jnp.int32, (CZ, FZ), 0)
    layer = lax.broadcasted_iota(jnp.int32, (CZ, FZ), 1)
    to_cell = (((layer + sz) & (FZ - 1)) >> 1 == target).astype(jnp.float32)
    to_place = (target == lz).astype(jnp.float32)
    one = jnp.concatenate([to_cell, to_place], axis=1)
    none = jnp.zeros_like(one)
    right = jnp.concatenate(
        [jnp.concatenate([one, none], axis=1), jnp.concatenate([none, one], axis=1)], axis=0
    )
    size = carried[0].shape[0]
    left = jnp.concatenate(
        [
            partial[2 * p].reshape(size, FZ),
            carried[2 * p],
            partial[2 * p + 1].reshape(size, FZ),
            carried[2 * p + 1],
        ],
        axis=1,
    )
    return exact_dot(left, right, NT)


def border_kernel(
    shift_at, count_at, v_at, occ_at, axis_at, pos_at, vel_at, mass_at,
    base, odd, even,
    shift, count, v, occ, axis, pos, vel, mass, twice, partial, sem,
):
    ends = ((pl.ds(0, SUB - 1), pl.ds(0, SUB - 1)), (pl.ds(FX - SUB + 1, SUB - 1), pl.ds(SUB - 1, SUB - 1)))
    pairs = [(shift_at, shift)]
    pairs += [(occ_at.at[there], occ.at[here]) for there, here in ends]
    pairs += [(v_at.at[:, there], v.at[:, here]) for there, here in ends]
    pairs += [(count_at, count), (pos_at, pos), (vel_at, vel), (mass_at, mass), (axis_at, axis)]
    copies = [pltpu.make_async_copy(a, b, sem.at[i]) for i, (a, b) in enumerate(pairs)]
    for copy in copies:
        copy.start()
    partial[:, :, 8:JP, :] = jnp.zeros((4, 2, JP - 8, FZ), jnp.float32)
    slot = slot_rows()
    zero = jnp.zeros((2 * FY, FZ), jnp.float32)
    for copy in copies[:3]:
        copy.wait()
    sx, sy, sz = shift[0], shift[1], shift[2]
    planes = 2 * (SUB - 1)
    live_planes(occ, range(planes), twice)
    for copy in copies[3:]:
        copy.wait()

    def plane(x, acc):
        return add_plane(v, twice, slot, x, x, acc)

    store_cells(lax.fori_loop(0, SUB - sx, plane, (zero,) * 4), sy, partial, 0)
    store_cells(lax.fori_loop(planes - sx, planes, plane, (zero,) * 4), sy, partial, 1)

    kx, jy, lz = colloid_cells(pos, sx, sy, sz)
    alive = live_row(count[0, 0]).astype(jnp.float32)
    weight = mass[0] * alive
    place = jnp.where(kx == 0, jy, jnp.where(kx == CX, JP + jy, 2 * JP))
    hit = lax.broadcasted_iota(jnp.int32, (2 * JP, FZ), 0) == place
    carried = [jnp.where(hit, vel[c] * weight, 0.0) for c in range(3)]
    carried.append(jnp.where(hit, weight, 0.0))
    for p in range(2):
        base[2 * JP * p : 2 * JP * (p + 1)] = along_z(partial, carried, sz, lz, p)
    side = parity("gx")
    number = None
    base[NUMBERS : NUMBERS + ROWS] = jnp.zeros((ROWS, FZ), jnp.float32)
    for k in range(CX):
        row = axis[k].astype(jnp.float32)
        row = jnp.concatenate([row, row], axis=1)
        base[NUMBERS + JP * k : NUMBERS + JP * k + CY] = row
        number = row if k == 0 else number
    for packet, end in ((odd, side), (even, 1 - side)):
        for p in range(2):
            start = pl.multiple_of(2 * JP * p + JP * end, JP)
            packet[8 * p : 8 * p + 8] = base[pl.ds(start, 8), :]
            packet[16 + p : 17 + p] = base[pl.ds(start + 8, 1), :]
        for c in range(3):
            packet[18 + c : 19 + c] = pos[c]
        packet[21:22] = alive
        packet[22:24] = jnp.zeros((2, FZ), jnp.float32)
        packet[24:32] = number
    for c in range(3):
        base[STATE + c : STATE + c + 1] = pos[c]
        base[STATE + 3 + c : STATE + 4 + c] = vel[c]
    base[STATE + 6 : STATE + 7] = mass[0]
    base[STATE + 7 : STATE + 8] = alive
    base[STATE + 8 : STATE + 9] = (kx * JP + jy).astype(jnp.float32)
    base[STATE + 9 : STATE + 10] = lz.astype(jnp.float32)
    base[STATE + 10 : STATE + 16] = jnp.zeros((6, FZ), jnp.float32)


def border_sums(grid_shift, count, v, occ, axis_index, pos, vel, mass):
    planes = 2 * (SUB - 1)
    return pl.pallas_call(
        border_kernel,
        out_shape=(struct(BASE, FZ), struct(32, FZ), struct(32, FZ)),
        in_specs=[HBM] * 8,
        out_specs=(IN_VMEM,) * 3,
        scratch_shapes=[
            SMEM((3,), jnp.int32),
            SMEM((1, 1), jnp.int32),
            VMEM((3, planes, 2 * FY, FZ), jnp.float32),
            VMEM((planes, FY, FZ), jnp.int32),
            VMEM((CX, CY, CZ), jnp.int32),
            VMEM((3, 1, FZ), jnp.float32),
            VMEM((3, 1, FZ), jnp.float32),
            VMEM((1, 1, FZ), jnp.float32),
            VMEM((2 * planes * FY, FZ), jnp.float32),
            VMEM((4, 2, JP, FZ), jnp.float32),
            DMA((10,)),
        ],
        cost_estimate=pl.CostEstimate(flops=1_000_000, bytes_accessed=800_000, transcendentals=0),
        name="border_sums",
    )(grid_shift, count, v, occ, axis_index, pos, vel, mass)


def inner_kernel(shift, v, occ, base, part, state, numbers, twice, partial):
    sx, sy, sz = shift[0], shift[1], shift[2]
    state[...] = base[STATE:NUMBERS]
    numbers[...] = base[NUMBERS:BASE]
    partial[:, :, 8:JP, :] = jnp.zeros((4, CX - 1, JP - 8, FZ), jnp.float32)
    slot = slot_rows()
    zero = jnp.zeros((2 * FY, FZ), jnp.float32)
    live_planes(occ, [SUB - sx + n for n in range(SUB * (CX - 1))], twice)
    for k in range(1, CX):
        acc = (zero,) * 4
        for j in range(SUB):
            acc = add_plane(v, twice, slot, SUB * (k - 1) + j, k * SUB - sx + j, acc)
        store_cells(acc, sy, partial, k - 1)
    weight = base[STATE + 6 : STATE + 7] * base[STATE + 7 : STATE + 8]
    place = base[STATE + 8 : STATE + 9].astype(jnp.int32) - JP
    lz = base[STATE + 9 : STATE + 10].astype(jnp.int32)
    inner = JP * (CX - 1)
    hit = lax.broadcasted_iota(jnp.int32, (inner, FZ), 0) == place
    carried = [
        jnp.where(hit, base[STATE + 3 + c : STATE + 4 + c] * weight, 0.0) for c in range(3)
    ]
    carried.append(jnp.where(hit, weight, 0.0))
    for p in range(2):
        first = p * ROWS
        part[first : first + JP] = base[2 * JP * p : 2 * JP * p + JP]
        part[first + JP : first + JP + inner] = along_z(partial, carried, sz, lz, p)
        part[first + CX * JP : first + ROWS] = base[2 * JP * p + JP : 2 * JP * (p + 1)]


def inner_sums(grid_shift, v, occ, base):
    return pl.pallas_call(
        inner_kernel,
        out_shape=(struct(2 * ROWS, FZ), struct(16, FZ), struct(ROWS, FZ)),
        in_specs=[IN_SMEM] + [IN_VMEM] * 3,
        out_specs=(IN_VMEM,) * 3,
        scratch_shapes=[
            VMEM((2 * SUB * (CX - 1) * FY, FZ), jnp.float32),
            VMEM((4, CX - 1, JP, FZ), jnp.float32),
        ],
        compiler_params=pltpu.CompilerParams(vmem_limit_bytes=TURN_LIMIT),
        cost_estimate=pl.CostEstimate(flops=4_000_000, bytes_accessed=3_700_000, transcendentals=0),
        name="inner_sums",
    )(grid_shift, v, occ, base)


def add_x(part, odd, even, full):
    full[...] = part[...]
    turned = parity("gx") * (CX * JP)
    for p in range(2):
        for packet, place in ((odd, turned), (even, CX * JP - turned)):
            start = pl.multiple_of(p * ROWS + place, JP)
            full[pl.ds(start, 8), :] += packet[8 * p : 8 * p + 8]
            full[pl.ds(start + 8, 1), :] += packet[16 + p : 17 + p]


def later_x(odd, even, rows):
    return jnp.where(parity("gx") == 1, odd[rows], even[rows])


def columns_kernel(part, odd1, even1, state, numbers, odd, even, full, ends):
    add_x(part, odd1, even1, full)
    for p in range(2):
        ends[0, 9 * p : 9 * p + 9] = full[pl.ds(p * ROWS, KX, JP), :]
        ends[1, 9 * p : 9 * p + 9] = full[pl.ds(p * ROWS + 8, KX, JP), :]
    side = parity("yz")
    for packet, end in ((odd, side), (even, 1 - side)):
        packet[0:18] = ends[end, 0:18]
        packet[18:22] = odd1[18:22]
        packet[22:25] = state[0:3]
        packet[25:26] = state[7:8]
        packet[26:30] = even1[18:22]
        packet[30:38] = numbers[pl.ds(0, CX, JP), :]
        packet[38:39] = later_x(odd1, even1, slice(24, 25))
        packet[39:40] = jnp.zeros((1, FZ), jnp.float32)


def columns(part, odd1, even1, state, numbers):
    return pl.pallas_call(
        columns_kernel,
        out_shape=(struct(40, FZ), struct(40, FZ)),
        in_specs=[IN_VMEM] * 5,
        out_specs=(IN_VMEM,) * 2,
        scratch_shapes=[VMEM((2 * ROWS, FZ), jnp.float32), VMEM((2, 24, FZ), jnp.float32)],
        compiler_params=pltpu.CompilerParams(vmem_limit_bytes=SMALL_LIMIT),
        cost_estimate=pl.CostEstimate(flops=100_000, bytes_accessed=500_000, transcendentals=0),
        name="columns",
    )(part, odd1, even1, state, numbers)


def store_around(rows, base, others):
    wide = [[jnp.broadcast_to(value, (8, FZ)) for value in packet] for packet in others]
    low = lax.broadcasted_iota(jnp.int32, (8, FZ), 1) < FZ // 2
    reach = None
    for c in range(4):
        rows[base + c] = wide[0][c]
        for p in range(4):
            a, b = wide[1 + 2 * p][c], wide[2 + 2 * p][c]
            rows[base + 4 + 4 * p + c] = jnp.where(low, a, pltpu.roll(b, FZ // 2, 1))
            late = jnp.where(low, pltpu.roll(a, FZ // 2, 1), b)
            rows[base + 20 + 4 * p + c] = late
            if c == 3:
                reach = late if reach is None else jnp.maximum(reach, late)
    return jnp.max(reach) > 0.0


def pair_force(devices, rows, terms):
    ones = jnp.ones((8, FZ), jnp.bfloat16)
    slot = lax.broadcasted_iota(jnp.int32, (FZ, FZ), 0)
    sub = TILE // 8

    for n, (own, live, others) in enumerate(devices):
        base = 36 * n
        crowded = store_around(rows, base, others)
        column = jnp.concatenate(list(own) + [jnp.zeros((5, FZ), jnp.float32)], axis=0).T

        def tile(t, n=n, column=column, base=base, crowded=crowded):
            part = column[TILE * t : TILE * t + TILE]
            mine = [
                jnp.broadcast_to(part[:, c : c + 1], (TILE, FZ)).reshape(sub, 8, FZ)
                for c in range(3)
            ]

            def force(places):
                total = None
                for place in places:
                    dx = mine[0] - rows[place][None]
                    dy = mine[1] - rows[place + 1][None]
                    dz = mine[2] - rows[place + 2][None]
                    dz = jnp.where(
                        dz > 0.5 * CZ, dz - CZ, jnp.where(dz < -0.5 * CZ, dz + CZ, dz)
                    )
                    reach = jnp.maximum(
                        rows[place + 3][None]
                        - (dx * dx + dy * dy + dz * dz) * (1.0 / (cutoff * cutoff)),
                        0.0,
                    )
                    weight = reach * reach
                    new = (weight * dx, weight * dy, weight * dz)
                    total = new if total is None else tuple(a + b for a, b in zip(total, new))
                return total

            at = [pl.ds(FZ * (3 * n + c) + TILE * t, TILE) for c in range(3)]
            for c, value in enumerate(force(range(base, base + 20, 4))):
                terms[at[c], :] = value.reshape(TILE, FZ)

            @pl.when(crowded)
            def _():
                for c, value in enumerate(force(range(base + 20, base + 36, 4))):
                    terms[at[c], :] = terms[at[c], :] + value.reshape(TILE, FZ)

        for t in range(FZ // TILE):
            pl.when(TILE * t < live)(functools.partial(tile, t))

    forces = []
    for n, (own, live, others) in enumerate(devices):
        left = jnp.where(
            jnp.concatenate([slot < live] * 3), terms[3 * FZ * n : 3 * FZ * (n + 1)], 0.0
        )
        back = None
        for part in range(2):
            piece = left.astype(jnp.bfloat16)
            term = lax.dot_general(ones, piece, NT, preferred_element_type=jnp.float32)
            back = term if back is None else back + term
            if part < 1:
                left = left - piece.astype(jnp.float32)
        forces.append([stiffness * back[0:1, FZ * c : FZ * c + FZ] for c in range(3)])
    return forces


def pair_scratch(width):
    return [
        VMEM((36 * width, 8, FZ), jnp.float32),
        VMEM((3 * FZ * width, FZ), jnp.float32),
    ]


def placed(packet, step_x, step_y):
    x, y, z, alive = packet
    return (x + step_x, y + step_y, z, jnp.where(alive > 0.0, 1.0, -1.0))


def middle_first(values):
    return values[4:5] + values[:4] + values[5:]


def toward(axis, cells):
    return ((2 * parity(axis) - 1) * cells).astype(jnp.float32)


def live_count(alive):
    return jnp.sum(alive).astype(jnp.int32)


def advance(own, velocity, mass, alive, force):
    velocity = [
        velocity[c] + timestep * jnp.where(alive > 0.0, force[c], 0.0) / mass for c in range(3)
    ]
    return [own[c] + timestep * velocity[c] for c in range(3)], velocity


def fields_kernel(
    count, part, odd1, even1, odd2, even2, state, numbers_in,
    field_out, rest_out, packets,
    full, numbers, pair_rows, pair_terms,
):
    add_x(part, odd1, even1, full)
    forward = parity("yz") == 1
    for p in range(2):
        rows = slice(9 * p, 9 * p + 9)
        first = pl.ds(p * ROWS, KX, JP)
        full[first, :] = full[first, :] + jnp.where(forward, even2[rows], odd2[rows])
        last = pl.ds(p * ROWS + 8, KX, JP)
        full[last, :] = full[last, :] + jnp.where(forward, odd2[rows], even2[rows])
    numbers[...] = numbers_in[...]
    numbers[JP * CX : JP * CX + 8] = later_x(odd1, even1, slice(24, 32))
    numbers[pl.ds(8, KX, JP), :] = jnp.where(forward, odd2[30:39], even2[30:39])

    lane = lax.broadcasted_iota(jnp.int32, (8, FZ), 1)
    number = (lane & (DIRECTIONS - 1)).astype(jnp.float32)
    height = 1.0 - (2.0 * number + 1.0) / DIRECTIONS
    radius = jnp.sqrt(1.0 - height * height)
    phase = number * golden
    index = numbers[...].astype(jnp.int32)
    n0, n1, n2 = [
        jnp.take_along_axis(jnp.broadcast_to(table[0:1], (ROWS, FZ)), index, axis=1)
        for table in (radius * jnp.cos(phase), radius * jnp.sin(phase), height)
    ]

    lower = lax.broadcasted_iota(jnp.int32, (ROWS, FZ), 1) < CZ
    first, second = full[0:ROWS], full[ROWS : 2 * ROWS]
    heavy = jnp.maximum(jnp.where(lower, pltpu.roll(second, CZ, 1), second), fill_mass)
    mean_xy = first / heavy
    mean_z = second / heavy
    mean_yx = pltpu.roll(mean_xy, CZ, 1)
    mean_z_up = pltpu.roll(mean_z, CZ, 1)
    turn = 1.0 - cos_angle
    t0, t1, t2 = turn * n0, turn * n1, turn * n2
    s0, s1, s2 = sin_angle * n0, sin_angle * n1, sin_angle * n2
    field_out[0] = jnp.where(lower, cos_angle + t0 * n0, t0 * n1 - s2)
    field_out[1] = jnp.where(lower, t0 * n2 + s1, t0 * n1 + s2)
    field_out[2] = jnp.where(lower, cos_angle + t1 * n1, t1 * n2 - s0)
    field_out[3] = jnp.where(lower, t0 * n2 - s1, t1 * n2 + s0)
    field_out[4] = jnp.where(lower, cos_angle + t2 * n2, mean_yx)
    field_out[5] = jnp.where(lower, mean_yx, mean_z_up)

    place = state[8:9].astype(jnp.int32)
    lz = state[9:10].astype(jnp.int32)
    to_place = (lax.broadcasted_iota(jnp.int32, (CZ, FZ), 0) == lz).astype(jnp.float32)
    none = jnp.zeros_like(to_place)
    right = jnp.concatenate(
        [jnp.concatenate([to_place, none], axis=1), jnp.concatenate([none, to_place], axis=1)],
        axis=0,
    )
    hit = lax.broadcasted_iota(jnp.int32, (ROWS, FZ), 0) == place
    picked = []
    for pair in (mean_xy, jnp.where(lower, mean_z, n0), jnp.where(lower, n1, n2)):
        at_z = exact_dot(pair, right, NN)
        for half in (at_z[:, :FZ], at_z[:, FZ:]):
            picked.append(jnp.sum(jnp.where(hit, half, 0.0), axis=0, keepdims=True))
    u, n = picked[:3], picked[3:]
    alive = state[7:8] > 0.0
    old = [state[3 + c : 4 + c] for c in range(3)]
    rel = [old[c] - u[c] for c in range(3)]
    cross = [n[1] * rel[2] - n[2] * rel[1], n[2] * rel[0] - n[0] * rel[2], n[0] * rel[1] - n[1] * rel[0]]
    along = n[0] * rel[0] + n[1] * rel[1] + n[2] * rel[2]
    velocity = [
        jnp.where(
            alive,
            u[c] + cos_angle * rel[c] + sin_angle * cross[c] + turn * along * n[c],
            old[c],
        )
        for c in range(3)
    ]

    own = [state[c : c + 1] for c in range(3)]
    alive_row = state[7:8]

    def rows(b, a):
        if b == 1 and a == 1:
            return own + [alive_row]
        if b == 1:
            source, base = (odd1, 18) if a == 0 else (even1, 18)
        else:
            source, base = (odd2 if b == 0 else even2), 18 + 4 * a
        return [source[base + c : base + c + 1] for c in range(4)]

    rest_out[0:7] = state[0:7]
    rest_out[7:8] = alive_row
    after = parity("gx") == 1
    others = []
    for b in range(3):
        step_y = (1 - b) * toward("yz", CY)
        slots = [rows(b, a) for a in range(3)]
        first = [jnp.where(after, e, o) for o, e in zip(slots[0], slots[2])]
        last = [jnp.where(after, o, e) for o, e in zip(slots[0], slots[2])]
        for a, packet in enumerate((first, slots[1], last)):
            others.append(placed(packet, (a - 1) * float(CX), step_y))
    force = pair_force([(own, count[0, 0], middle_first(others))], pair_rows, pair_terms)[0]
    moved, velocity = advance(own, velocity, state[6:7], alive_row, force)
    packet = jnp.concatenate(moved + [alive_row] + velocity + [state[6:7]], axis=0)
    for g in range(packets.shape[0]):
        packets[g] = packet


def cell_fields(count, part, odd1, even1, odd2, even2, state, numbers):
    return pl.pallas_call(
        fields_kernel,
        out_shape=(struct(6, ROWS, FZ), struct(8, FZ), struct(lax.axis_size("gx"), 8, FZ)),
        in_specs=[IN_SMEM] + [IN_VMEM] * 7,
        out_specs=(IN_VMEM,) * 3,
        scratch_shapes=[
            VMEM((2 * ROWS, FZ), jnp.float32),
            VMEM((ROWS, FZ), jnp.float32),
            *pair_scratch(1),
        ],
        compiler_params=pltpu.CompilerParams(vmem_limit_bytes=SMALL_LIMIT),
        cost_estimate=pl.CostEstimate(flops=4_000_000, bytes_accessed=1_000_000, transcendentals=0),
        name="cell_fields",
    )(count, part, odd1, even1, odd2, even2, state, numbers)


def padded(rows):
    return -(-rows // 8) * 8


def clear_tail(ref, used):
    if used < ref.shape[0]:
        ref[used:] = jnp.zeros((ref.shape[0] - used, FZ), jnp.float32)


def pick_kernel(width, packets, row_out, moving_out):
    count = packets.shape[0]
    me = lax.axis_index("gx")
    for a in range(width):
        source = lax.rem(me + a - width // 2 + 8 * count, count)
        row_out[4 * a : 4 * a + 4] = packets[source, 0:4]
        if 0 < a < width - 1:
            moving_out[4 * a - 4 : 4 * a] = packets[source, 4:8]
    clear_tail(row_out, 4 * width)
    clear_tail(moving_out, 4 * (width - 2))


def pick(width, packets):
    return pl.pallas_call(
        functools.partial(pick_kernel, width),
        out_shape=(struct(padded(4 * width), FZ), struct(padded(4 * (width - 2)), FZ)),
        in_specs=[IN_VMEM],
        out_specs=(IN_VMEM,) * 2,
        compiler_params=pltpu.CompilerParams(vmem_limit_bytes=SMALL_LIMIT),
        cost_estimate=pl.CostEstimate(flops=10_000, bytes_accessed=100_000, transcendentals=0),
        name="pick",
    )(packets)


def substep_moves(width, row, moving, odd, even, rows, terms):
    sources = (odd, row, even)
    devices = []
    for n in range(width):
        at = 4 * (n + 1)
        own = [row[at + c : at + c + 1] for c in range(3)]
        others = []
        for b, source in enumerate(sources):
            step_y = (1 - b) * toward("yz", CY)
            for step in (-1, 0, 1):
                start = at + 4 * step
                packet = [source[start + c : start + c + 1] for c in range(4)]
                others.append(placed(packet, step * float(CX), step_y))
        devices.append((own, live_count(row[at + 3 : at + 4]), middle_first(others)))
    forces = pair_force(devices, rows, terms)
    results = []
    for n in range(width):
        alive = row[4 * n + 7 : 4 * n + 8]
        velocity = [moving[4 * n + c : 4 * n + c + 1] for c in range(3)]
        mass = moving[4 * n + 3 : 4 * n + 4]
        results.append((*advance(devices[n][0], velocity, mass, alive, forces[n]), alive, mass))
    return results


def substep_kernel(width, row, moving, odd, even, row_out, moving_out, rows, terms):
    results = substep_moves(width, row, moving, odd, even, rows, terms)
    for n, (moved, velocity, alive, mass) in enumerate(results):
        row_out[4 * n : 4 * n + 4] = jnp.concatenate(moved + [alive], axis=0)
        if 0 < n < width - 1:
            moving_out[4 * n - 4 : 4 * n] = jnp.concatenate(velocity + [mass], axis=0)
    clear_tail(row_out, 4 * width)
    clear_tail(moving_out, 4 * (width - 2))


def last_kernel(row, moving, odd, even, rest, pos_out, vel_out, rows, terms):
    ((moved, velocity, alive, mass),) = substep_moves(1, row, moving, odd, even, rows, terms)
    keep = rest[7:8] > 0.0
    for c in range(3):
        pos_out[c] = jnp.where(keep, moved[c], rest[c : c + 1])
        vel_out[c] = jnp.where(keep, velocity[c], rest[3 + c : 4 + c])


def substep(width, row, moving, odd, even, rest):
    if width > 1:
        kernel = functools.partial(substep_kernel, width)
        shapes = (struct(padded(4 * width), FZ), struct(padded(4 * (width - 2)), FZ))
        operands = (row, moving, odd, even)
    else:
        kernel = last_kernel
        shapes = (struct(3, 1, FZ), struct(3, 1, FZ))
        operands = (row, moving, odd, even, rest)
    return pl.pallas_call(
        kernel,
        out_shape=shapes,
        in_specs=[IN_VMEM] * len(operands),
        out_specs=(IN_VMEM,) * 2,
        scratch_shapes=pair_scratch(width),
        compiler_params=pltpu.CompilerParams(vmem_limit_bytes=SMALL_LIMIT),
        cost_estimate=pl.CostEstimate(
            flops=4_000_000 * width, bytes_accessed=100_000, transcendentals=0
        ),
        name="substep",
    )(*operands)


def turn_kernel(ks, shift, v, occ, field, *refs):
    out_at, out, twice, wide, wsem = refs[-5:]
    sx, sy, sz = shift[0], shift[1], shift[2]
    places = []
    stores = []
    for i, k in enumerate(ks):
        if k < CX:
            places += [k * SUB - sx + j for j in range(SUB)]
            here, there = pl.ds(SUB * i, SUB), pl.ds(SUB * k - sx, SUB)
            stores.append(
                [pltpu.make_async_copy(out.at[:, here], out_at.at[:, there], wsem.at[SUB * i])]
            )
        else:
            around_end = [(FX - sx + j) & (FX - 1) for j in range(SUB)]
            places += around_end
            stores.append(
                [
                    pltpu.make_async_copy(
                        out.at[:, pl.ds(SUB * i + j, 1)],
                        out_at.at[:, pl.ds(x, 1)],
                        wsem.at[SUB * i + j],
                    )
                    for j, x in enumerate(around_end)
                ]
            )
    source = lax.broadcasted_iota(jnp.int32, (CZ, FZ), 0)
    layer = lax.broadcasted_iota(jnp.int32, (CZ, FZ), 1)
    spread = (((layer + sz) & (FZ - 1)) >> 1 == source).astype(jnp.float32)
    none = jnp.zeros_like(spread)
    right = jnp.concatenate(
        [jnp.concatenate([spread, none], axis=1), jnp.concatenate([none, spread], axis=1)],
        axis=0,
    )
    layers = list(ks) + ([0] if CX in ks else [])
    for f in range(6):
        left = jnp.concatenate([field[f, JP * k : JP * k + JP] for k in layers])
        both = exact_dot(left, right, NN, parts=2)
        wide[2 * f] = both[:, :FZ]
        wide[2 * f + 1] = both[:, FZ:]
    row = lax.broadcasted_iota(jnp.int32, (8, FZ), 0)
    slot = (row & 1).astype(jnp.float32)
    low = row < 8 - 2 * sy

    def turn_layer(at, planes, t):
        f = [
            jnp.where(low, wide[i, pl.ds(JP * at + t, 1), :], wide[i, pl.ds(JP * at + t + 1, 1), :])
            for i in range(12)
        ]
        rows = pl.ds(pl.multiple_of(8 * t, 8), 8)

        def plane(n, x):
            live = twice[pl.ds(pl.multiple_of(n * 2 * FY + 8 * t, 8), 8), :] > slot
            old = [v[c, x, rows, :] for c in range(3)]
            rel = [old[c] - f[9 + c] for c in range(3)]
            for c in range(3):
                new = f[9 + c] + (
                    f[3 * c] * rel[0] + f[3 * c + 1] * rel[1] + f[3 * c + 2] * rel[2]
                )
                out[c, n, rows, :] = jnp.where(live, new, old[c])

        planes(plane)

    live_planes(occ, places, twice)
    for i, k in enumerate(ks):

        def column(t, carry, i=i, k=k):
            def some(first, last):
                def run(plane):
                    def step(j, carry):
                        plane(SUB * i + j, (FX - sx + j) & (FX - 1))
                        return carry

                    lax.fori_loop(first, last, step, 0)

                return run

            if k < CX:
                turn_layer(
                    i, lambda plane: [plane(SUB * i + j, places[SUB * i + j]) for j in range(SUB)], t
                )
            else:
                turn_layer(i, some(0, sx), t)
                turn_layer(i + 1, some(sx, SUB), t)
            return carry

        lax.fori_loop(0, CY, column, 0)
        for copy in stores[i]:
            copy.start()
    for group in stores:
        for copy in group:
            copy.wait()


def turn_solvent(ks, grid_shift, v, occ, field, done=None):
    planes = SUB * len(ks)
    layers = len(ks) + (CX in ks)
    return pl.pallas_call(
        functools.partial(turn_kernel, ks),
        out_shape=struct(*v.shape),
        in_specs=[IN_SMEM, IN_VMEM, IN_VMEM, IN_VMEM] + [HBM] * (done is not None),
        out_specs=HBM,
        input_output_aliases={} if done is None else {4: 0},
        scratch_shapes=[
            VMEM((3, planes, 2 * FY, FZ), jnp.float32),
            VMEM((2 * planes * FY, FZ), jnp.float32),
            VMEM((12, JP * layers, FZ), jnp.float32),
            DMA((planes,)),
        ],
        compiler_params=pltpu.CompilerParams(vmem_limit_bytes=TURN_LIMIT),
        cost_estimate=pl.CostEstimate(flops=3_000_000, bytes_accessed=1_300_000, transcendentals=0),
        name="turn_solvent",
    )(grid_shift, v, occ, field, *([] if done is None else [done]))


def per_device(
    solvent_vel,
    occupancy,
    grid_shift,
    axis_index,
    colloid_pos,
    colloid_vel,
    colloid_mass,
    colloid_count,
):
    v = solvent_vel.reshape(3, FX, 2 * FY, FZ)
    pos = colloid_pos.reshape(3, 1, FZ)
    vel = colloid_vel.reshape(3, 1, FZ)
    mass = colloid_mass
    count = colloid_count

    base, odd, even = border_sums(grid_shift, count, v, occupancy, axis_index, pos, vel, mass)
    odd1, even1 = swap_both(odd, even, "gx")
    part, state, numbers = inner_sums(grid_shift, v, occupancy, base)
    odd, even = columns(part, odd1, even1, state, numbers)
    odd2, even2 = swap_both(odd, even, "yz")
    field, rest, packets = cell_fields(count, part, odd1, even1, odd2, even2, state, numbers)
    packets = lax.all_to_all(packets, "gx", 0, 0)
    width = 2 * (SUBSTEPS - 1) + 1
    row, moving = pick(width, packets)
    solvent_out = None
    for ks in TURNED:
        width -= 2
        if solvent_out is None:
            row, field = lax.optimization_barrier((row, field))
        else:
            row, solvent_out = lax.optimization_barrier((row, solvent_out))
        solvent_out = turn_solvent(ks, grid_shift, v, occupancy, field, solvent_out)
        odd, even = swap_both(row, row, "yz")
        odd, solvent_out = lax.optimization_barrier((odd, solvent_out))
        row, moving = substep(width, row, moving, odd, even, rest)
    position, velocity = row, moving
    return (
        solvent_out.reshape(solvent_vel.shape),
        position[:, None],
        velocity[:, None],
    )


def solution(mesh):
    return jax.shard_map(
        per_device,
        mesh=mesh,
        in_specs=(
            P(None, "gx", "yz", None, None),
            P("gx", "yz", None),
            P(),
            P("gx", "yz", None),
            P(None, "gx", "yz", None),
            P(None, "gx", "yz", None),
            P("gx", "yz", None),
            P("gx", "yz"),
        ),
        out_specs=(
            P(None, "gx", "yz", None, None),
            P(None, "gx", "yz", None),
            P(None, "gx", "yz", None),
        ),
        check_vma=False,
    )
```

```python
import functools
import math

import jax
import jax.numpy as jnp
from jax import lax
from jax.experimental import pallas as pl
from jax.experimental.pallas import tpu as pltpu
from jax.sharding import PartitionSpec as P

CX = 8
CY = 8
CZ = 64
SUB = 4
SUBSTEPS = 4
DIRECTIONS = 64
FX = 32
FY = 32
FZ = 128
KX = CX + 1
JY = CY + 1
JP = 16
ROWS = KX * JP

turn_angle = 130.0 * math.pi / 180.0
cos_angle = math.cos(turn_angle)
sin_angle = math.sin(turn_angle)
golden = math.pi * (3.0 - math.sqrt(5.0))
cutoff = 1.5
stiffness = 20.0
timestep = 0.05
fill_mass = 16.0

SMEM = pltpu.SMEM
VMEM = pltpu.VMEM
HBM = pl.BlockSpec(memory_space=pltpu.HBM)
IN_VMEM = pl.BlockSpec(memory_space=VMEM)
IN_SMEM = pl.BlockSpec(memory_space=SMEM)
DMA = pltpu.SemaphoreType.DMA
NT = (((1,), (1,)), ((), ()))
NN = (((1,), (0,)), ((), ()))
STATE = 4 * JP
NUMBERS = STATE + 16
BASE = NUMBERS + ROWS
TURNED = ((1, 2, 3), (4, 5, 6), (7, CX))
TILE = 32
SMALL_LIMIT = 8 * 1024 * 1024
TURN_LIMIT = 16 * 1024 * 1024


def swapped(value, axis, first):
    count = lax.axis_size(axis)
    pairs = []
    for low in range(first, count + first, 2):
        a, b = low % count, (low + 1) % count
        pairs += [(a, b), (b, a)]
    return lax.ppermute(value, axis, pairs)


def swap_both(odd, even, axis):
    return swapped(odd, axis, 1), swapped(even, axis, 0)


def struct(*shape):
    return jax.ShapeDtypeStruct(shape, jnp.float32)


def exact_dot(left, right, dims, parts=2):
    right = right.astype(jnp.bfloat16)
    total = None
    for part in range(parts):
        piece = left.astype(jnp.bfloat16)
        term = lax.dot_general(piece, right, dims, preferred_element_type=jnp.float32)
        total = term if total is None else total + term
        if part < parts - 1:
            left = left - piece.astype(jnp.float32)
    return total


def colloid_cells(pos, sx, sy, sz):
    cell_x = jnp.clip(jnp.floor(pos[0] * SUB).astype(jnp.int32), 0, FX - 1)
    cell_y = jnp.clip(jnp.floor(pos[1] * SUB).astype(jnp.int32), 0, FY - 1)
    cell_z = jnp.clip(jnp.floor(pos[2] * 2.0).astype(jnp.int32), 0, FZ - 1)
    return ((cell_x + sx) >> 2, (cell_y + sy) >> 2, ((cell_z + sz) & (FZ - 1)) >> 1)


def live_row(count):
    return lax.broadcasted_iota(jnp.int32, (1, FZ), 1) < count


def parity(axis):
    return lax.axis_index(axis) & 1


def live_planes(occ, places, twice):
    for n, x in enumerate(places):
        slots = occ[x].astype(jnp.float32)
        twice[pl.ds(2 * FY * n, FY, 2), :] = slots
        twice[pl.ds(2 * FY * n + 1, FY, 2), :] = slots


def add_plane(v, twice, slot, n, x, acc):
    live = twice[pl.ds(pl.multiple_of(n * 2 * FY, 2 * FY), 2 * FY), :] > slot
    masked = [jnp.where(live, v[c, x], 0.0) for c in range(3)] + [jnp.where(live, 1.0, 0.0)]
    return tuple(a + m for a, m in zip(acc, masked))


def store_cells(acc, sy, partial, at):
    row = lax.broadcasted_iota(jnp.int32, (8, FZ), 0)
    low = (row < 8 - 2 * sy)[None]
    blank = jnp.zeros((1, 8, FZ), jnp.float32)
    for c in range(4):
        parts = acc[c].reshape(CY, 8, FZ)
        picked = jnp.where(low, jnp.concatenate([parts, blank]), jnp.concatenate([blank, parts]))
        partial[c, at, 0:JY, :] = jnp.sum(picked, axis=1)


def slot_rows():
    return (lax.broadcasted_iota(jnp.int32, (2 * FY, FZ), 0) & 1).astype(jnp.float32)


def along_z(partial, carried, sz, lz, p):
    target = lax.broadcasted_iota(jnp.int32, (CZ, FZ), 0)
    layer = lax.broadcasted_iota(jnp.int32, (CZ, FZ), 1)
    to_cell = (((layer + sz) & (FZ - 1)) >> 1 == target).astype(jnp.float32)
    to_place = (target == lz).astype(jnp.float32)
    one = jnp.concatenate([to_cell, to_place], axis=1)
    none = jnp.zeros_like(one)
    right = jnp.concatenate(
        [jnp.concatenate([one, none], axis=1), jnp.concatenate([none, one], axis=1)], axis=0
    )
    size = carried[0].shape[0]
    left = jnp.concatenate(
        [
            partial[2 * p].reshape(size, FZ),
            carried[2 * p],
            partial[2 * p + 1].reshape(size, FZ),
            carried[2 * p + 1],
        ],
        axis=1,
    )
    return exact_dot(left, right, NT)


def border_kernel(
    shift_at, count_at, v_at, occ_at, axis_at, pos_at, vel_at, mass_at,
    base, odd, even,
    shift, count, v, occ, axis, pos, vel, mass, twice, partial, sem,
):
    ends = ((pl.ds(0, SUB - 1), pl.ds(0, SUB - 1)), (pl.ds(FX - SUB + 1, SUB - 1), pl.ds(SUB - 1, SUB - 1)))
    pairs = [(shift_at, shift)]
    pairs += [(occ_at.at[there], occ.at[here]) for there, here in ends]
    pairs += [(v_at.at[:, there], v.at[:, here]) for there, here in ends]
    pairs += [(count_at, count), (pos_at, pos), (vel_at, vel), (mass_at, mass), (axis_at, axis)]
    copies = [pltpu.make_async_copy(a, b, sem.at[i]) for i, (a, b) in enumerate(pairs)]
    for copy in copies:
        copy.start()
    partial[:, :, 8:JP, :] = jnp.zeros((4, 2, JP - 8, FZ), jnp.float32)
    slot = slot_rows()
    zero = jnp.zeros((2 * FY, FZ), jnp.float32)
    for copy in copies[:3]:
        copy.wait()
    sx, sy, sz = shift[0], shift[1], shift[2]
    planes = 2 * (SUB - 1)
    live_planes(occ, range(planes), twice)
    for copy in copies[3:]:
        copy.wait()

    def plane(x, acc):
        return add_plane(v, twice, slot, x, x, acc)

    store_cells(lax.fori_loop(0, SUB - sx, plane, (zero,) * 4), sy, partial, 0)
    store_cells(lax.fori_loop(planes - sx, planes, plane, (zero,) * 4), sy, partial, 1)

    kx, jy, lz = colloid_cells(pos, sx, sy, sz)
    alive = live_row(count[0, 0]).astype(jnp.float32)
    weight = mass[0] * alive
    place = jnp.where(kx == 0, jy, jnp.where(kx == CX, JP + jy, 2 * JP))
    hit = lax.broadcasted_iota(jnp.int32, (2 * JP, FZ), 0) == place
    carried = [jnp.where(hit, vel[c] * weight, 0.0) for c in range(3)]
    carried.append(jnp.where(hit, weight, 0.0))
    for p in range(2):
        base[2 * JP * p : 2 * JP * (p + 1)] = along_z(partial, carried, sz, lz, p)
    side = parity("gx")
    number = None
    base[NUMBERS : NUMBERS + ROWS] = jnp.zeros((ROWS, FZ), jnp.float32)
    for k in range(CX):
        row = axis[k].astype(jnp.float32)
        row = jnp.concatenate([row, row], axis=1)
        base[NUMBERS + JP * k : NUMBERS + JP * k + CY] = row
        number = row if k == 0 else number
    for packet, end in ((odd, side), (even, 1 - side)):
        for p in range(2):
            start = pl.multiple_of(2 * JP * p + JP * end, JP)
            packet[8 * p : 8 * p + 8] = base[pl.ds(start, 8), :]
            packet[16 + p : 17 + p] = base[pl.ds(start + 8, 1), :]
        for c in range(3):
            packet[18 + c : 19 + c] = pos[c]
        packet[21:22] = alive
        packet[22:24] = jnp.zeros((2, FZ), jnp.float32)
        packet[24:32] = number
    for c in range(3):
        base[STATE + c : STATE + c + 1] = pos[c]
        base[STATE + 3 + c : STATE + 4 + c] = vel[c]
    base[STATE + 6 : STATE + 7] = mass[0]
    base[STATE + 7 : STATE + 8] = alive
    base[STATE + 8 : STATE + 9] = (kx * JP + jy).astype(jnp.float32)
    base[STATE + 9 : STATE + 10] = lz.astype(jnp.float32)
    base[STATE + 10 : STATE + 16] = jnp.zeros((6, FZ), jnp.float32)


def border_sums(grid_shift, count, v, occ, axis_index, pos, vel, mass):
    planes = 2 * (SUB - 1)
    return pl.pallas_call(
        border_kernel,
        out_shape=(struct(BASE, FZ), struct(32, FZ), struct(32, FZ)),
        in_specs=[HBM] * 8,
        out_specs=(IN_VMEM,) * 3,
        scratch_shapes=[
            SMEM((3,), jnp.int32),
            SMEM((1, 1), jnp.int32),
            VMEM((3, planes, 2 * FY, FZ), jnp.float32),
            VMEM((planes, FY, FZ), jnp.int32),
            VMEM((CX, CY, CZ), jnp.int32),
            VMEM((3, 1, FZ), jnp.float32),
            VMEM((3, 1, FZ), jnp.float32),
            VMEM((1, 1, FZ), jnp.float32),
            VMEM((2 * planes * FY, FZ), jnp.float32),
            VMEM((4, 2, JP, FZ), jnp.float32),
            DMA((10,)),
        ],
        cost_estimate=pl.CostEstimate(flops=1_000_000, bytes_accessed=800_000, transcendentals=0),
        name="border_sums",
    )(grid_shift, count, v, occ, axis_index, pos, vel, mass)


def inner_kernel(shift, v, occ, base, part, state, numbers, twice, partial):
    sx, sy, sz = shift[0], shift[1], shift[2]
    state[...] = base[STATE:NUMBERS]
    numbers[...] = base[NUMBERS:BASE]
    partial[:, :, 8:JP, :] = jnp.zeros((4, CX - 1, JP - 8, FZ), jnp.float32)
    slot = slot_rows()
    zero = jnp.zeros((2 * FY, FZ), jnp.float32)
    live_planes(occ, [SUB - sx + n for n in range(SUB * (CX - 1))], twice)
    for k in range(1, CX):
        acc = (zero,) * 4
        for j in range(SUB):
            acc = add_plane(v, twice, slot, SUB * (k - 1) + j, k * SUB - sx + j, acc)
        store_cells(acc, sy, partial, k - 1)
    weight = base[STATE + 6 : STATE + 7] * base[STATE + 7 : STATE + 8]
    place = base[STATE + 8 : STATE + 9].astype(jnp.int32) - JP
    lz = base[STATE + 9 : STATE + 10].astype(jnp.int32)
    inner = JP * (CX - 1)
    hit = lax.broadcasted_iota(jnp.int32, (inner, FZ), 0) == place
    carried = [
        jnp.where(hit, base[STATE + 3 + c : STATE + 4 + c] * weight, 0.0) for c in range(3)
    ]
    carried.append(jnp.where(hit, weight, 0.0))
    for p in range(2):
        first = p * ROWS
        part[first : first + JP] = base[2 * JP * p : 2 * JP * p + JP]
        part[first + JP : first + JP + inner] = along_z(partial, carried, sz, lz, p)
        part[first + CX * JP : first + ROWS] = base[2 * JP * p + JP : 2 * JP * (p + 1)]


def inner_sums(grid_shift, v, occ, base):
    return pl.pallas_call(
        inner_kernel,
        out_shape=(struct(2 * ROWS, FZ), struct(16, FZ), struct(ROWS, FZ)),
        in_specs=[IN_SMEM] + [IN_VMEM] * 3,
        out_specs=(IN_VMEM,) * 3,
        scratch_shapes=[
            VMEM((2 * SUB * (CX - 1) * FY, FZ), jnp.float32),
            VMEM((4, CX - 1, JP, FZ), jnp.float32),
        ],
        compiler_params=pltpu.CompilerParams(vmem_limit_bytes=TURN_LIMIT),
        cost_estimate=pl.CostEstimate(flops=4_000_000, bytes_accessed=3_700_000, transcendentals=0),
        name="inner_sums",
    )(grid_shift, v, occ, base)


def add_x(part, odd, even, full):
    full[...] = part[...]
    turned = parity("gx") * (CX * JP)
    for p in range(2):
        for packet, place in ((odd, turned), (even, CX * JP - turned)):
            start = pl.multiple_of(p * ROWS + place, JP)
            full[pl.ds(start, 8), :] += packet[8 * p : 8 * p + 8]
            full[pl.ds(start + 8, 1), :] += packet[16 + p : 17 + p]


def later_x(odd, even, rows):
    return jnp.where(parity("gx") == 1, odd[rows], even[rows])


def columns_kernel(part, odd1, even1, state, numbers, odd, even, full, ends):
    add_x(part, odd1, even1, full)
    for p in range(2):
        ends[0, 9 * p : 9 * p + 9] = full[pl.ds(p * ROWS, KX, JP), :]
        ends[1, 9 * p : 9 * p + 9] = full[pl.ds(p * ROWS + 8, KX, JP), :]
    side = parity("yz")
    for packet, end in ((odd, side), (even, 1 - side)):
        packet[0:18] = ends[end, 0:18]
        packet[18:22] = odd1[18:22]
        packet[22:25] = state[0:3]
        packet[25:26] = state[7:8]
        packet[26:30] = even1[18:22]
        packet[30:38] = numbers[pl.ds(0, CX, JP), :]
        packet[38:39] = later_x(odd1, even1, slice(24, 25))
        packet[39:40] = jnp.zeros((1, FZ), jnp.float32)


def columns(part, odd1, even1, state, numbers):
    return pl.pallas_call(
        columns_kernel,
        out_shape=(struct(40, FZ), struct(40, FZ)),
        in_specs=[IN_VMEM] * 5,
        out_specs=(IN_VMEM,) * 2,
        scratch_shapes=[VMEM((2 * ROWS, FZ), jnp.float32), VMEM((2, 24, FZ), jnp.float32)],
        compiler_params=pltpu.CompilerParams(vmem_limit_bytes=SMALL_LIMIT),
        cost_estimate=pl.CostEstimate(flops=100_000, bytes_accessed=500_000, transcendentals=0),
        name="columns",
    )(part, odd1, even1, state, numbers)


def store_around(rows, base, others):
    wide = [[jnp.broadcast_to(value, (8, FZ)) for value in packet] for packet in others]
    low = lax.broadcasted_iota(jnp.int32, (8, FZ), 1) < FZ // 2
    reach = None
    for c in range(4):
        rows[base + c] = wide[0][c]
        for p in range(4):
            a, b = wide[1 + 2 * p][c], wide[2 + 2 * p][c]
            rows[base + 4 + 4 * p + c] = jnp.where(low, a, pltpu.roll(b, FZ // 2, 1))
            late = jnp.where(low, pltpu.roll(a, FZ // 2, 1), b)
            rows[base + 20 + 4 * p + c] = late
            if c == 3:
                reach = late if reach is None else jnp.maximum(reach, late)
    return jnp.max(reach) > 0.0


def pair_force(devices, rows, terms):
    ones = jnp.ones((8, FZ), jnp.bfloat16)
    slot = lax.broadcasted_iota(jnp.int32, (FZ, FZ), 0)
    sub = TILE // 8

    for n, (own, live, others) in enumerate(devices):
        base = 36 * n
        crowded = store_around(rows, base, others)
        column = jnp.concatenate(list(own) + [jnp.zeros((5, FZ), jnp.float32)], axis=0).T

        def tile(t, n=n, column=column, base=base, crowded=crowded):
            part = column[TILE * t : TILE * t + TILE]
            mine = [
                jnp.broadcast_to(part[:, c : c + 1], (TILE, FZ)).reshape(sub, 8, FZ)
                for c in range(3)
            ]

            def force(places):
                total = None
                for place in places:
                    dx = mine[0] - rows[place][None]
                    dy = mine[1] - rows[place + 1][None]
                    dz = mine[2] - rows[place + 2][None]
                    dz = jnp.where(
                        dz > 0.5 * CZ, dz - CZ, jnp.where(dz < -0.5 * CZ, dz + CZ, dz)
                    )
                    reach = jnp.maximum(
                        rows[place + 3][None]
                        - (dx * dx + dy * dy + dz * dz) * (1.0 / (cutoff * cutoff)),
                        0.0,
                    )
                    weight = reach * reach
                    new = (weight * dx, weight * dy, weight * dz)
                    total = new if total is None else tuple(a + b for a, b in zip(total, new))
                return total

            at = [pl.ds(FZ * (3 * n + c) + TILE * t, TILE) for c in range(3)]
            for c, value in enumerate(force(range(base, base + 20, 4))):
                terms[at[c], :] = value.reshape(TILE, FZ)

            @pl.when(crowded)
            def _():
                for c, value in enumerate(force(range(base + 20, base + 36, 4))):
                    terms[at[c], :] = terms[at[c], :] + value.reshape(TILE, FZ)

        for t in range(FZ // TILE):
            pl.when(TILE * t < live)(functools.partial(tile, t))

    forces = []
    for n, (own, live, others) in enumerate(devices):
        left = jnp.where(
            jnp.concatenate([slot < live] * 3), terms[3 * FZ * n : 3 * FZ * (n + 1)], 0.0
        )
        back = None
        for part in range(2):
            piece = left.astype(jnp.bfloat16)
            term = lax.dot_general(ones, piece, NT, preferred_element_type=jnp.float32)
            back = term if back is None else back + term
            if part < 1:
                left = left - piece.astype(jnp.float32)
        forces.append([stiffness * back[0:1, FZ * c : FZ * c + FZ] for c in range(3)])
    return forces


def pair_scratch(width):
    return [
        VMEM((36 * width, 8, FZ), jnp.float32),
        VMEM((3 * FZ * width, FZ), jnp.float32),
    ]


def placed(packet, step_x, step_y):
    x, y, z, alive = packet
    return (x + step_x, y + step_y, z, jnp.where(alive > 0.0, 1.0, -1.0))


def middle_first(values):
    return values[4:5] + values[:4] + values[5:]


def toward(axis, cells):
    return ((2 * parity(axis) - 1) * cells).astype(jnp.float32)


def live_count(alive):
    return jnp.sum(alive).astype(jnp.int32)


def advance(own, velocity, mass, alive, force):
    velocity = [
        velocity[c] + timestep * jnp.where(alive > 0.0, force[c], 0.0) / mass for c in range(3)
    ]
    return [own[c] + timestep * velocity[c] for c in range(3)], velocity


def fields_kernel(
    count, part, odd1, even1, odd2, even2, state, numbers_in,
    field_out, rest_out, packets,
    full, numbers, pair_rows, pair_terms,
):
    add_x(part, odd1, even1, full)
    forward = parity("yz") == 1
    for p in range(2):
        rows = slice(9 * p, 9 * p + 9)
        first = pl.ds(p * ROWS, KX, JP)
        full[first, :] = full[first, :] + jnp.where(forward, even2[rows], odd2[rows])
        last = pl.ds(p * ROWS + 8, KX, JP)
        full[last, :] = full[last, :] + jnp.where(forward, odd2[rows], even2[rows])
    numbers[...] = numbers_in[...]
    numbers[JP * CX : JP * CX + 8] = later_x(odd1, even1, slice(24, 32))
    numbers[pl.ds(8, KX, JP), :] = jnp.where(forward, odd2[30:39], even2[30:39])

    lane = lax.broadcasted_iota(jnp.int32, (8, FZ), 1)
    number = (lane & (DIRECTIONS - 1)).astype(jnp.float32)
    height = 1.0 - (2.0 * number + 1.0) / DIRECTIONS
    radius = jnp.sqrt(1.0 - height * height)
    phase = number * golden
    index = numbers[...].astype(jnp.int32)
    n0, n1, n2 = [
        jnp.take_along_axis(jnp.broadcast_to(table[0:1], (ROWS, FZ)), index, axis=1)
        for table in (radius * jnp.cos(phase), radius * jnp.sin(phase), height)
    ]

    lower = lax.broadcasted_iota(jnp.int32, (ROWS, FZ), 1) < CZ
    first, second = full[0:ROWS], full[ROWS : 2 * ROWS]
    heavy = jnp.maximum(jnp.where(lower, pltpu.roll(second, CZ, 1), second), fill_mass)
    mean_xy = first / heavy
    mean_z = second / heavy
    mean_yx = pltpu.roll(mean_xy, CZ, 1)
    mean_z_up = pltpu.roll(mean_z, CZ, 1)
    turn = 1.0 - cos_angle
    t0, t1, t2 = turn * n0, turn * n1, turn * n2
    s0, s1, s2 = sin_angle * n0, sin_angle * n1, sin_angle * n2
    field_out[0] = jnp.where(lower, cos_angle + t0 * n0, t0 * n1 - s2)
    field_out[1] = jnp.where(lower, t0 * n2 + s1, t0 * n1 + s2)
    field_out[2] = jnp.where(lower, cos_angle + t1 * n1, t1 * n2 - s0)
    field_out[3] = jnp.where(lower, t0 * n2 - s1, t1 * n2 + s0)
    field_out[4] = jnp.where(lower, cos_angle + t2 * n2, mean_yx)
    field_out[5] = jnp.where(lower, mean_yx, mean_z_up)

    place = state[8:9].astype(jnp.int32)
    lz = state[9:10].astype(jnp.int32)
    to_place = (lax.broadcasted_iota(jnp.int32, (CZ, FZ), 0) == lz).astype(jnp.float32)
    none = jnp.zeros_like(to_place)
    right = jnp.concatenate(
        [jnp.concatenate([to_place, none], axis=1), jnp.concatenate([none, to_place], axis=1)],
        axis=0,
    )
    hit = lax.broadcasted_iota(jnp.int32, (ROWS, FZ), 0) == place
    picked = []
    for pair in (mean_xy, jnp.where(lower, mean_z, n0), jnp.where(lower, n1, n2)):
        at_z = exact_dot(pair, right, NN)
        for half in (at_z[:, :FZ], at_z[:, FZ:]):
            picked.append(jnp.sum(jnp.where(hit, half, 0.0), axis=0, keepdims=True))
    u, n = picked[:3], picked[3:]
    alive = state[7:8] > 0.0
    old = [state[3 + c : 4 + c] for c in range(3)]
    rel = [old[c] - u[c] for c in range(3)]
    cross = [n[1] * rel[2] - n[2] * rel[1], n[2] * rel[0] - n[0] * rel[2], n[0] * rel[1] - n[1] * rel[0]]
    along = n[0] * rel[0] + n[1] * rel[1] + n[2] * rel[2]
    velocity = [
        jnp.where(
            alive,
            u[c] + cos_angle * rel[c] + sin_angle * cross[c] + turn * along * n[c],
            old[c],
        )
        for c in range(3)
    ]

    own = [state[c : c + 1] for c in range(3)]
    alive_row = state[7:8]

    def rows(b, a):
        if b == 1 and a == 1:
            return own + [alive_row]
        if b == 1:
            source, base = (odd1, 18) if a == 0 else (even1, 18)
        else:
            source, base = (odd2 if b == 0 else even2), 18 + 4 * a
        return [source[base + c : base + c + 1] for c in range(4)]

    rest_out[0:7] = state[0:7]
    rest_out[7:8] = alive_row
    after = parity("gx") == 1
    others = []
    for b in range(3):
        step_y = (1 - b) * toward("yz", CY)
        slots = [rows(b, a) for a in range(3)]
        first = [jnp.where(after, e, o) for o, e in zip(slots[0], slots[2])]
        last = [jnp.where(after, o, e) for o, e in zip(slots[0], slots[2])]
        for a, packet in enumerate((first, slots[1], last)):
            others.append(placed(packet, (a - 1) * float(CX), step_y))
    force = pair_force([(own, count[0, 0], middle_first(others))], pair_rows, pair_terms)[0]
    moved, velocity = advance(own, velocity, state[6:7], alive_row, force)
    packet = jnp.concatenate(moved + [alive_row] + velocity + [state[6:7]], axis=0)
    for g in range(packets.shape[0]):
        packets[g] = packet


def cell_fields(count, part, odd1, even1, odd2, even2, state, numbers):
    return pl.pallas_call(
        fields_kernel,
        out_shape=(struct(6, ROWS, FZ), struct(8, FZ), struct(lax.axis_size("gx"), 8, FZ)),
        in_specs=[IN_SMEM] + [IN_VMEM] * 7,
        out_specs=(IN_VMEM,) * 3,
        scratch_shapes=[
            VMEM((2 * ROWS, FZ), jnp.float32),
            VMEM((ROWS, FZ), jnp.float32),
            *pair_scratch(1),
        ],
        compiler_params=pltpu.CompilerParams(vmem_limit_bytes=SMALL_LIMIT),
        cost_estimate=pl.CostEstimate(flops=4_000_000, bytes_accessed=1_000_000, transcendentals=0),
        name="cell_fields",
    )(count, part, odd1, even1, odd2, even2, state, numbers)


def padded(rows):
    return -(-rows // 8) * 8


def clear_tail(ref, used):
    if used < ref.shape[0]:
        ref[used:] = jnp.zeros((ref.shape[0] - used, FZ), jnp.float32)


def pick_kernel(width, packets, row_out, moving_out):
    count = packets.shape[0]
    me = lax.axis_index("gx")
    for a in range(width):
        source = lax.rem(me + a - width // 2 + 8 * count, count)
        row_out[4 * a : 4 * a + 4] = packets[source, 0:4]
        if 0 < a < width - 1:
            moving_out[4 * a - 4 : 4 * a] = packets[source, 4:8]
    clear_tail(row_out, 4 * width)
    clear_tail(moving_out, 4 * (width - 2))


def pick(width, packets):
    return pl.pallas_call(
        functools.partial(pick_kernel, width),
        out_shape=(struct(padded(4 * width), FZ), struct(padded(4 * (width - 2)), FZ)),
        in_specs=[IN_VMEM],
        out_specs=(IN_VMEM,) * 2,
        compiler_params=pltpu.CompilerParams(vmem_limit_bytes=SMALL_LIMIT),
        cost_estimate=pl.CostEstimate(flops=10_000, bytes_accessed=100_000, transcendentals=0),
        name="pick",
    )(packets)


def substep_moves(width, row, moving, odd, even, rows, terms):
    sources = (odd, row, even)
    devices = []
    for n in range(width):
        at = 4 * (n + 1)
        own = [row[at + c : at + c + 1] for c in range(3)]
        others = []
        for b, source in enumerate(sources):
            step_y = (1 - b) * toward("yz", CY)
            for step in (-1, 0, 1):
                start = at + 4 * step
                packet = [source[start + c : start + c + 1] for c in range(4)]
                others.append(placed(packet, step * float(CX), step_y))
        devices.append((own, live_count(row[at + 3 : at + 4]), middle_first(others)))
    forces = pair_force(devices, rows, terms)
    results = []
    for n in range(width):
        alive = row[4 * n + 7 : 4 * n + 8]
        velocity = [moving[4 * n + c : 4 * n + c + 1] for c in range(3)]
        mass = moving[4 * n + 3 : 4 * n + 4]
        results.append((*advance(devices[n][0], velocity, mass, alive, forces[n]), alive, mass))
    return results


def substep_kernel(width, row, moving, odd, even, row_out, moving_out, rows, terms):
    results = substep_moves(width, row, moving, odd, even, rows, terms)
    for n, (moved, velocity, alive, mass) in enumerate(results):
        row_out[4 * n : 4 * n + 4] = jnp.concatenate(moved + [alive], axis=0)
        if 0 < n < width - 1:
            moving_out[4 * n - 4 : 4 * n] = jnp.concatenate(velocity + [mass], axis=0)
    clear_tail(row_out, 4 * width)
    clear_tail(moving_out, 4 * (width - 2))


def last_kernel(row, moving, odd, even, rest, pos_out, vel_out, rows, terms):
    ((moved, velocity, alive, mass),) = substep_moves(1, row, moving, odd, even, rows, terms)
    keep = rest[7:8] > 0.0
    for c in range(3):
        pos_out[c] = jnp.where(keep, moved[c], rest[c : c + 1])
        vel_out[c] = jnp.where(keep, velocity[c], rest[3 + c : 4 + c])


def substep(width, row, moving, odd, even, rest):
    if width > 1:
        kernel = functools.partial(substep_kernel, width)
        shapes = (struct(padded(4 * width), FZ), struct(padded(4 * (width - 2)), FZ))
        operands = (row, moving, odd, even)
    else:
        kernel = last_kernel
        shapes = (struct(3, 1, FZ), struct(3, 1, FZ))
        operands = (row, moving, odd, even, rest)
    return pl.pallas_call(
        kernel,
        out_shape=shapes,
        in_specs=[IN_VMEM] * len(operands),
        out_specs=(IN_VMEM,) * 2,
        scratch_shapes=pair_scratch(width),
        compiler_params=pltpu.CompilerParams(vmem_limit_bytes=SMALL_LIMIT),
        cost_estimate=pl.CostEstimate(
            flops=4_000_000 * width, bytes_accessed=100_000, transcendentals=0
        ),
        name="substep",
    )(*operands)


def turn_kernel(ks, shift, v, occ, field, *refs):
    out_at, out, twice, wide, wsem = refs[-5:]
    sx, sy, sz = shift[0], shift[1], shift[2]
    places = []
    stores = []
    for i, k in enumerate(ks):
        if k < CX:
            places += [k * SUB - sx + j for j in range(SUB)]
            here, there = pl.ds(SUB * i, SUB), pl.ds(SUB * k - sx, SUB)
            stores.append(
                [pltpu.make_async_copy(out.at[:, here], out_at.at[:, there], wsem.at[SUB * i])]
            )
        else:
            around_end = [(FX - sx + j) & (FX - 1) for j in range(SUB)]
            places += around_end
            stores.append(
                [
                    pltpu.make_async_copy(
                        out.at[:, pl.ds(SUB * i + j, 1)],
                        out_at.at[:, pl.ds(x, 1)],
                        wsem.at[SUB * i + j],
                    )
                    for j, x in enumerate(around_end)
                ]
            )
    source = lax.broadcasted_iota(jnp.int32, (CZ, FZ), 0)
    layer = lax.broadcasted_iota(jnp.int32, (CZ, FZ), 1)
    spread = (((layer + sz) & (FZ - 1)) >> 1 == source).astype(jnp.float32)
    none = jnp.zeros_like(spread)
    right = jnp.concatenate(
        [jnp.concatenate([spread, none], axis=1), jnp.concatenate([none, spread], axis=1)],
        axis=0,
    )
    layers = list(ks) + ([0] if CX in ks else [])
    for f in range(6):
        left = jnp.concatenate([field[f, JP * k : JP * k + JP] for k in layers])
        both = exact_dot(left, right, NN, parts=2)
        wide[2 * f] = both[:, :FZ]
        wide[2 * f + 1] = both[:, FZ:]
    row = lax.broadcasted_iota(jnp.int32, (8, FZ), 0)
    slot = (row & 1).astype(jnp.float32)
    low = row < 8 - 2 * sy

    def turn_layer(at, planes, t):
        f = [
            jnp.where(low, wide[i, pl.ds(JP * at + t, 1), :], wide[i, pl.ds(JP * at + t + 1, 1), :])
            for i in range(12)
        ]
        rows = pl.ds(pl.multiple_of(8 * t, 8), 8)

        def plane(n, x):
            live = twice[pl.ds(pl.multiple_of(n * 2 * FY + 8 * t, 8), 8), :] > slot
            old = [v[c, x, rows, :] for c in range(3)]
            rel = [old[c] - f[9 + c] for c in range(3)]
            for c in range(3):
                new = f[9 + c] + (
                    f[3 * c] * rel[0] + f[3 * c + 1] * rel[1] + f[3 * c + 2] * rel[2]
                )
                out[c, n, rows, :] = jnp.where(live, new, old[c])

        planes(plane)

    live_planes(occ, places, twice)
    for i, k in enumerate(ks):

        def column(t, carry, i=i, k=k):
            def some(first, last):
                def run(plane):
                    def step(j, carry):
                        plane(SUB * i + j, (FX - sx + j) & (FX - 1))
                        return carry

                    lax.fori_loop(first, last, step, 0)

                return run

            if k < CX:
                turn_layer(
                    i, lambda plane: [plane(SUB * i + j, places[SUB * i + j]) for j in range(SUB)], t
                )
            else:
                turn_layer(i, some(0, sx), t)
                turn_layer(i + 1, some(sx, SUB), t)
            return carry

        lax.fori_loop(0, CY, column, 0)
        for copy in stores[i]:
            copy.start()
    for group in stores:
        for copy in group:
            copy.wait()


def turn_solvent(ks, grid_shift, v, occ, field, done=None):
    planes = SUB * len(ks)
    layers = len(ks) + (CX in ks)
    return pl.pallas_call(
        functools.partial(turn_kernel, ks),
        out_shape=struct(*v.shape),
        in_specs=[IN_SMEM, IN_VMEM, IN_VMEM, IN_VMEM] + [HBM] * (done is not None),
        out_specs=HBM,
        input_output_aliases={} if done is None else {4: 0},
        scratch_shapes=[
            VMEM((3, planes, 2 * FY, FZ), jnp.float32),
            VMEM((2 * planes * FY, FZ), jnp.float32),
            VMEM((12, JP * layers, FZ), jnp.float32),
            DMA((planes,)),
        ],
        compiler_params=pltpu.CompilerParams(vmem_limit_bytes=TURN_LIMIT),
        cost_estimate=pl.CostEstimate(flops=3_000_000, bytes_accessed=1_300_000, transcendentals=0),
        name="turn_solvent",
    )(grid_shift, v, occ, field, *([] if done is None else [done]))


def per_device(
    solvent_vel,
    occupancy,
    grid_shift,
    axis_index,
    colloid_pos,
    colloid_vel,
    colloid_mass,
    colloid_count,
):
    v = solvent_vel.reshape(3, FX, 2 * FY, FZ)
    pos = colloid_pos.reshape(3, 1, FZ)
    vel = colloid_vel.reshape(3, 1, FZ)
    mass = colloid_mass
    count = colloid_count

    base, odd, even = border_sums(grid_shift, count, v, occupancy, axis_index, pos, vel, mass)
    odd1, even1 = swap_both(odd, even, "gx")
    part, state, numbers = inner_sums(grid_shift, v, occupancy, base)
    odd, even = columns(part, odd1, even1, state, numbers)
    odd2, even2 = swap_both(odd, even, "yz")
    field, rest, packets = cell_fields(count, part, odd1, even1, odd2, even2, state, numbers)
    packets = lax.all_to_all(packets, "gx", 0, 0)
    width = 2 * (SUBSTEPS - 1) + 1
    row, moving = pick(width, packets)
    solvent_out = None
    for ks in TURNED:
        width -= 2
        if solvent_out is None:
            row, field = lax.optimization_barrier((row, field))
        else:
            row, solvent_out = lax.optimization_barrier((row, solvent_out))
        solvent_out = turn_solvent(ks, grid_shift, v, occupancy, field, solvent_out)
        odd, even = swap_both(row, row, "yz")
        odd, solvent_out = lax.optimization_barrier((odd, solvent_out))
        row, moving = substep(width, row, moving, odd, even, rest)
    position, velocity = row, moving
    return (
        solvent_out.reshape(solvent_vel.shape),
        position[:, None],
        velocity[:, None],
    )


def solution(mesh):
    return jax.shard_map(
        per_device,
        mesh=mesh,
        in_specs=(
            P(None, "gx", "yz", None, None),
            P("gx", "yz", None),
            P(),
            P("gx", "yz", None),
            P(None, "gx", "yz", None),
            P(None, "gx", "yz", None),
            P("gx", "yz", None),
            P("gx", "yz"),
        ),
        out_specs=(
            P(None, "gx", "yz", None, None),
            P(None, "gx", "yz", None),
            P(None, "gx", "yz", None),
        ),
        check_vma=False,
    )
```
